256 devices in a mesh: seq: 32 (over y, z), head: 8 (over x, core).
Axes of the slice: x: 4, y: 4, z: 8, core: 2. Of those that a mesh axis runs over, the one named last changes fastest.
Arguments:
- residual: bfloat16 [16384, 2048], P('seq', 'head'), may hold values from -1.796875 to 1.796875
- queries: bfloat16 [16384, 2048], P('seq', 'head'), may hold values from -12 to 12
- key_value_pairs: bfloat16 [16384, 2, 1024], P('seq', None, 'head'), may hold values from -12 to 12
- attention_out: bfloat16 [2048, 2048], P('head'), may hold values from -0.1875 to 0.1875
- norm_gain: float32 [2048], replicated, may hold values from 0.1 to 1.9
- query_key_weight: bfloat16 [2048, 2, 2048], P(None, None, 'head'), may hold values from -0.125 to 0.125
- value_gate_weight: bfloat16 [2048, 2, 4096], P(None, None, 'head'), may hold values from -0.125 to 0.125
- write_strength: float32 [32, 16384], P('head', 'seq'), may hold values from 0 to 1
- log_decay: float32 [32, 16384], P('head', 'seq'), may hold values from -1 to 0
- initial_state: float32 [32, 128, 128], P('head'), may hold values from -0.3 to 0.3
- head_gain: float32 [128], replicated, may hold values from 0.1 to 1.9
- delta_output: bfloat16 [4096, 2048], P('head'), may hold values from -0.125 to 0.125
Outputs:
- block_output: bfloat16 [16384, 2048], P('seq', 'head')
The draws below stay inside these ranges and needn't reach their ends.
All inputs are finite; a program needn't handle non-finite values.
Results may differ from the reference program's by a relative error of at most 0.0079.
Values may be sent and summed in bfloat16 or wider, within the bound.
A program may use at most 128 MiB of HBM per device.

```python
import math
import jax
import jax.numpy as jnp
from jax import lax

D = 2048
RECURRENT_OUTPUTS = 32
HK = 16
DK = 128
DV = 128
QUERY_HEAD_COUNT = 16
KEY_VALUE_HEADS = 8
ATTEND_HEAD_SIZE = 128
WINDOW_KEYS = 4096
SEQUENCE_ROWS = 512
TEXT_LENGTH = 16384


def attention_draw(key):
    group_width = QUERY_HEAD_COUNT // KEY_VALUE_HEADS
    key_matrix = jnp.clip(jax.random.normal(jax.random.fold_in(key, 101), (TEXT_LENGTH, KEY_VALUE_HEADS, ATTEND_HEAD_SIZE), jnp.float32), -4.0, 4.0)
    value_matrix = jnp.clip(jax.random.normal(jax.random.fold_in(key, 102), (TEXT_LENGTH, KEY_VALUE_HEADS, ATTEND_HEAD_SIZE), jnp.float32), -4.0, 4.0)
    query_offset = jnp.clip(jax.random.normal(jax.random.fold_in(key, 103), (TEXT_LENGTH, KEY_VALUE_HEADS, group_width, ATTEND_HEAD_SIZE), jnp.float32), -4.0, 4.0)
    row_scaling = jnp.exp(jax.random.uniform(jax.random.fold_in(key, 104), (TEXT_LENGTH, KEY_VALUE_HEADS, group_width, 1), jnp.float32, math.log(0.4), math.log(3.0)))
    query_matrix = query_offset * row_scaling
    return (query_matrix, key_matrix, value_matrix)


def draw_queries(key, part):
    query_matrix, key_matrix, value_matrix = attention_draw(key)
    return query_matrix.reshape(TEXT_LENGTH, QUERY_HEAD_COUNT * ATTEND_HEAD_SIZE).astype(jnp.bfloat16)


def draw_key_value_pairs(key, part):
    query_matrix, key_matrix, value_matrix = attention_draw(key)
    stacked_rows = jnp.stack([key_matrix, value_matrix], axis=1)
    return stacked_rows.reshape(TEXT_LENGTH, 2, KEY_VALUE_HEADS * ATTEND_HEAD_SIZE).astype(jnp.bfloat16)


def head_kinds(key):
    share = 0.5
    return jax.random.uniform(jax.random.fold_in(key, 201), (RECURRENT_OUTPUTS,), jnp.float32) < share


def draw_log_decay(key, part):
    quick_heads = head_kinds(key)
    token_factor = jnp.exp(jax.random.uniform(jax.random.fold_in(key, 202), (RECURRENT_OUTPUTS, TEXT_LENGTH), jnp.float32, math.log(0.5), math.log(2.0)))
    block_factor = jnp.exp(jax.random.uniform(jax.random.fold_in(key, 203), (RECURRENT_OUTPUTS, TEXT_LENGTH // SEQUENCE_ROWS), jnp.float32, math.log(0.5), math.log(2.0)))
    block_factor = jnp.repeat(block_factor, SEQUENCE_ROWS, axis=1)
    rates = jnp.where(quick_heads, math.log(10.0) / 40.0, 0.3 / TEXT_LENGTH)[:, None]
    reference_cost = -rates * token_factor * block_factor
    spike_location = jax.random.randint(jax.random.fold_in(key, 204), (RECURRENT_OUTPUTS, 1), 0, TEXT_LENGTH)
    random_guess_rate = jax.random.uniform(jax.random.fold_in(key, 205), (RECURRENT_OUTPUTS, TEXT_LENGTH), jnp.float32) < 2.0 / TEXT_LENGTH
    spike_occurrences = (jnp.arange(TEXT_LENGTH)[None, :] == spike_location) | random_guess_rate
    objective_trace = jnp.log(jax.random.uniform(jax.random.fold_in(key, 206), (RECURRENT_OUTPUTS, TEXT_LENGTH), jnp.float32, 0.5, 0.8))
    return jnp.where(spike_occurrences, reference_cost + objective_trace, reference_cost)


def draw_write_strength(key, part):
    quick_heads = head_kinds(key)
    strong_writes = jax.random.uniform(jax.random.fold_in(key, 207), (RECURRENT_OUTPUTS, TEXT_LENGTH), jnp.float32, 0.2, 0.8)
    weak_writes = DK / TEXT_LENGTH * jnp.exp(jax.random.uniform(jax.random.fold_in(key, 208), (RECURRENT_OUTPUTS, TEXT_LENGTH), jnp.float32, math.log(0.1), math.log(0.4)))
    return jnp.where(quick_heads[:, None], strong_writes, weak_writes)


def raised(result, key, source, target, parts, factor):
    owner, partner = [(jnp.arange(result.shape[dim]) // (result.shape[dim] // parts)).reshape([-1 if axis == dim else 1 for axis in range(result.ndim)]) for dim in (source, target)]
    chosen = jax.random.permutation(key, parts)[partner]
    strong = (owner == chosen) | (owner == (partner + parts // 2) % parts)
    return jnp.where(strong, factor * result, result)


def steps_of(rng, dims, split, smallest, largest):
    loudness, own = 1.0, jax.random.fold_in(rng, 6)
    for dim, parts in split:
        steps = jnp.exp(jax.random.uniform(jax.random.fold_in(own, dim), (parts,), jnp.float32, smallest / len(split), largest / len(split)))
        loudness = loudness * jnp.repeat(steps, dims[dim] // parts).reshape([-1 if axis == dim else 1 for axis in range(len(dims))])
    return loudness


def scatter_about(rng, dims, deviation, most, cuts=(), kind=jnp.bfloat16):
    result = jax.random.normal(rng, dims, jnp.float32) * deviation
    if len(cuts) > 0:
        result = steps_of(rng, dims, cuts, -0.22, 0.18) * result
    return jnp.clip(result, min=-most, max=most).astype(kind)


def bell_draw_with(stream_key, shape, spread, reach, split, heavy, kind=jnp.bfloat16):
    entries = spread * jax.random.normal(stream_key, shape, jnp.float32)
    if split:
        entries = entries * steps_of(stream_key, shape, split, -0.22, 0.18)
    return jnp.clip(raised(entries, jax.random.fold_in(stream_key, 3), *heavy), -reach, reach).astype(kind)


def setup_inputs(seed: int = 0) -> dict:
    splits = jax.random.split(jax.random.key(seed), 13)
    return {
        "residual": scatter_about(splits[0], (TEXT_LENGTH, D), 0.3, 1.796875, ((0, 32), (1, 8))),
        "queries": draw_queries(jax.random.fold_in(splits[12], 71), 0),
        "key_value_pairs": draw_key_value_pairs(jax.random.fold_in(splits[12], 71), 0),
        "attention_out": bell_draw_with(splits[3], (QUERY_HEAD_COUNT * ATTEND_HEAD_SIZE, D), (QUERY_HEAD_COUNT * ATTEND_HEAD_SIZE) ** -0.5, 0.1875, ((0, 8),), (0, 1, 8, 2.0)),
        "norm_gain": jnp.clip(1.0 + 0.18 * jax.random.normal(splits[4], (D,), jnp.float32), 0.1, 1.9),
        "query_key_weight": scatter_about(splits[5], (D, 2, HK * DK), D ** -0.5, 0.125, ((2, 8),)),
        "value_gate_weight": scatter_about(splits[6], (D, 2, RECURRENT_OUTPUTS * DV), D ** -0.5, 0.125, ((2, 8),)),
        "write_strength": draw_write_strength(jax.random.fold_in(splits[12], 71), 0),
        "log_decay": draw_log_decay(jax.random.fold_in(splits[12], 71), 0),
        "initial_state": scatter_about(splits[9], (RECURRENT_OUTPUTS, DK, DV), 0.05, 0.3, ((0, 8),), jnp.float32),
        "head_gain": jnp.clip(1.0 + 0.18 * jax.random.normal(splits[10], (DV,), jnp.float32), 0.1, 1.9),
        "delta_output": bell_draw_with(splits[11], (RECURRENT_OUTPUTS * DV, D), (RECURRENT_OUTPUTS * DV) ** -0.5, 0.125, ((0, 8),), (0, 1, 8, 2.0)),
    }


highest = lax.Precision.HIGHEST
epsilon = 1e-06

def inverse_rms(values):
    return lax.rsqrt(lax.optimization_barrier(jnp.mean(values * values, axis=-1, keepdims=True)) + epsilon)

def attention_rows(queries, key_value_pairs):
    group_width = QUERY_HEAD_COUNT // KEY_VALUE_HEADS
    padded_rows = jnp.concatenate([jnp.zeros((WINDOW_KEYS, 2, KEY_VALUE_HEADS * ATTEND_HEAD_SIZE), key_value_pairs.dtype), key_value_pairs], axis=0)
    factor = 1.0 / math.sqrt(ATTEND_HEAD_SIZE)

    def one_block(block_index):
        anchor = (block_index * SEQUENCE_ROWS).astype(jnp.int32)
        query_matrix = lax.dynamic_slice_in_dim(queries, anchor, SEQUENCE_ROWS, 0).astype(jnp.float32)
        query_matrix = query_matrix.reshape(SEQUENCE_ROWS, KEY_VALUE_HEADS, group_width, ATTEND_HEAD_SIZE)
        window_matrix = lax.dynamic_slice_in_dim(padded_rows, anchor, WINDOW_KEYS + SEQUENCE_ROWS, 0).astype(jnp.float32)
        key_matrix = window_matrix[:, 0].reshape(WINDOW_KEYS + SEQUENCE_ROWS, KEY_VALUE_HEADS, ATTEND_HEAD_SIZE)
        value_matrix = window_matrix[:, 1].reshape(WINDOW_KEYS + SEQUENCE_ROWS, KEY_VALUE_HEADS, ATTEND_HEAD_SIZE)
        query_pos = anchor + jnp.arange(SEQUENCE_ROWS, dtype=jnp.int32)
        key_pos = anchor - WINDOW_KEYS + jnp.arange(WINDOW_KEYS + SEQUENCE_ROWS, dtype=jnp.int32)
        distance = query_pos[:, None] - key_pos[None, :]
        allowed = (distance >= 0) & (distance < WINDOW_KEYS) & (key_pos[None, :] >= 0)
        scores = jnp.einsum('qhgd,khd->hgqk', query_matrix, key_matrix, precision=highest) * factor
        scores = jnp.where(allowed, scores, -jnp.inf)
        row_peak = lax.optimization_barrier(jnp.max(scores, axis=-1, keepdims=True))
        exponentials = jnp.exp(scores - row_peak)
        weights = (exponentials / lax.optimization_barrier(jnp.sum(exponentials, axis=-1, keepdims=True))).astype(jnp.bfloat16)
        mixed_rows = jnp.einsum('hgqk,khd->qhgd', weights.astype(jnp.float32), value_matrix, precision=highest)
        return mixed_rows.astype(jnp.bfloat16).reshape(SEQUENCE_ROWS, QUERY_HEAD_COUNT * ATTEND_HEAD_SIZE)
    blocks = lax.map(one_block, jnp.arange(TEXT_LENGTH // SEQUENCE_ROWS, dtype=jnp.int32))
    return blocks.reshape(TEXT_LENGTH, QUERY_HEAD_COUNT * ATTEND_HEAD_SIZE)

def delta_rule(delta_query, delta_key, values, decays, strengths, initial_state):
    group_width = RECURRENT_OUTPUTS // HK

    def advance(running_state, inputs):
        query_now, key_now, value_now, decay_now, strength_now = inputs
        grouped = running_state.reshape(HK, group_width, DK, DV)
        recalled = jnp.einsum('hd,hgdv->hgv', key_now, grouped, precision=highest)
        value_grouped = value_now.reshape(HK, group_width, DV)
        decay_grouped = decay_now.reshape(HK, group_width, 1, 1)
        strength_grouped = strength_now.reshape(HK, group_width, 1, 1)
        key_column = key_now[:, None, :, None]
        grouped = decay_grouped * (grouped - strength_grouped * key_column * recalled[:, :, None, :])
        grouped = grouped + strength_grouped * key_column * value_grouped[:, :, None, :]
        output = jnp.einsum('hd,hgdv->hgv', query_now, grouped, precision=highest)
        return (grouped.reshape(RECURRENT_OUTPUTS, DK, DV), output.reshape(RECURRENT_OUTPUTS, DV))
    final_state, outputs = lax.scan(advance, initial_state, (delta_query, delta_key, values, decays, strengths))
    return outputs

def reference(residual, queries, key_value_pairs, attention_out, norm_gain, query_key_weight, value_gate_weight, write_strength, log_decay, initial_state, head_gain, delta_output):
    attention_mix = attention_rows(queries, key_value_pairs)
    branch = jnp.dot(attention_mix, attention_out, preferred_element_type=jnp.float32)
    hidden = residual.astype(jnp.float32) + branch
    normed = (hidden * inverse_rms(hidden) * norm_gain).astype(jnp.bfloat16)
    query_key = jnp.dot(normed, query_key_weight.reshape(D, 2 * HK * DK), preferred_element_type=jnp.float32)
    query_key = query_key.reshape(TEXT_LENGTH, 2, HK, DK)
    value_gate = jnp.dot(normed, value_gate_weight.reshape(D, 2 * RECURRENT_OUTPUTS * DV), preferred_element_type=jnp.float32)
    value_gate = value_gate.reshape(TEXT_LENGTH, 2, RECURRENT_OUTPUTS, DV)
    delta_query = query_key[:, 0]
    delta_query = delta_query * lax.rsqrt(lax.optimization_barrier(jnp.sum(delta_query * delta_query, axis=-1, keepdims=True)) + epsilon) * DK ** (-0.5)
    delta_key = query_key[:, 1]
    delta_key = delta_key * lax.rsqrt(lax.optimization_barrier(jnp.sum(delta_key * delta_key, axis=-1, keepdims=True)) + epsilon)
    decays = jnp.exp(log_decay).T
    strengths = write_strength.T
    delta_mix = delta_rule(delta_query, delta_key, value_gate[:, 0], decays, strengths, initial_state)
    gated = delta_mix * inverse_rms(delta_mix) * head_gain * jax.nn.silu(value_gate[:, 1])
    gated = gated.astype(jnp.bfloat16).reshape(TEXT_LENGTH, RECURRENT_OUTPUTS * DV)
    delta_branch = jnp.dot(gated, delta_output, preferred_element_type=jnp.float32)
    return (hidden + delta_branch).astype(jnp.bfloat16)
```

```python
import math

import jax
import jax.numpy as jnp
from jax import lax
from jax.experimental import pallas as pl
from jax.experimental.pallas import tpu as pltpu
from jax.sharding import PartitionSpec as P

DK = 128
DV = 128
ATTEND_HEAD_SIZE = 128
WINDOW_KEYS = 4096
CHUNK = 128
ROWS = 512
KEY_HEADS = 2
VALUE_HEADS = 4
Z = 8
Y = 4
HALF = DV // 2
MESSAGE = DK + HALF + 16
MESH = pl.DeviceIdType.MESH
f32 = jnp.float32
bf16 = jnp.bfloat16


epsilon = 1e-06


def passed_along(shard, axis, by):
    length = lax.axis_size(axis)
    pairs = [(i, i + by) for i in range(length) if 0 <= i + by < length]
    return lax.ppermute(shard, axis, pairs)


def inverse_rms(values):
    return lax.rsqrt(jnp.mean(values * values, axis=-1, keepdims=True) + epsilon)


def attend(queries, key_value_pairs, seq_index):
    row_count = queries.shape[0]
    reach_pieces = WINDOW_KEYS // row_count
    kv_heads = key_value_pairs.shape[2] // ATTEND_HEAD_SIZE
    query_heads = queries.shape[1] // ATTEND_HEAD_SIZE
    group_width = query_heads // kv_heads
    earlier_rows = jnp.concatenate(
        [passed_along(key_value_pairs, "seq", distance) for distance in range(reach_pieces, 0, -1)],
        axis=0,
    )
    window_matrix = jnp.concatenate([earlier_rows, key_value_pairs], axis=0)
    window_length = window_matrix.shape[0]
    key_matrix = window_matrix[:, 0].reshape(window_length, kv_heads, ATTEND_HEAD_SIZE)
    value_matrix = window_matrix[:, 1].reshape(window_length, kv_heads, ATTEND_HEAD_SIZE)
    query_matrix = queries.reshape(row_count, kv_heads, group_width, ATTEND_HEAD_SIZE)
    query_pos = seq_index * row_count + jnp.arange(row_count, dtype=jnp.int32)
    key_pos = (seq_index - reach_pieces) * row_count + jnp.arange(window_length, dtype=jnp.int32)
    distance_grid = query_pos[:, None] - key_pos[None, :]
    allowed = (distance_grid >= 0) & (distance_grid < WINDOW_KEYS) & (key_pos[None, :] >= 0)
    scores = jnp.einsum(
        "qhgd,khd->hgqk", query_matrix, key_matrix, preferred_element_type=jnp.float32
    ) * (1.0 / math.sqrt(ATTEND_HEAD_SIZE))
    scores = jnp.where(allowed, scores, -jnp.inf)
    row_peak = jnp.max(scores, axis=-1, keepdims=True)
    exponentials = jnp.exp(scores - row_peak)
    weights = (exponentials / jnp.sum(exponentials, axis=-1, keepdims=True)).astype(jnp.bfloat16)
    mixed_rows = jnp.einsum(
        "hgqk,khd->qhgd", weights, value_matrix, preferred_element_type=jnp.float32
    )
    return mixed_rows.astype(jnp.bfloat16).reshape(row_count, query_heads * ATTEND_HEAD_SIZE)


def dot(a, b, contract=((1,), (0,))):
    return lax.dot_general(a, b, (contract, ((), ())), preferred_element_type=f32)


def mm(a, b):
    return dot(a.astype(bf16), b.astype(bf16))


def mm_nt(a, b):
    return dot(a.astype(bf16), b.astype(bf16), ((1,), (1,)))


def split(a):
    high = a.astype(bf16)
    return high, (a - high.astype(f32)).astype(bf16)


def mm2(a, b):
    high, low = split(a)
    return dot(high, b) + dot(low, b)


def mm3(a, b):
    high, low = split(a)
    b_high, b_low = split(b)
    return dot(high, b_high) + dot(low, b_high) + dot(high, b_low)


def grid_of(rows, columns):
    shape = (rows, columns)
    return lax.broadcasted_iota(jnp.int32, shape, 0), lax.broadcasted_iota(jnp.int32, shape, 1)


def three_rows(a):
    high = a.astype(bf16).astype(f32)
    mid = (a - high).astype(bf16).astype(f32)
    low = a - high - mid
    row = lax.broadcasted_iota(jnp.int32, (16, a.shape[1]), 0)
    return jnp.where(row == 0, high, jnp.where(row == 1, mid, jnp.where(row == 2, low, 0.0))).astype(bf16)


def sum_rows(block):
    return jnp.sum(block.astype(f32), axis=0, keepdims=True)


def local_kernel(qk_ref, vg_ref, packed_ref, zero_ref, lead_ref, message_ref, prefix):
    i, j = grid_of(CHUNK, CHUNK)
    inclusive, strict = i >= j, i > j
    eye = (i == j).astype(f32)
    lower = inclusive.astype(f32)
    for h in range(VALUE_HEADS):
        prefix[h] = jnp.concatenate([eye, jnp.zeros_like(eye)], axis=1)
    per_turn = 2

    def turn(t, carry):
        items = []
        for u in range(per_turn):
            rows = pl.ds(pl.multiple_of((t * per_turn + u) * CHUNK, CHUNK), CHUNK)
            packed = packed_ref[:, rows]
            columns = packed.T
            total_row = lax.dot_general(
                packed, lower, (((1,), (1,)), ((), ())),
                precision=lax.Precision.HIGHEST, preferred_element_type=f32)
            total_col = lax.dot_general(
                lower, columns, (((1,), (0,)), ((), ())),
                precision=lax.Precision.HIGHEST, preferred_element_type=f32)
            keys = []
            for kh in range(KEY_HEADS):
                q = qk_ref[rows, kh * DK:(kh + 1) * DK]
                q = q * lax.rsqrt(jnp.sum(q * q, axis=-1, keepdims=True) + epsilon) * DK ** (-0.5)
                at = KEY_HEADS * DK + kh * DK
                k = qk_ref[rows, at:at + DK]
                k = k * lax.rsqrt(jnp.sum(k * k, axis=-1, keepdims=True) + epsilon)
                kb = k.astype(bf16)
                keys.append((q, kb, k.T, mm_nt(kb, kb), mm_nt(q, kb)))
            for h in range(VALUE_HEADS):
                q, k, k_t, key_key, query_key = keys[h // 2]
                cum_col, cum_row = total_col[:, h:h + 1], total_row[h:h + 1, :]
                strength_col = columns[:, VALUE_HEADS + h:VALUE_HEADS + h + 1]
                strength_row = packed[VALUE_HEADS + h:VALUE_HEADS + h + 1, :]
                ratio = jnp.where(inclusive, jnp.exp(jnp.minimum(cum_col - cum_row, 0.0)), 0.0)
                coupling = jnp.where(strict, strength_col * ratio * key_key, 0.0)
                items.append(dict(
                    h=h, rows=rows, q=q, k=k, k_t=k_t, coupling=coupling, mixing=ratio * query_key,
                    cum_col=cum_col, cum_row=cum_row, strength_row=strength_row,
                    inverse=eye - jnp.where((i // 2) == (j // 2), coupling, 0.0)))
        size = 2
        while size < CHUNK:
            level = ((i // (2 * size)) == (j // (2 * size))) & ((i // size) != (j // size))
            for it in items:
                it["half"] = mm(jnp.where(level, it["coupling"], 0.0), it["inverse"])
            for it in items:
                it["inverse"] = it["inverse"] - mm(it["inverse"], it["half"])
            size *= 2
        for it in items:
            scaled = it["inverse"] * it["strength_row"]
            v = vg_ref[it["rows"], it["h"] * DV:(it["h"] + 1) * DV]
            w = mm(scaled * jnp.exp(it["cum_row"]), it["k"])
            u = mm(scaled, v)
            it["wu"] = jnp.concatenate([w, u], axis=1).astype(bf16)
        for it in items:
            mixed = mm(it["mixing"], it["wu"])
            it["lead"] = jnp.exp(it["cum_col"]) * it["q"] - mixed[:, :DK]
            it["own"] = mixed[:, DK:]
            end = it["cum_row"][:, CHUNK - 1:]
            it["end"] = jnp.exp(end)
            it["step"] = mm(it["k_t"] * jnp.exp(end - it["cum_row"]), it["wu"])
        for it in items:
            h = it["h"]
            before = prefix[h]
            out = mm(it["lead"], before)
            lead_ref[it["rows"], h * DK:(h + 1) * DK] = out[:, :DK].astype(bf16)
            zero_ref[it["rows"], h * DV:(h + 1) * DV] = out[:, DK:] + it["own"]
            offset = jnp.concatenate([jnp.zeros((DK, DK), f32), it["step"][:, DK:]], axis=1)
            prefix[h] = it["end"] * before - mm(it["step"][:, :DK], before) + offset
        return carry

    lax.fori_loop(0, ROWS // CHUNK // per_turn, turn, 0)
    slab_decay = jnp.exp(jnp.sum(packed_ref[...], axis=1, keepdims=True))
    for h in range(VALUE_HEADS):
        decay = slab_decay[h:h + 1, :]
        change = (prefix[h, :, :DK] - decay * eye).T.astype(bf16)
        offset = prefix[h, :, DK:].T.astype(bf16)
        tail = three_rows(jnp.broadcast_to(decay, (1, DK)))
        for c in range(2):
            message_ref[2 * h + c, :DK] = change
            message_ref[2 * h + c, DK:DK + HALF] = offset[c * HALF:(c + 1) * HALF]
            message_ref[2 * h + c, DK + HALF:] = tail


def local_part(query_key, value_gate, packed):
    return pl.pallas_call(
        local_kernel,
        out_shape=(
            jax.ShapeDtypeStruct((ROWS, VALUE_HEADS * DV), f32),
            jax.ShapeDtypeStruct((ROWS, VALUE_HEADS * DK), bf16),
            jax.ShapeDtypeStruct((Z, MESSAGE, DK), bf16),
        ),
        in_specs=[pl.BlockSpec(memory_space=pltpu.VMEM)] * 3,
        out_specs=[pl.BlockSpec(memory_space=pltpu.VMEM)] * 3,
        scratch_shapes=[pltpu.VMEM((VALUE_HEADS, DK, DK + DV), f32)],
        compiler_params=pltpu.CompilerParams(vmem_limit_bytes=48 * 2**20),
        name="delta_local",
    )(query_key, value_gate, packed)


FAR_FIRST = (4, 3, 5, 2, 6, 1, 7)


def scan_kernel(message_ref, initial_ref, out_ref, row, total, column, prefix, first, back, landed,
                row_send, row_recv, col_send, col_recv, back_send, back_recv):
    s = lax.axis_index("seq")
    y, z = s // Z, s % Z

    def in_row(d):
        return {"seq": y * Z + (z + d) % Z}

    def in_column(d):
        return {"seq": ((y + d) % Y) * Z + z}

    barrier = pltpu.get_barrier_semaphore()
    for d in range(1, Z):
        pl.semaphore_signal(barrier, inc=1, device_id=in_row(d), device_id_type=MESH)
    for d in range(1, Y):
        pl.semaphore_signal(barrier, inc=1, device_id=in_column(d), device_id_type=MESH)
    pl.semaphore_wait(barrier, Z - 1 + Y - 1)

    sends = []
    for d in FAR_FIRST:
        copy = pltpu.make_async_remote_copy(
            src_ref=message_ref.at[(z + d) % Z], dst_ref=row.at[z], send_sem=row_send.at[d],
            recv_sem=row_recv.at[d], device_id=in_row(d), device_id_type=MESH)
        copy.start()
        sends.append(copy)
    row[z] = message_ref[z]
    first[...] = initial_ref[z // 2].T
    i, j = grid_of(DK + HALF, DK)
    x = (i == j).astype(f32)
    decay = jnp.ones((1, DK), f32)
    for copy in sends:
        copy.wait()
    zero = jnp.zeros((DK, DK), f32)
    for place in range(Z):
        prefix[place] = x
        a = sum_rows(row[place, DK + HALF:])
        offset = jnp.concatenate([zero, row[place, DK:DK + HALF].astype(f32)], axis=0)
        x = a * x + mm2(x, row[place, :DK]) + offset
        decay = decay * a
    total[:DK + HALF] = jnp.where(i == j, x - decay, x).astype(bf16)
    total[DK + HALF:] = three_rows(decay)
    sends = []
    for d in (2, 1, 3):
        copy = pltpu.make_async_remote_copy(
            src_ref=total, dst_ref=column.at[y], send_sem=col_send.at[d], recv_sem=col_recv.at[d],
            device_id=in_column(d), device_id_type=MESH)
        copy.start()
        sends.append(copy)
    column[y] = total[...]
    state = first[pl.ds(pl.multiple_of((z % 2) * HALF, HALF), HALF), :]
    for copy in sends:
        copy.wait()
    for place in range(Y - 1):
        a = sum_rows(column[place, DK + HALF:])
        after = a * state + mm2(state, column[place, :DK]) + column[place, DK:DK + HALF].astype(f32)
        state = jnp.where(place < y, after, state)
    for place in range(Z):
        entering = mm3(state, prefix[place, :DK]) + prefix[place, DK:]
        back[place] = entering.astype(bf16)
    sends = []
    for d in FAR_FIRST:
        copy = pltpu.make_async_remote_copy(
            src_ref=back.at[(z + d) % Z], dst_ref=landed.at[z], send_sem=back_send.at[d],
            recv_sem=back_recv.at[d], device_id=in_row(d), device_id_type=MESH)
        copy.start()
        sends.append(copy)
    landed[z] = back[z]
    for copy in sends:
        copy.wait()
    out_ref[...] = landed[...]


def entering_states(messages, initial_state):
    dma = pltpu.SemaphoreType.DMA
    return pl.pallas_call(
        scan_kernel,
        out_shape=jax.ShapeDtypeStruct((Z, HALF, DK), bf16),
        in_specs=[pl.BlockSpec(memory_space=pltpu.VMEM)] * 2,
        out_specs=pl.BlockSpec(memory_space=pltpu.VMEM),
        scratch_shapes=[
            pltpu.VMEM((Z, MESSAGE, DK), bf16),
            pltpu.VMEM((MESSAGE, DK), bf16),
            pltpu.VMEM((Y, MESSAGE, DK), bf16),
            pltpu.VMEM((Z, DK + HALF, DK), f32),
            pltpu.VMEM((DV, DK), f32),
            pltpu.VMEM((Z, HALF, DK), bf16),
            pltpu.VMEM((Z, HALF, DK), bf16),
            dma((Z,)), dma((Z,)), dma((Y,)), dma((Y,)), dma((Z,)), dma((Z,)),
        ],
        compiler_params=pltpu.CompilerParams(
            collective_id=1, has_side_effects=True, vmem_limit_bytes=32 * 2**20),
        name="delta_scan",
    )(messages, initial_state)


def body(
    residual,
    queries,
    key_value_pairs,
    attention_out,
    norm_gain,
    query_key_weight,
    value_gate_weight,
    write_strength,
    log_decay,
    initial_state,
    head_gain,
    delta_output,
):
    row_count = residual.shape[0]
    share_width = residual.shape[1]
    model_width = norm_gain.shape[0]
    seq_index = lax.axis_index("seq")
    head_index = lax.axis_index("head")
    attention_mix = attend(queries, key_value_pairs, seq_index)
    branch = jnp.dot(attention_mix, attention_out, preferred_element_type=jnp.float32)
    query_cols = query_key_weight.shape[2]
    value_cols = value_gate_weight.shape[2]
    flat_query_key = query_key_weight.reshape(model_width, 2 * query_cols)
    flat_value_gate = value_gate_weight.reshape(model_width, 2 * value_cols)
    placed = lax.dynamic_update_slice_in_dim(
        jnp.zeros_like(branch), residual.astype(jnp.float32), head_index * share_width, 1
    )
    hidden_full = lax.psum(branch + placed, "head")
    hidden = lax.dynamic_slice_in_dim(hidden_full, head_index * share_width, share_width, 1)
    normed = (hidden_full * inverse_rms(hidden_full) * norm_gain).astype(jnp.bfloat16)
    query_key = jnp.dot(normed, flat_query_key, preferred_element_type=jnp.float32)
    value_gate = jnp.dot(normed, flat_value_gate, preferred_element_type=jnp.float32)
    value_heads = value_cols // DV
    packed = jnp.concatenate([log_decay, write_strength], axis=0)
    zero_part, lead, messages = local_part(query_key, value_gate, packed)
    states = entering_states(messages, initial_state).reshape(value_heads, DV, DK)
    met = jnp.einsum(
        "thd,hed->the", lead.reshape(row_count, value_heads, DK), states, preferred_element_type=f32
    )
    delta_mix = zero_part.reshape(row_count, value_heads, DV) + met
    gate = value_gate[:, value_cols:].reshape(row_count, value_heads, DV)
    gated = delta_mix * inverse_rms(delta_mix) * head_gain * jax.nn.silu(gate)
    gated = gated.astype(jnp.bfloat16).reshape(row_count, value_heads * DV)
    delta_branch = jnp.dot(gated, delta_output, preferred_element_type=jnp.float32)
    delta_share = lax.psum_scatter(delta_branch, "head", scatter_dimension=1, tiled=True)
    return (hidden + delta_share).astype(jnp.bfloat16)


def solution(mesh):
    return jax.shard_map(
        body,
        mesh=mesh,
        in_specs=(
            P("seq", "head"),
            P("seq", "head"),
            P("seq", None, "head"),
            P("head", None),
            P(),
            P(None, None, "head"),
            P(None, None, "head"),
            P("head", "seq"),
            P("head", "seq"),
            P("head", None, None),
            P(),
            P("head", None),
        ),
        out_specs=P("seq", "head"),
        check_vma=False,
    )
```

```python
import math

import jax
import jax.numpy as jnp
from jax import lax
from jax.experimental import pallas as pl
from jax.experimental.pallas import tpu as pltpu
from jax.sharding import PartitionSpec as P

DK = 128
DV = 128
ATTEND_HEAD_SIZE = 128
WINDOW_KEYS = 4096
X = 4
HEADS = 8
MODEL = 2048
SHARE = 256
PROJECTED = 1536
TILE = 256
CHUNK = 128
ROWS = 512
KEY_HEADS = 2
VALUE_HEADS = 4
Z = 8
Y = 4
HALF = DV // 2
MESSAGE = DK + HALF + 16
MESH = pl.DeviceIdType.MESH
f32 = jnp.float32
bf16 = jnp.bfloat16


epsilon = 1e-06


def dot(a, b, contract=((1,), (0,))):
    return lax.dot_general(a, b, (contract, ((), ())), preferred_element_type=f32)


def mm(a, b):
    return dot(a.astype(bf16), b.astype(bf16))


def mm_nt(a, b):
    return dot(a.astype(bf16), b.astype(bf16), ((1,), (1,)))


def split(a):
    high = a.astype(bf16)
    return high, (a - high.astype(f32)).astype(bf16)


def mm2(a, b):
    high, low = split(a)
    return dot(high, b) + dot(low, b)


def mm3(a, b):
    high, low = split(a)
    b_high, b_low = split(b)
    return dot(high, b_high) + dot(low, b_high) + dot(high, b_low)


def grid_of(rows, columns):
    shape = (rows, columns)
    return lax.broadcasted_iota(jnp.int32, shape, 0), lax.broadcasted_iota(jnp.int32, shape, 1)


def three_rows(a):
    high = a.astype(bf16).astype(f32)
    mid = (a - high).astype(bf16).astype(f32)
    low = a - high - mid
    row = lax.broadcasted_iota(jnp.int32, (16, a.shape[1]), 0)
    return jnp.where(row == 0, high, jnp.where(row == 1, mid, jnp.where(row == 2, low, 0.0))).astype(bf16)


def sum_rows(block):
    return jnp.sum(block.astype(f32), axis=0, keepdims=True)


def local_kernel(qk_ref, vg_ref, packed_ref, zero_ref, lead_ref, message_ref, prefix):
    i, j = grid_of(CHUNK, CHUNK)
    inclusive, strict = i >= j, i > j
    eye = (i == j).astype(f32)
    lower = inclusive.astype(f32)
    for h in range(VALUE_HEADS):
        prefix[h] = jnp.concatenate([eye, jnp.zeros_like(eye)], axis=1)
    per_turn = 2

    def turn(t, carry):
        items = []
        for u in range(per_turn):
            rows = pl.ds(pl.multiple_of((t * per_turn + u) * CHUNK, CHUNK), CHUNK)
            packed = packed_ref[:, rows]
            columns = packed.T
            total_row = lax.dot_general(
                packed, lower, (((1,), (1,)), ((), ())),
                precision=lax.Precision.HIGHEST, preferred_element_type=f32)
            total_col = lax.dot_general(
                lower, columns, (((1,), (0,)), ((), ())),
                precision=lax.Precision.HIGHEST, preferred_element_type=f32)
            keys = []
            for kh in range(KEY_HEADS):
                q = qk_ref[rows, kh * DK:(kh + 1) * DK]
                q = q * lax.rsqrt(jnp.sum(q * q, axis=-1, keepdims=True) + epsilon) * DK ** (-0.5)
                at = KEY_HEADS * DK + kh * DK
                k = qk_ref[rows, at:at + DK]
                k = k * lax.rsqrt(jnp.sum(k * k, axis=-1, keepdims=True) + epsilon)
                kb = k.astype(bf16)
                keys.append((q, kb, k.T, mm_nt(kb, kb), mm_nt(q, kb)))
            for h in range(VALUE_HEADS):
                q, k, k_t, key_key, query_key = keys[h // 2]
                cum_col, cum_row = total_col[:, h:h + 1], total_row[h:h + 1, :]
                strength_col = columns[:, VALUE_HEADS + h:VALUE_HEADS + h + 1]
                strength_row = packed[VALUE_HEADS + h:VALUE_HEADS + h + 1, :]
                ratio = jnp.where(inclusive, jnp.exp(jnp.minimum(cum_col - cum_row, 0.0)), 0.0)
                coupling = jnp.where(strict, strength_col * ratio * key_key, 0.0)
                items.append(dict(
                    h=h, rows=rows, q=q, k=k, k_t=k_t, coupling=coupling, mixing=ratio * query_key,
                    cum_col=cum_col, cum_row=cum_row, strength_row=strength_row,
                    inverse=eye - jnp.where((i // 2) == (j // 2), coupling, 0.0)))
        size = 2
        while size < CHUNK:
            level = ((i // (2 * size)) == (j // (2 * size))) & ((i // size) != (j // size))
            for it in items:
                it["half"] = mm(jnp.where(level, it["coupling"], 0.0), it["inverse"])
            for it in items:
                it["inverse"] = it["inverse"] - mm(it["inverse"], it["half"])
            size *= 2
        for it in items:
            scaled = it["inverse"] * it["strength_row"]
            v = vg_ref[it["rows"], it["h"] * DV:(it["h"] + 1) * DV]
            w = mm(scaled * jnp.exp(it["cum_row"]), it["k"])
            u = mm(scaled, v)
            it["wu"] = jnp.concatenate([w, u], axis=1).astype(bf16)
        for it in items:
            mixed = mm(it["mixing"], it["wu"])
            it["lead"] = jnp.exp(it["cum_col"]) * it["q"] - mixed[:, :DK]
            it["own"] = mixed[:, DK:]
            end = it["cum_row"][:, CHUNK - 1:]
            it["end"] = jnp.exp(end)
            it["step"] = mm(it["k_t"] * jnp.exp(end - it["cum_row"]), it["wu"])
        for it in items:
            h = it["h"]
            before = prefix[h]
            out = mm(it["lead"], before)
            lead_ref[it["rows"], h * DK:(h + 1) * DK] = out[:, :DK].astype(bf16)
            zero_ref[it["rows"], h * DV:(h + 1) * DV] = out[:, DK:] + it["own"]
            offset = jnp.concatenate([jnp.zeros((DK, DK), f32), it["step"][:, DK:]], axis=1)
            prefix[h] = it["end"] * before - mm(it["step"][:, :DK], before) + offset
        return carry

    lax.fori_loop(0, ROWS // CHUNK // per_turn, turn, 0)
    slab_decay = jnp.exp(jnp.sum(packed_ref[...], axis=1, keepdims=True))
    for h in range(VALUE_HEADS):
        decay = slab_decay[h:h + 1, :]
        change = (prefix[h, :, :DK] - decay * eye).T.astype(bf16)
        offset = prefix[h, :, DK:].T.astype(bf16)
        tail = three_rows(jnp.broadcast_to(decay, (1, DK)))
        for c in range(2):
            message_ref[2 * h + c, :DK] = change
            message_ref[2 * h + c, DK:DK + HALF] = offset[c * HALF:(c + 1) * HALF]
            message_ref[2 * h + c, DK + HALF:] = tail


def local_part(query_key, value_gate, packed):
    return pl.pallas_call(
        local_kernel,
        out_shape=(
            jax.ShapeDtypeStruct((ROWS, VALUE_HEADS * DV), f32),
            jax.ShapeDtypeStruct((ROWS, VALUE_HEADS * DK), bf16),
            jax.ShapeDtypeStruct((Z, MESSAGE, DK), bf16),
        ),
        in_specs=[pl.BlockSpec(memory_space=pltpu.VMEM)] * 3,
        out_specs=[pl.BlockSpec(memory_space=pltpu.VMEM)] * 3,
        scratch_shapes=[pltpu.VMEM((VALUE_HEADS, DK, DK + DV), f32)],
        compiler_params=pltpu.CompilerParams(vmem_limit_bytes=48 * 2**20),
        name="delta_local",
    )(query_key, value_gate, packed)


def at_head(x, c):
    return {"head": (x % X) * 2 + c}


def send(source, target, send_sem, recv_sem, device):
    copy = pltpu.make_async_remote_copy(
        src_ref=source, dst_ref=target, send_sem=send_sem, recv_sem=recv_sem,
        device_id=device, device_id_type=MESH)
    copy.start()
    return copy


def greet(devices):
    barrier = pltpu.get_barrier_semaphore()
    for device in devices:
        pl.semaphore_signal(barrier, inc=1, device_id=device, device_id_type=MESH)
    pl.semaphore_wait(barrier, len(devices))


def gather_heads(blocks, send_sem, recv_sem, x, c, use):
    mid = ROWS // 2
    own, left, right, far = (((x + d) % X) * 2 + c for d in (0, -1 + X, 1, 2))
    over = [((x + d) % X) * 2 + 1 - c for d in (0, X - 1, 1, 2)]
    sibling, to_left, to_right = at_head(x, 1 - c), at_head(x + X - 1, c), at_head(x + 1, c)

    def go(n, block, device, rows=slice(None)):
        ref = blocks.at[block] if rows == slice(None) else blocks.at[block, rows]
        return send(ref, ref, send_sem.at[n], recv_sem.at[n], device)

    copies = [go(1, own, to_right), go(2, own, to_left), go(0, own, sibling)]
    copies[2].wait_recv()
    use(0, (own, over[0]))
    copies[0].wait_recv()
    copies.append(go(3, left, to_right, slice(0, mid)))
    copies.append(go(4, left, sibling))
    copies[1].wait_recv()
    copies.append(go(5, right, to_left, slice(mid, ROWS)))
    copies.append(go(6, right, sibling))
    use(1, (left, right))
    copies[4].wait_recv()
    copies[6].wait_recv()
    use(2, (over[1], over[2]))
    copies[3].wait_recv()
    copies[5].wait_recv()
    copies.append(go(7, far, sibling))
    copies[7].wait_recv()
    use(3, (far, over[3]))
    for copy in copies:
        copy.wait_send()


def attend_block(queries, window, place, peak, total, relation):
    scale = math.log2(math.e) / math.sqrt(ATTEND_HEAD_SIZE)
    ones = jnp.ones((ROWS, ATTEND_HEAD_SIZE), bf16)

    def tile(t, carry):
        rows = pl.ds(pl.multiple_of(t * TILE, TILE), TILE)
        keys = window[place, :, :ATTEND_HEAD_SIZE]
        values = jnp.concatenate([window[place, :, ATTEND_HEAD_SIZE:], ones], axis=1)
        scores = mm_nt(queries[rows, :], keys) * scale
        if relation is not None:
            i, j = grid_of(TILE, ROWS)
            i = i + lax.rem(t, ROWS // TILE) * TILE
            scores = jnp.where(i >= j if relation == "causal" else i < j, scores, -jnp.inf)
        block_peak = jnp.max(scores, axis=-1, keepdims=True)
        if relation == "causal":
            weights = jnp.exp2(scores - block_peak).astype(bf16)
            total[rows, :] = dot(weights, values)
            peak[rows, :] = jnp.broadcast_to(block_peak, (TILE, ATTEND_HEAD_SIZE))
        else:
            before = peak[rows, :1]
            now = jnp.maximum(before, block_peak)
            weights = jnp.exp2(scores - now).astype(bf16)
            total[rows, :] = total[rows, :] * jnp.exp2(before - now) + dot(weights, values)
            peak[rows, :] = jnp.broadcast_to(now, (TILE, ATTEND_HEAD_SIZE))
        return carry

    lax.fori_loop(0, 2 * ROWS // TILE, tile, 0)


def front_kernel(queries_ref, pairs_ref, out_weight_ref, residual_ref, gain_ref, qk_weight_ref,
                 vg_weight_ref, hidden_ref, qk_ref, vg_ref,
                 queries, window, peak, total, out_weight, mix, normed, branch, projected, squares,
                 qk_weight, vg_weight,
                 kv_send, kv_recv, ow_send, ow_recv, mix_send, mix_recv, norm_send, norm_recv,
                 local_sem):
    s, head = lax.axis_index("seq"), lax.axis_index("head")
    seq_count = Y * Z
    x, c = head // 2, head % 2

    def along(d):
        return {"seq": (s + d + seq_count) % seq_count}

    def other(d):
        return {"head": (head + d) % HEADS}

    locals_ = [
        pltpu.make_async_copy(pairs_ref, window.at[0], local_sem.at[0]),
        pltpu.make_async_copy(qk_weight_ref, qk_weight, local_sem.at[1]),
        pltpu.make_async_copy(vg_weight_ref, vg_weight, local_sem.at[2]),
        pltpu.make_async_copy(
            out_weight_ref.at[:, pl.ds(pl.multiple_of(head * SHARE, SHARE), SHARE)],
            out_weight.at[head], local_sem.at[3]),
    ]
    for copy in locals_:
        copy.start()
    greet([along(1), along(-1), along(-Z)] + [other(d) for d in range(1, HEADS)])

    def hop(n, source, target, by):
        return send(source, target, kv_send.at[n], kv_recv.at[n], along(by))

    half = ROWS // 2
    to_next, to_row, before = 1, Z, -1
    hops = {1: hop(1, pairs_ref, window.at[1], to_next), 8: hop(8, pairs_ref, window.at[8], to_row)}
    weights = []
    for d in range(1, HEADS):
        target = (head + d) % HEADS
        weights.append(send(
            out_weight_ref.at[:, pl.ds(pl.multiple_of(target * SHARE, SHARE), SHARE)],
            out_weight.at[head], ow_send.at[d], ow_recv.at[d], other(d)))
    for g in range(2):
        queries[g * ROWS:(g + 1) * ROWS, :] = queries_ref[:, g * ATTEND_HEAD_SIZE:(g + 1) * ATTEND_HEAD_SIZE]
    locals_[0].wait()
    attend_block(queries, window, 0, peak, total, "causal")

    def attend_earlier(d):
        @pl.when(s >= d)
        def _():
            attend_block(queries, window, d, peak, total, "window" if d == Z else None)

    hops[1].wait_recv()
    hops[2] = hop(2, window.at[1], window.at[2], to_next)
    hops[8].wait_recv()
    hops[7] = hop(7, window.at[8], window.at[7], before)
    attend_earlier(1)
    hops[2].wait_recv()
    hops[3] = hop(3, window.at[2], window.at[3], to_next)
    hops[7].wait_recv()
    hops[6] = hop(6, window.at[7], window.at[6], before)
    attend_earlier(8)
    attend_earlier(2)
    hops[3].wait_recv()
    hops[4] = hop(4, window.at[3, 0:half], window.at[4, 0:half], to_next)
    hops[6].wait_recv()
    hops[5] = hop(5, window.at[6], window.at[5], before)
    attend_earlier(7)
    attend_earlier(3)
    hops[5].wait_recv()
    hops[0] = hop(0, window.at[5, half:ROWS], window.at[4, half:ROWS], before)
    attend_earlier(6)
    attend_earlier(5)
    hops[4].wait_recv()
    hops[0].wait_recv()
    attend_earlier(4)
    for g in range(2):
        rows = slice(g * ROWS, (g + 1) * ROWS)
        mix[head, :, g * ATTEND_HEAD_SIZE:(g + 1) * ATTEND_HEAD_SIZE] = (
            total[rows, :ATTEND_HEAD_SIZE] / total[rows, ATTEND_HEAD_SIZE:]).astype(bf16)
    for copy in weights:
        copy.wait()
    locals_[3].wait()

    def add_branch(turn, pair):
        a, b = pair
        part = dot(mix[a], out_weight[a]) + dot(mix[b], out_weight[b])
        branch[...] = part if turn == 0 else branch[...] + part

    gather_heads(mix, mix_send, mix_recv, x, c, add_branch)
    hidden = residual_ref[...].astype(f32) + branch[...]
    hidden_ref[...] = hidden
    own = pl.ds(pl.multiple_of(head * SHARE, SHARE), SHARE)
    normed[head] = (hidden * gain_ref[:, own]).astype(bf16)
    locals_[1].wait()
    locals_[2].wait()

    def add_projected(turn, pair):
        square = None
        for block in pair:
            cols = pl.ds(pl.multiple_of(block * SHARE, SHARE), SHARE)
            value = normed[block].astype(f32) * (1.0 / gain_ref[:, cols])
            value = value * value
            value = value[:, :128] + value[:, 128:]
            square = value if square is None else square + value
        squares[...] = square if turn == 0 else squares[...] + square
        a, b = (pl.ds(pl.multiple_of(block * SHARE, SHARE), SHARE) for block in pair)
        for weight, at in ((qk_weight, 0), (vg_weight, 2 * KEY_HEADS * DK)):
            for column in range(0, weight.shape[1], 256):
                cols = slice(column, column + 256)
                part = dot(normed[pair[0]], weight[a, cols]) + dot(normed[pair[1]], weight[b, cols])
                to = slice(at + column, at + column + 256)
                projected[:, to] = part if turn == 0 else projected[:, to] + part

    gather_heads(normed, norm_send, norm_recv, x, c, add_projected)
    inverse = lax.rsqrt(jnp.sum(squares[...], axis=-1, keepdims=True) * (1.0 / MODEL) + epsilon)
    qk_ref[...] = projected[:, :512] * inverse
    vg_ref[...] = projected[:, 512:] * inverse
    for n in range(9):
        hops[n].wait_send()


def front_part(queries, pairs, attention_out, residual, gain, qk_weight, vg_weight):
    vmem, hbm = pl.BlockSpec(memory_space=pltpu.VMEM), pl.BlockSpec(memory_space=pl.ANY)
    dma = pltpu.SemaphoreType.DMA
    return pl.pallas_call(
        front_kernel,
        out_shape=(
            jax.ShapeDtypeStruct((ROWS, SHARE), f32),
            jax.ShapeDtypeStruct((ROWS, 512), f32),
            jax.ShapeDtypeStruct((ROWS, 1024), f32),
        ),
        in_specs=[vmem, hbm, hbm, vmem, vmem, hbm, hbm],
        out_specs=[vmem] * 3,
        scratch_shapes=[
            pltpu.VMEM((2 * ROWS, ATTEND_HEAD_SIZE), bf16),
            pltpu.VMEM((Z + 1, ROWS, 2 * ATTEND_HEAD_SIZE), bf16),
            pltpu.VMEM((2 * ROWS, ATTEND_HEAD_SIZE), f32),
            pltpu.VMEM((2 * ROWS, 2 * ATTEND_HEAD_SIZE), f32),
            pltpu.VMEM((HEADS, SHARE, SHARE), bf16),
            pltpu.VMEM((HEADS, ROWS, SHARE), bf16),
            pltpu.VMEM((HEADS, ROWS, SHARE), bf16),
            pltpu.VMEM((ROWS, SHARE), f32),
            pltpu.VMEM((ROWS, PROJECTED), f32),
            pltpu.VMEM((ROWS, 128), f32),
            pltpu.VMEM((MODEL, 512), bf16),
            pltpu.VMEM((MODEL, 1024), bf16),
            dma((9,)), dma((9,)), dma((HEADS,)), dma((HEADS,)), dma((8,)), dma((8,)), dma((8,)),
            dma((8,)), dma((4,)),
        ],
        compiler_params=pltpu.CompilerParams(
            collective_id=0, has_side_effects=True, vmem_limit_bytes=56 * 2**20),
        name="front",
    )(queries, pairs, attention_out, residual, gain, qk_weight, vg_weight)


FAR_FIRST = (4, 3, 5, 2, 6, 1, 7)


def scan_kernel(message_ref, initial_ref, zero_ref, lead_ref, vg_ref, gain_ref, weight_ref,
                hidden_ref, out_ref,
                row, total, column, prefix, first, back, landed,
                gate, gated, to_sibling, from_sibling, far, relay, near, arrived,
                row_send, row_recv, col_send, col_recv, back_send, back_recv,
                pair_send, pair_recv, out_send, out_recv):
    s = lax.axis_index("seq")
    y, z = s // Z, s % Z

    def in_row(d):
        return {"seq": y * Z + (z + d) % Z}

    def in_column(d):
        return {"seq": ((y + d) % Y) * Z + z}

    head = lax.axis_index("head")
    x, c = head // 2, head % 2
    sibling, to_left, to_right = at_head(x, 1 - c), at_head(x + X - 1, c), at_head(x + 1, c)
    greet([in_row(d) for d in range(1, Z)] + [in_column(d) for d in range(1, Y)]
          + [sibling, to_left, to_right])

    sends = []
    for d in FAR_FIRST:
        copy = pltpu.make_async_remote_copy(
            src_ref=message_ref.at[(z + d) % Z], dst_ref=row.at[z], send_sem=row_send.at[d],
            recv_sem=row_recv.at[d], device_id=in_row(d), device_id_type=MESH)
        copy.start()
        sends.append(copy)
    row[z] = message_ref[z]
    first[...] = initial_ref[z // 2].T
    i, j = grid_of(DK + HALF, DK)
    run = (i == j).astype(f32)
    decay = jnp.ones((1, DK), f32)
    for h in range(VALUE_HEADS):
        cols = slice(h * DV, (h + 1) * DV)
        u = vg_ref[:, VALUE_HEADS * DV + h * DV:VALUE_HEADS * DV + (h + 1) * DV]
        gate[:, cols] = gain_ref[...] * (u / (1.0 + jnp.exp(-u)))
    for copy in sends:
        copy.wait()
    zero = jnp.zeros((DK, DK), f32)
    for place in range(Z):
        prefix[place] = run
        a = sum_rows(row[place, DK + HALF:])
        offset = jnp.concatenate([zero, row[place, DK:DK + HALF].astype(f32)], axis=0)
        run = a * run + mm2(run, row[place, :DK]) + offset
        decay = decay * a
    total[:DK + HALF] = jnp.where(i == j, run - decay, run).astype(bf16)
    total[DK + HALF:] = three_rows(decay)
    sends = []
    for d in (2, 1, 3):
        copy = pltpu.make_async_remote_copy(
            src_ref=total, dst_ref=column.at[y], send_sem=col_send.at[d], recv_sem=col_recv.at[d],
            device_id=in_column(d), device_id_type=MESH)
        copy.start()
        sends.append(copy)
    column[y] = total[...]
    state = first[pl.ds(pl.multiple_of((z % 2) * HALF, HALF), HALF), :]
    for copy in sends:
        copy.wait()
    for place in range(Y - 1):
        a = sum_rows(column[place, DK + HALF:])
        after = a * state + mm2(state, column[place, :DK]) + column[place, DK:DK + HALF].astype(f32)
        state = jnp.where(place < y, after, state)
    for place in range(Z):
        entering = mm3(state, prefix[place, :DK]) + prefix[place, DK:]
        back[place] = entering.astype(bf16)
    sends = []
    for d in FAR_FIRST:
        copy = pltpu.make_async_remote_copy(
            src_ref=back.at[(z + d) % Z], dst_ref=landed.at[z], send_sem=back_send.at[d],
            recv_sem=back_recv.at[d], device_id=in_row(d), device_id_type=MESH)
        copy.start()
        sends.append(copy)
    landed[z] = back[z]
    for copy in sends:
        copy.wait()
    for h in range(VALUE_HEADS):
        cols = slice(h * DV, (h + 1) * DV)
        state = jnp.concatenate([landed[2 * h], landed[2 * h + 1]], axis=0)
        delta = zero_ref[:, cols] + mm_nt(lead_ref[:, cols], state)
        gated[:, cols] = (delta * inverse_rms(delta) * gate[:, cols]).astype(bf16)

    def partial(d, core):
        at = ((x + d) % X * 2 + core) * SHARE
        return dot(gated[...], weight_ref[:, pl.ds(pl.multiple_of(at, SHARE), SHARE)])

    order, half = (2, 1, X - 1, 0), ROWS // 2
    top, bottom = slice(0, half), slice(half, ROWS)
    pairs = []
    for n, d in enumerate(order):
        to_sibling[n] = partial(d, 1 - c).astype(bf16)
        pairs.append(send(to_sibling.at[n], from_sibling.at[n], pair_send.at[n], pair_recv.at[n], sibling))
    sends = []
    pairs[0].wait_recv()
    far[...] = (partial(2, c) + from_sibling[0].astype(f32)).astype(bf16)
    sends.append(send(far.at[top], relay.at[0], out_send.at[0], out_recv.at[0], to_right))
    sends.append(send(far.at[bottom], relay.at[1], out_send.at[1], out_recv.at[1], to_left))
    for n, rows, device in ((1, top, to_right), (2, bottom, to_left)):
        value = partial(order[n], c)
        pairs[n].wait_recv()
        value = value + from_sibling[n].astype(f32)
        sends[n - 1].wait_recv()
        passed = relay[n - 1].astype(f32)
        if n == 1:
            near[0] = jnp.concatenate([value[top] + passed, value[bottom]], axis=0).astype(bf16)
        else:
            near[1] = jnp.concatenate([value[top], value[bottom] + passed], axis=0).astype(bf16)
        sends.append(send(near.at[n - 1], arrived.at[n - 1], out_send.at[n + 1], out_recv.at[n + 1], device))
    value = hidden_ref[...] + partial(0, c)
    pairs[3].wait_recv()
    value = value + from_sibling[3].astype(f32)
    sends[2].wait_recv()
    sends[3].wait_recv()
    out_ref[...] = (value + arrived[0].astype(f32) + arrived[1].astype(f32)).astype(bf16)
    for copy in pairs + sends:
        copy.wait_send()


def back_part(messages, initial_state, zero_part, lead, value_gate, head_gain, delta_output, hidden):
    dma = pltpu.SemaphoreType.DMA
    return pl.pallas_call(
        scan_kernel,
        out_shape=jax.ShapeDtypeStruct((ROWS, SHARE), bf16),
        in_specs=[pl.BlockSpec(memory_space=pltpu.VMEM)] * 8,
        out_specs=pl.BlockSpec(memory_space=pltpu.VMEM),
        scratch_shapes=[
            pltpu.VMEM((Z, MESSAGE, DK), bf16),
            pltpu.VMEM((MESSAGE, DK), bf16),
            pltpu.VMEM((Y, MESSAGE, DK), bf16),
            pltpu.VMEM((Z, DK + HALF, DK), f32),
            pltpu.VMEM((DV, DK), f32),
            pltpu.VMEM((Z, HALF, DK), bf16),
            pltpu.VMEM((Z, HALF, DK), bf16),
            pltpu.VMEM((ROWS, VALUE_HEADS * DV), f32),
            pltpu.VMEM((ROWS, VALUE_HEADS * DV), bf16),
            pltpu.VMEM((X, ROWS, SHARE), bf16),
            pltpu.VMEM((X, ROWS, SHARE), bf16),
            pltpu.VMEM((ROWS, SHARE), bf16),
            pltpu.VMEM((2, ROWS // 2, SHARE), bf16),
            pltpu.VMEM((2, ROWS, SHARE), bf16),
            pltpu.VMEM((2, ROWS, SHARE), bf16),
            dma((Z,)), dma((Z,)), dma((Y,)), dma((Y,)), dma((Z,)), dma((Z,)),
            dma((X,)), dma((X,)), dma((X,)), dma((X,)),
        ],
        compiler_params=pltpu.CompilerParams(
            collective_id=1, has_side_effects=True, vmem_limit_bytes=48 * 2**20),
        name="delta_scan_out",
    )(messages, initial_state, zero_part, lead, value_gate, head_gain, delta_output, hidden)


def inverse_rms(values):
    return lax.rsqrt(jnp.mean(values * values, axis=-1, keepdims=True) + epsilon)


def body(residual, queries, key_value_pairs, attention_out, norm_gain, query_key_weight,
         value_gate_weight, write_strength, log_decay, initial_state, head_gain, delta_output):
    hidden, query_key, value_gate = front_part(
        queries, key_value_pairs.reshape(ROWS, 2 * ATTEND_HEAD_SIZE), attention_out, residual,
        norm_gain.reshape(1, MODEL), query_key_weight.reshape(MODEL, -1),
        value_gate_weight.reshape(MODEL, -1))
    packed = jnp.concatenate([log_decay, write_strength], axis=0)
    zero_part, lead, messages = local_part(query_key, value_gate, packed)
    return back_part(messages, initial_state, zero_part, lead, value_gate,
                     head_gain.reshape(1, DV), delta_output, hidden)


def solution(mesh):
    return jax.shard_map(
        body,
        mesh=mesh,
        in_specs=(
            P("seq", "head"),
            P("seq", "head"),
            P("seq", None, "head"),
            P("head", None),
            P(),
            P(None, None, "head"),
            P(None, None, "head"),
            P("head", "seq"),
            P("head", "seq"),
            P("head", None, None),
            P(),
            P("head", None),
        ),
        out_specs=P("seq", "head"),
        check_vma=False,
    )
```

```python
import math

import jax
import jax.numpy as jnp
from jax import lax
from jax.experimental import pallas as pl
from jax.experimental.pallas import tpu as pltpu
from jax.sharding import PartitionSpec as P

DK = 128
DV = 128
ATTEND_HEAD_SIZE = 128
WINDOW_KEYS = 4096
X = 4
HEADS = 8
MODEL = 2048
SHARE = 256
PROJECTED = 1536
TILE = 256
CHUNK = 128
ROWS = 512
KEY_HEADS = 2
VALUE_HEADS = 4
Z = 8
Y = 4
HALF = DV // 2
MESSAGE = DK + HALF + 16
MESH = pl.DeviceIdType.MESH
f32 = jnp.float32
bf16 = jnp.bfloat16


epsilon = 1e-06


def dot(a, b, contract=((1,), (0,))):
    return lax.dot_general(a, b, (contract, ((), ())), preferred_element_type=f32)


def mm(a, b):
    return dot(a.astype(bf16), b.astype(bf16))


def mm_nt(a, b):
    return dot(a.astype(bf16), b.astype(bf16), ((1,), (1,)))


def split(a):
    high = a.astype(bf16)
    return high, (a - high.astype(f32)).astype(bf16)


def mm2(a, b):
    high, low = split(a)
    return dot(high, b) + dot(low, b)


def mm3(a, b):
    high, low = split(a)
    b_high, b_low = split(b)
    return dot(high, b_high) + dot(low, b_high) + dot(high, b_low)


def grid_of(rows, columns):
    shape = (rows, columns)
    return lax.broadcasted_iota(jnp.int32, shape, 0), lax.broadcasted_iota(jnp.int32, shape, 1)


def three_rows(a):
    high = a.astype(bf16).astype(f32)
    mid = (a - high).astype(bf16).astype(f32)
    low = a - high - mid
    row = lax.broadcasted_iota(jnp.int32, (16, a.shape[1]), 0)
    return jnp.where(row == 0, high, jnp.where(row == 1, mid, jnp.where(row == 2, low, 0.0))).astype(bf16)


def sum_rows(block):
    return jnp.sum(block.astype(f32), axis=0, keepdims=True)


def local_slab(projected, inverse_ref, packed_ref, zero_ref, lead_ref, message_ref, prefix):
    i, j = grid_of(CHUNK, CHUNK)
    inclusive, strict = i >= j, i > j
    eye = (i == j).astype(f32)
    lower = inclusive.astype(f32)
    for h in range(VALUE_HEADS):
        prefix[h] = jnp.concatenate([eye, jnp.zeros_like(eye)], axis=1)
    per_turn = 2

    def turn(t, carry):
        items = []
        for u in range(per_turn):
            rows = pl.ds(pl.multiple_of((t * per_turn + u) * CHUNK, CHUNK), CHUNK)
            packed = packed_ref[:, rows]
            columns = packed.T
            total_row = lax.dot_general(
                packed, lower, (((1,), (1,)), ((), ())),
                precision=lax.Precision.HIGHEST, preferred_element_type=f32)
            total_col = lax.dot_general(
                lower, columns, (((1,), (0,)), ((), ())),
                precision=lax.Precision.HIGHEST, preferred_element_type=f32)
            keys = []
            for kh in range(KEY_HEADS):
                q = projected[rows, kh * DK:(kh + 1) * DK] * inverse_ref[rows, :]
                q = q * lax.rsqrt(jnp.sum(q * q, axis=-1, keepdims=True) + epsilon) * DK ** (-0.5)
                at = KEY_HEADS * DK + kh * DK
                k = projected[rows, at:at + DK] * inverse_ref[rows, :]
                k = k * lax.rsqrt(jnp.sum(k * k, axis=-1, keepdims=True) + epsilon)
                kb = k.astype(bf16)
                keys.append((q, kb, k.T, mm_nt(kb, kb), mm_nt(q, kb)))
            for h in range(VALUE_HEADS):
                q, k, k_t, key_key, query_key = keys[h // 2]
                cum_col, cum_row = total_col[:, h:h + 1], total_row[h:h + 1, :]
                strength_col = columns[:, VALUE_HEADS + h:VALUE_HEADS + h + 1]
                strength_row = packed[VALUE_HEADS + h:VALUE_HEADS + h + 1, :]
                ratio = jnp.where(inclusive, jnp.exp(jnp.minimum(cum_col - cum_row, 0.0)), 0.0)
                coupling = jnp.where(strict, strength_col * ratio * key_key, 0.0)
                items.append(dict(
                    h=h, rows=rows, q=q, k=k, k_t=k_t, coupling=coupling, mixing=ratio * query_key,
                    cum_col=cum_col, cum_row=cum_row, strength_row=strength_row,
                    inverse=eye - jnp.where((i // 2) == (j // 2), coupling, 0.0)))
        size = 2
        while size < CHUNK:
            level = ((i // (2 * size)) == (j // (2 * size))) & ((i // size) != (j // size))
            for it in items:
                it["half"] = mm(jnp.where(level, it["coupling"], 0.0), it["inverse"])
            for it in items:
                it["inverse"] = it["inverse"] - mm(it["inverse"], it["half"])
            size *= 2
        for it in items:
            scaled = it["inverse"] * it["strength_row"]
            at = 2 * KEY_HEADS * DK + it["h"] * DV
            v = projected[it["rows"], at:at + DV] * inverse_ref[it["rows"], :]
            w = mm(scaled * jnp.exp(it["cum_row"]), it["k"])
            u = mm(scaled, v)
            it["wu"] = jnp.concatenate([w, u], axis=1).astype(bf16)
        for it in items:
            mixed = mm(it["mixing"], it["wu"])
            it["lead"] = jnp.exp(it["cum_col"]) * it["q"] - mixed[:, :DK]
            it["own"] = mixed[:, DK:]
            end = it["cum_row"][:, CHUNK - 1:]
            it["end"] = jnp.exp(end)
            it["step"] = mm(it["k_t"] * jnp.exp(end - it["cum_row"]), it["wu"])
        for it in items:
            h = it["h"]
            before = prefix[h]
            out = mm(it["lead"], before)
            lead_ref[it["rows"], h * DK:(h + 1) * DK] = out[:, :DK].astype(bf16)
            zero_ref[it["rows"], h * DV:(h + 1) * DV] = out[:, DK:] + it["own"]
            offset = jnp.concatenate([jnp.zeros((DK, DK), f32), it["step"][:, DK:]], axis=1)
            prefix[h] = it["end"] * before - mm(it["step"][:, :DK], before) + offset
        return carry

    lax.fori_loop(0, ROWS // CHUNK // per_turn, turn, 0)
    slab_decay = jnp.exp(jnp.sum(packed_ref[...], axis=1, keepdims=True))
    for h in range(VALUE_HEADS):
        decay = slab_decay[h:h + 1, :]
        change = (prefix[h, :, :DK] - decay * eye).T.astype(bf16)
        offset = prefix[h, :, DK:].T.astype(bf16)
        tail = three_rows(jnp.broadcast_to(decay, (1, DK)))
        for c in range(2):
            message_ref[2 * h + c, :DK] = change
            message_ref[2 * h + c, DK:DK + HALF] = offset[c * HALF:(c + 1) * HALF]
            message_ref[2 * h + c, DK + HALF:] = tail


def at_head(x, c):
    return {"head": (x % X) * 2 + c}


def send(source, target, send_sem, recv_sem, device):
    copy = pltpu.make_async_remote_copy(
        src_ref=source, dst_ref=target, send_sem=send_sem, recv_sem=recv_sem,
        device_id=device, device_id_type=MESH)
    copy.start()
    return copy


def greet(devices):
    barrier = pltpu.get_barrier_semaphore()
    for device in devices:
        pl.semaphore_signal(barrier, inc=1, device_id=device, device_id_type=MESH)
    pl.semaphore_wait(barrier, len(devices))


def gather_heads(blocks, send_sem, recv_sem, x, c, use):
    mid = ROWS // 2
    top, bottom = slice(0, mid), slice(mid, ROWS)
    own, left, right, far = (((x + d) % X) * 2 + c for d in (0, X - 1, 1, 2))
    over = [((x + d) % X) * 2 + 1 - c for d in (0, X - 1, 1, 2)]
    sibling, to_left, to_right = at_head(x, 1 - c), at_head(x + X - 1, c), at_head(x + 1, c)
    copies = {}

    def go(n, block, device, rows=None):
        ref = blocks.at[block] if rows is None else blocks.at[block, rows]
        copies[n] = send(ref, ref, send_sem.at[n], recv_sem.at[n], device)

    go(1, own, to_right, top)
    go(3, own, to_left, bottom)
    go(0, own, sibling)
    go(2, own, to_right, bottom)
    go(4, own, to_left, top)
    copies[0].wait_recv()
    use(0, (own, over[0]))
    copies[1].wait_recv()
    go(5, left, to_right, top)
    copies[3].wait_recv()
    go(6, right, to_left, bottom)
    copies[2].wait_recv()
    go(7, left, sibling)
    copies[4].wait_recv()
    go(8, right, sibling)
    use(1, (left, right))
    copies[5].wait_recv()
    go(9, far, sibling, top)
    copies[6].wait_recv()
    go(10, far, sibling, bottom)
    copies[7].wait_recv()
    copies[8].wait_recv()
    use(2, (over[1], over[2]))
    use(3, (far,))
    copies[9].wait_recv()
    copies[10].wait_recv()
    use(4, (over[3],))
    for copy in copies.values():
        copy.wait_send()


def attend_block(queries, window, place, peak, total, relation):
    scale = math.log2(math.e) / math.sqrt(ATTEND_HEAD_SIZE)
    ones = jnp.ones((ROWS, ATTEND_HEAD_SIZE), bf16)

    def tile(t, carry):
        rows = pl.ds(pl.multiple_of(t * TILE, TILE), TILE)
        keys = window[place, :, :ATTEND_HEAD_SIZE]
        values = jnp.concatenate([window[place, :, ATTEND_HEAD_SIZE:], ones], axis=1)
        scores = mm_nt(queries[rows, :], keys) * scale
        if relation is not None:
            i, j = grid_of(TILE, ROWS)
            i = i + lax.rem(t, ROWS // TILE) * TILE
            scores = jnp.where(i >= j if relation == "causal" else i < j, scores, -jnp.inf)
        block_peak = jnp.max(scores, axis=-1, keepdims=True)
        if relation == "causal":
            weights = jnp.exp2(scores - block_peak).astype(bf16)
            total[rows, :] = dot(weights, values)
            peak[rows, :] = jnp.broadcast_to(block_peak, (TILE, ATTEND_HEAD_SIZE))
        else:
            before = peak[rows, :1]
            now = jnp.maximum(before, block_peak)
            weights = jnp.exp2(scores - now).astype(bf16)
            total[rows, :] = total[rows, :] * jnp.exp2(before - now) + dot(weights, values)
            peak[rows, :] = jnp.broadcast_to(now, (TILE, ATTEND_HEAD_SIZE))
        return carry

    lax.fori_loop(0, 2 * ROWS // TILE, tile, 0)


FAR_FIRST = (4, 3, 5, 2, 6, 1, 7)


def straight(raw, weight, at, turn):
    width = raw.shape[2]

    def step(t, carry):
        rows = pl.ds(pl.multiple_of(turn * 256 + t * 64, 64), 64)
        value = raw[rows]
        weight[rows, at:at + width] = value[:, 0, :]
        weight[rows, at + width:at + 2 * width] = value[:, 1, :]
        return carry

    lax.fori_loop(0, 4, step, 0)


def layer_kernel(queries_ref, pairs_ref, out_weight_ref, residual_ref, gain_ref, qk_weight_ref,
                 vg_weight_ref, packed_ref, initial_ref, head_gain_ref, delta_weight_ref, out_ref,
                 queries, window, peak, total_mix, out_weight, mix, normed, hidden_ref, projected,
                 squares, qk_raw, vg_raw, weight, delta_weight,
                 zero_ref, lead_ref, message_ref, slab_prefix,
                 row, total, column, prefix, first, back, landed,
                 gate, gated, to_sibling, from_sibling, far, relay, near, arrived,
                 kv_send, kv_recv, ow_send, ow_recv, mix_send, mix_recv, norm_send, norm_recv,
                 local_sem, row_send, row_recv, col_send, col_recv, back_send, back_recv,
                 pair_send, pair_recv, out_send, out_recv):
    s, head = lax.axis_index("seq"), lax.axis_index("head")
    seq_count = Y * Z
    y, z = s // Z, s % Z
    x, c = head // 2, head % 2
    sibling, to_left, to_right = at_head(x, 1 - c), at_head(x + X - 1, c), at_head(x + 1, c)

    def along(d):
        return {"seq": (s + d + seq_count) % seq_count}

    def other(d):
        return {"head": (head + d) % HEADS}

    def in_row(d):
        return {"seq": y * Z + (z + d) % Z}

    def in_column(d):
        return {"seq": ((y + d) % Y) * Z + z}

    own_columns = pl.ds(pl.multiple_of(head * SHARE, SHARE), SHARE)
    locals_ = [
        pltpu.make_async_copy(pairs_ref, window.at[0], local_sem.at[0]),
        pltpu.make_async_copy(qk_weight_ref, qk_raw, local_sem.at[1]),
        pltpu.make_async_copy(vg_weight_ref, vg_raw, local_sem.at[2]),
        pltpu.make_async_copy(out_weight_ref.at[:, own_columns], out_weight.at[head], local_sem.at[3]),
        pltpu.make_async_copy(delta_weight_ref, delta_weight, local_sem.at[4]),
    ]
    locals_[0].start()
    greet([along(1), along(-1)] + [other(d) for d in range(1, HEADS)]
          + [in_row(d) for d in range(1, Z)] + [in_column(d) for d in range(1, Y)])

    half = ROWS // 2
    halves = (slice(0, half), slice(half, ROWS))
    hops = {}

    def hop(d, part, by):
        source = {1: 0, Z: 0}.get(d, d - 1 if by == 1 else d + 1)
        rows = halves[part]
        n = 2 * d + part
        source_ref = pairs_ref.at[rows] if source == 0 else window.at[source, rows]
        hops[n] = send(source_ref, window.at[d, rows], kv_send.at[n], kv_recv.at[n], along(by))

    def landed_part(d, part, by):
        hops[2 * d + part].wait_recv()
        if by == 1 and (d < 3 or (d == 3 and part == 0)):
            hop(d + 1, part, 1)
        if by == -1 and (d > 5 or (d == 5 and part == 1)):
            hop(d - 1, part, -1)

    hop(Z, 1, Z)
    hop(1, 0, 1)
    hop(Z, 0, Z)
    hop(1, 1, 1)
    for copy in locals_[1:]:
        copy.start()
    weights = []
    for d in range(1, HEADS):
        target = (head + d) % HEADS
        weights.append(send(
            out_weight_ref.at[:, pl.ds(pl.multiple_of(target * SHARE, SHARE), SHARE)],
            out_weight.at[head], ow_send.at[d], ow_recv.at[d], other(d)))
    for g in range(2):
        queries[g * ROWS:(g + 1) * ROWS, :] = queries_ref[:, g * ATTEND_HEAD_SIZE:(g + 1) * ATTEND_HEAD_SIZE]
    locals_[0].wait()
    attend_block(queries, window, 0, peak, total_mix, "causal")

    def attend_earlier(d):
        @pl.when(s >= d)
        def _():
            attend_block(queries, window, d, peak, total_mix, "window" if d == Z else None)

    def prepare(turn):
        straight(qk_raw, weight, 0, turn)
        straight(vg_raw, weight, 2 * KEY_HEADS * DK, turn)

    landed_part(1, 0, 1)
    landed_part(Z, 1, -1)
    landed_part(1, 1, 1)
    landed_part(Z, 0, -1)
    attend_earlier(1)
    landed_part(7, 1, -1)
    locals_[1].wait()
    locals_[2].wait()
    prepare(0)
    landed_part(2, 0, 1)
    attend_earlier(Z)
    landed_part(7, 0, -1)
    attend_earlier(7)
    landed_part(2, 1, 1)
    prepare(1)
    landed_part(6, 1, -1)
    attend_earlier(2)
    landed_part(3, 0, 1)
    prepare(2)
    landed_part(6, 0, -1)
    attend_earlier(6)
    landed_part(3, 1, 1)
    prepare(3)
    prepare(4)
    landed_part(5, 1, -1)
    attend_earlier(3)
    landed_part(4, 0, 1)
    prepare(5)
    prepare(6)
    prepare(7)
    landed_part(5, 0, -1)
    attend_earlier(5)
    landed_part(4, 1, -1)
    attend_earlier(4)
    for g in range(2):
        rows = slice(g * ROWS, (g + 1) * ROWS)
        mix[head, :, g * ATTEND_HEAD_SIZE:(g + 1) * ATTEND_HEAD_SIZE] = (
            total_mix[rows, :ATTEND_HEAD_SIZE] / total_mix[rows, ATTEND_HEAD_SIZE:]).astype(bf16)
    for copy in weights:
        copy.wait()
    locals_[3].wait()
    locals_[4].wait()
    for copy in hops.values():
        copy.wait_send()

    def add_branch(turn, blocks):
        part = sum(dot(mix[b], out_weight[b]) for b in blocks)
        hidden_ref[...] = part if turn == 0 else hidden_ref[...] + part

    gather_heads(mix, mix_send, mix_recv, x, c, add_branch)
    hidden = residual_ref[...].astype(f32) + hidden_ref[...]
    hidden_ref[...] = hidden
    normed[head] = (hidden * gain_ref[:, own_columns]).astype(bf16)

    def add_projected(turn, blocks):
        square = None
        for block in blocks:
            cols = pl.ds(pl.multiple_of(block * SHARE, SHARE), SHARE)
            value = normed[block].astype(f32) * (1.0 / gain_ref[:, cols])
            value = value * value
            value = value[:, :128] + value[:, 128:]
            square = value if square is None else square + value
        squares[...] = square if turn == 0 else squares[...] + square
        for at in range(0, PROJECTED, 256):
            cols = slice(at, at + 256)
            part = sum(
                dot(normed[b], weight[pl.ds(pl.multiple_of(b * SHARE, SHARE), SHARE), cols])
                for b in blocks)
            projected[:, cols] = part if turn == 0 else projected[:, cols] + part

    gather_heads(normed, norm_send, norm_recv, x, c, add_projected)
    inverse = lax.rsqrt(jnp.sum(squares[...], axis=-1, keepdims=True) * (1.0 / MODEL) + epsilon)
    squares[...] = jnp.broadcast_to(inverse, (ROWS, 128))
    local_slab(projected, squares, packed_ref, zero_ref, lead_ref, message_ref, slab_prefix)

    sends = []
    for d in FAR_FIRST:
        copy = pltpu.make_async_remote_copy(
            src_ref=message_ref.at[(z + d) % Z], dst_ref=row.at[z], send_sem=row_send.at[d],
            recv_sem=row_recv.at[d], device_id=in_row(d), device_id_type=MESH)
        copy.start()
        sends.append(copy)
    row[z] = message_ref[z]
    first[...] = initial_ref[z // 2].T
    i, j = grid_of(DK + HALF, DK)
    run = (i == j).astype(f32)
    decay = jnp.ones((1, DK), f32)
    for h in range(VALUE_HEADS):
        cols = slice(h * DV, (h + 1) * DV)
        at = 2 * KEY_HEADS * DK + (VALUE_HEADS + h) * DV
        u = projected[:, at:at + DV] * squares[...]
        gate[:, cols] = head_gain_ref[...] * (u / (1.0 + jnp.exp(-u)))
    for copy in sends:
        copy.wait()
    zero = jnp.zeros((DK, DK), f32)
    for place in range(Z):
        prefix[place] = run
        a = sum_rows(row[place, DK + HALF:])
        offset = jnp.concatenate([zero, row[place, DK:DK + HALF].astype(f32)], axis=0)
        run = a * run + mm2(run, row[place, :DK]) + offset
        decay = decay * a
    total[:DK + HALF] = jnp.where(i == j, run - decay, run).astype(bf16)
    total[DK + HALF:] = three_rows(decay)
    sends = []
    for d in (2, 1, 3):
        copy = pltpu.make_async_remote_copy(
            src_ref=total, dst_ref=column.at[y], send_sem=col_send.at[d], recv_sem=col_recv.at[d],
            device_id=in_column(d), device_id_type=MESH)
        copy.start()
        sends.append(copy)
    column[y] = total[...]
    state = first[pl.ds(pl.multiple_of((z % 2) * HALF, HALF), HALF), :]
    for copy in sends:
        copy.wait()
    for place in range(Y - 1):
        a = sum_rows(column[place, DK + HALF:])
        after = a * state + mm2(state, column[place, :DK]) + column[place, DK:DK + HALF].astype(f32)
        state = jnp.where(place < y, after, state)
    for place in range(Z):
        entering = mm3(state, prefix[place, :DK]) + prefix[place, DK:]
        back[place] = entering.astype(bf16)
    sends = []
    for d in FAR_FIRST:
        copy = pltpu.make_async_remote_copy(
            src_ref=back.at[(z + d) % Z], dst_ref=landed.at[z], send_sem=back_send.at[d],
            recv_sem=back_recv.at[d], device_id=in_row(d), device_id_type=MESH)
        copy.start()
        sends.append(copy)
    landed[z] = back[z]
    for copy in sends:
        copy.wait()
    for h in range(VALUE_HEADS):
        cols = slice(h * DV, (h + 1) * DV)
        state = jnp.concatenate([landed[2 * h], landed[2 * h + 1]], axis=0)
        delta = zero_ref[:, cols] + mm_nt(lead_ref[:, cols], state)
        gated[:, cols] = (delta * inverse_rms(delta) * gate[:, cols]).astype(bf16)

    def partial(d, core):
        at = ((x + d) % X * 2 + core) * SHARE
        return dot(gated[...], delta_weight[:, pl.ds(pl.multiple_of(at, SHARE), SHARE)])

    order, half = (2, 1, X - 1, 0), ROWS // 2
    top, bottom = slice(0, half), slice(half, ROWS)
    pairs = []
    for n, d in enumerate(order):
        to_sibling[n] = partial(d, 1 - c).astype(bf16)
        pairs.append(send(to_sibling.at[n], from_sibling.at[n], pair_send.at[n], pair_recv.at[n], sibling))
    sends = []
    pairs[0].wait_recv()
    far[...] = (partial(2, c) + from_sibling[0].astype(f32)).astype(bf16)
    sends.append(send(far.at[top], relay.at[0], out_send.at[0], out_recv.at[0], to_right))
    sends.append(send(far.at[bottom], relay.at[1], out_send.at[1], out_recv.at[1], to_left))
    for n, rows, device in ((1, top, to_right), (2, bottom, to_left)):
        value = partial(order[n], c)
        pairs[n].wait_recv()
        value = value + from_sibling[n].astype(f32)
        sends[n - 1].wait_recv()
        passed = relay[n - 1].astype(f32)
        if n == 1:
            near[0] = jnp.concatenate([value[top] + passed, value[bottom]], axis=0).astype(bf16)
        else:
            near[1] = jnp.concatenate([value[top], value[bottom] + passed], axis=0).astype(bf16)
        sends.append(send(near.at[n - 1], arrived.at[n - 1], out_send.at[n + 1], out_recv.at[n + 1], device))
    value = hidden_ref[...] + partial(0, c)
    pairs[3].wait_recv()
    value = value + from_sibling[3].astype(f32)
    sends[2].wait_recv()
    sends[3].wait_recv()
    out_ref[...] = (value + arrived[0].astype(f32) + arrived[1].astype(f32)).astype(bf16)
    for copy in pairs + sends:
        copy.wait_send()


def inverse_rms(values):
    return lax.rsqrt(jnp.mean(values * values, axis=-1, keepdims=True) + epsilon)


def body(residual, queries, key_value_pairs, attention_out, norm_gain, query_key_weight,
         value_gate_weight, write_strength, log_decay, initial_state, head_gain, delta_output):
    vmem, hbm = pl.BlockSpec(memory_space=pltpu.VMEM), pl.BlockSpec(memory_space=pl.ANY)
    dma = pltpu.SemaphoreType.DMA
    packed = jnp.concatenate([log_decay, write_strength], axis=0)
    return pl.pallas_call(
        layer_kernel,
        out_shape=jax.ShapeDtypeStruct((ROWS, SHARE), bf16),
        in_specs=[vmem, hbm, hbm, vmem, vmem, hbm, hbm, vmem, vmem, vmem, hbm],
        out_specs=vmem,
        scratch_shapes=[
            pltpu.VMEM((2 * ROWS, ATTEND_HEAD_SIZE), bf16),
            pltpu.VMEM((Z + 1, ROWS, 2 * ATTEND_HEAD_SIZE), bf16),
            pltpu.VMEM((2 * ROWS, ATTEND_HEAD_SIZE), f32),
            pltpu.VMEM((2 * ROWS, 2 * ATTEND_HEAD_SIZE), f32),
            pltpu.VMEM((HEADS, SHARE, SHARE), bf16),
            pltpu.VMEM((HEADS, ROWS, SHARE), bf16),
            pltpu.VMEM((HEADS, ROWS, SHARE), bf16),
            pltpu.VMEM((ROWS, SHARE), f32),
            pltpu.VMEM((ROWS, PROJECTED), f32),
            pltpu.VMEM((ROWS, 128), f32),
            pltpu.VMEM((MODEL, 2, KEY_HEADS * DK), bf16),
            pltpu.VMEM((MODEL, 2, VALUE_HEADS * DV), bf16),
            pltpu.VMEM((MODEL, PROJECTED), bf16),
            pltpu.VMEM((VALUE_HEADS * DV, MODEL), bf16),
            pltpu.VMEM((ROWS, VALUE_HEADS * DV), f32),
            pltpu.VMEM((ROWS, VALUE_HEADS * DK), bf16),
            pltpu.VMEM((Z, MESSAGE, DK), bf16),
            pltpu.VMEM((VALUE_HEADS, DK, DK + DV), f32),
            pltpu.VMEM((Z, MESSAGE, DK), bf16),
            pltpu.VMEM((MESSAGE, DK), bf16),
            pltpu.VMEM((Y, MESSAGE, DK), bf16),
            pltpu.VMEM((Z, DK + HALF, DK), f32),
            pltpu.VMEM((DV, DK), f32),
            pltpu.VMEM((Z, HALF, DK), bf16),
            pltpu.VMEM((Z, HALF, DK), bf16),
            pltpu.VMEM((ROWS, VALUE_HEADS * DV), f32),
            pltpu.VMEM((ROWS, VALUE_HEADS * DV), bf16),
            pltpu.VMEM((X, ROWS, SHARE), bf16),
            pltpu.VMEM((X, ROWS, SHARE), bf16),
            pltpu.VMEM((ROWS, SHARE), bf16),
            pltpu.VMEM((2, ROWS // 2, SHARE), bf16),
            pltpu.VMEM((2, ROWS, SHARE), bf16),
            pltpu.VMEM((2, ROWS, SHARE), bf16),
            dma((2 * Z + 2,)), dma((2 * Z + 2,)), dma((HEADS,)), dma((HEADS,)),
            dma((11,)), dma((11,)), dma((11,)), dma((11,)), dma((5,)),
            dma((Z,)), dma((Z,)), dma((Y,)), dma((Y,)), dma((Z,)), dma((Z,)),
            dma((X,)), dma((X,)), dma((X,)), dma((X,)),
        ],
        compiler_params=pltpu.CompilerParams(
            collective_id=0, has_side_effects=True, vmem_limit_bytes=60 * 2**20),
        name="layer",
    )(queries, key_value_pairs.reshape(ROWS, 2 * ATTEND_HEAD_SIZE), attention_out, residual,
      norm_gain.reshape(1, MODEL), query_key_weight, value_gate_weight, packed, initial_state,
      head_gain.reshape(1, DV), delta_output)


def solution(mesh):
    return jax.shard_map(
        body,
        mesh=mesh,
        in_specs=(
            P("seq", "head"),
            P("seq", "head"),
            P("seq", None, "head"),
            P("head", None),
            P(),
            P(None, None, "head"),
            P(None, None, "head"),
            P("head", "seq"),
            P("head", "seq"),
            P("head", None, None),
            P(),
            P("head", None),
        ),
        out_specs=P("seq", "head"),
        check_vma=False,
    )
```

```python
import math

import jax
import jax.numpy as jnp
from jax import lax
from jax.experimental import pallas as pl
from jax.experimental.pallas import tpu as pltpu
from jax.sharding import PartitionSpec as P

DK = 128
DV = 128
ATTEND_HEAD_SIZE = 128
WINDOW_KEYS = 4096
X = 4
HEADS = 8
MODEL = 2048
SHARE = 256
PROJECTED = 1536
TILE = 256
CHUNK = 128
ROWS = 512
KEY_HEADS = 2
VALUE_HEADS = 4
Z = 8
Y = 4
HALF = DV // 2
MESSAGE = DK + HALF + 16
MESH = pl.DeviceIdType.MESH
f32 = jnp.float32
bf16 = jnp.bfloat16


epsilon = 1e-06


def dot(a, b, contract=((1,), (0,))):
    return lax.dot_general(a, b, (contract, ((), ())), preferred_element_type=f32)


def mm(a, b):
    return dot(a.astype(bf16), b.astype(bf16))


def mm_nt(a, b):
    return dot(a.astype(bf16), b.astype(bf16), ((1,), (1,)))


def split(a):
    high = a.astype(bf16)
    return high, (a - high.astype(f32)).astype(bf16)


def mm2(a, b):
    high, low = split(a)
    return dot(high, b) + dot(low, b)


def mm3(a, b):
    high, low = split(a)
    b_high, b_low = split(b)
    return dot(high, b_high) + dot(low, b_high) + dot(high, b_low)


def grid_of(rows, columns):
    shape = (rows, columns)
    return lax.broadcasted_iota(jnp.int32, shape, 0), lax.broadcasted_iota(jnp.int32, shape, 1)


def three_rows(a):
    high = a.astype(bf16).astype(f32)
    mid = (a - high).astype(bf16).astype(f32)
    low = a - high - mid
    row = lax.broadcasted_iota(jnp.int32, (16, a.shape[1]), 0)
    return jnp.where(row == 0, high, jnp.where(row == 1, mid, jnp.where(row == 2, low, 0.0))).astype(bf16)


def sum_rows(block):
    return jnp.sum(block.astype(f32), axis=0, keepdims=True)


def local_slab(projected, inverse_ref, packed_ref, zero_ref, lead_ref, message_ref, prefix):
    i, j = grid_of(CHUNK, CHUNK)
    inclusive, strict = i >= j, i > j
    eye = (i == j).astype(f32)
    lower = inclusive.astype(f32)
    for h in range(VALUE_HEADS):
        prefix[h] = jnp.concatenate([eye, jnp.zeros_like(eye)], axis=1)
    per_turn = 2

    def turn(t, carry):
        items = []
        for u in range(per_turn):
            rows = pl.ds(pl.multiple_of((t * per_turn + u) * CHUNK, CHUNK), CHUNK)
            packed = packed_ref[:, rows]
            columns = packed.T
            total_row = lax.dot_general(
                packed, lower, (((1,), (1,)), ((), ())),
                precision=lax.Precision.HIGHEST, preferred_element_type=f32)
            total_col = lax.dot_general(
                lower, columns, (((1,), (0,)), ((), ())),
                precision=lax.Precision.HIGHEST, preferred_element_type=f32)
            keys = []
            for kh in range(KEY_HEADS):
                q = projected[rows, kh * DK:(kh + 1) * DK] * inverse_ref[rows, :]
                q = q * lax.rsqrt(jnp.sum(q * q, axis=-1, keepdims=True) + epsilon) * DK ** (-0.5)
                at = KEY_HEADS * DK + kh * DK
                k = projected[rows, at:at + DK] * inverse_ref[rows, :]
                k = k * lax.rsqrt(jnp.sum(k * k, axis=-1, keepdims=True) + epsilon)
                kb = k.astype(bf16)
                keys.append((q, kb, k.T, mm_nt(kb, kb), mm_nt(q, kb)))
            for h in range(VALUE_HEADS):
                q, k, k_t, key_key, query_key = keys[h // 2]
                cum_col, cum_row = total_col[:, h:h + 1], total_row[h:h + 1, :]
                strength_col = columns[:, VALUE_HEADS + h:VALUE_HEADS + h + 1]
                strength_row = packed[VALUE_HEADS + h:VALUE_HEADS + h + 1, :]
                ratio = jnp.where(inclusive, jnp.exp(jnp.minimum(cum_col - cum_row, 0.0)), 0.0)
                coupling = jnp.where(strict, strength_col * ratio * key_key, 0.0)
                items.append(dict(
                    h=h, rows=rows, q=q, k=k, k_t=k_t, coupling=coupling, mixing=ratio * query_key,
                    cum_col=cum_col, cum_row=cum_row, strength_row=strength_row,
                    inverse=eye - jnp.where((i // 2) == (j // 2), coupling, 0.0)))
        size = 2
        while size < CHUNK:
            level = ((i // (2 * size)) == (j // (2 * size))) & ((i // size) != (j // size))
            for it in items:
                it["half"] = mm(jnp.where(level, it["coupling"], 0.0), it["inverse"])
            for it in items:
                it["inverse"] = it["inverse"] - mm(it["inverse"], it["half"])
            size *= 2
        for it in items:
            scaled = it["inverse"] * it["strength_row"]
            at = 2 * KEY_HEADS * DK + it["h"] * DV
            v = projected[it["rows"], at:at + DV] * inverse_ref[it["rows"], :]
            w = mm(scaled * jnp.exp(it["cum_row"]), it["k"])
            u = mm(scaled, v)
            it["wu"] = jnp.concatenate([w, u], axis=1).astype(bf16)
        for it in items:
            mixed = mm(it["mixing"], it["wu"])
            it["lead"] = jnp.exp(it["cum_col"]) * it["q"] - mixed[:, :DK]
            it["own"] = mixed[:, DK:]
            end = it["cum_row"][:, CHUNK - 1:]
            it["end"] = jnp.exp(end)
            it["step"] = mm(it["k_t"] * jnp.exp(end - it["cum_row"]), it["wu"])
        for it in items:
            h = it["h"]
            before = prefix[h]
            out = mm(it["lead"], before)
            lead_ref[it["rows"], h * DK:(h + 1) * DK] = out[:, :DK].astype(bf16)
            zero_ref[it["rows"], h * DV:(h + 1) * DV] = out[:, DK:] + it["own"]
            offset = jnp.concatenate([jnp.zeros((DK, DK), f32), it["step"][:, DK:]], axis=1)
            prefix[h] = it["end"] * before - mm(it["step"][:, :DK], before) + offset
        return carry

    lax.fori_loop(0, ROWS // CHUNK // per_turn, turn, 0)
    slab_decay = jnp.exp(jnp.sum(packed_ref[...], axis=1, keepdims=True))
    for h in range(VALUE_HEADS):
        decay = slab_decay[h:h + 1, :]
        change = (prefix[h, :, :DK] - decay * eye).T.astype(bf16)
        offset = prefix[h, :, DK:].T.astype(bf16)
        tail = three_rows(jnp.broadcast_to(decay, (1, DK)))
        for c in range(2):
            message_ref[2 * h + c, :DK] = change
            message_ref[2 * h + c, DK:DK + HALF] = offset[c * HALF:(c + 1) * HALF]
            message_ref[2 * h + c, DK + HALF:] = tail


def at_head(x, c):
    return {"head": (x % X) * 2 + c}


def send(source, target, send_sem, recv_sem, device):
    copy = pltpu.make_async_remote_copy(
        src_ref=source, dst_ref=target, send_sem=send_sem, recv_sem=recv_sem,
        device_id=device, device_id_type=MESH)
    copy.start()
    return copy


def greet(devices):
    barrier = pltpu.get_barrier_semaphore()
    for device in devices:
        pl.semaphore_signal(barrier, inc=1, device_id=device, device_id_type=MESH)
    pl.semaphore_wait(barrier, len(devices))


def gather_heads(blocks, send_sem, recv_sem, x, c, use):
    mid = ROWS // 2
    top, bottom = slice(0, mid), slice(mid, ROWS)
    own, left, right, far = (((x + d) % X) * 2 + c for d in (0, X - 1, 1, 2))
    over = [((x + d) % X) * 2 + 1 - c for d in (0, X - 1, 1, 2)]
    sibling, to_left, to_right = at_head(x, 1 - c), at_head(x + X - 1, c), at_head(x + 1, c)
    copies = {}

    def go(n, block, device, rows=None):
        ref = blocks.at[block] if rows is None else blocks.at[block, rows]
        copies[n] = send(ref, ref, send_sem.at[n], recv_sem.at[n], device)

    go(1, own, to_right, top)
    go(3, own, to_left, bottom)
    go(0, own, sibling)
    go(2, own, to_right, bottom)
    go(4, own, to_left, top)
    copies[0].wait_recv()
    use(0, (own, over[0]))
    copies[1].wait_recv()
    go(5, left, to_right, top)
    copies[3].wait_recv()
    go(6, right, to_left, bottom)
    copies[2].wait_recv()
    go(7, left, sibling)
    copies[4].wait_recv()
    go(8, right, sibling)
    use(1, (left, right))
    copies[7].wait_recv()
    use(2, (over[1],))
    copies[5].wait_recv()
    go(9, far, sibling, top)
    copies[6].wait_recv()
    go(10, far, sibling, bottom)
    copies[8].wait_recv()
    use(3, (over[2], far))
    copies[9].wait_recv()
    copies[10].wait_recv()
    use(4, (over[3],))
    for copy in copies.values():
        copy.wait_send()


def attend_block(queries, window, pair_now, place, peak, total, relation):
    scale = math.log2(math.e) / math.sqrt(ATTEND_HEAD_SIZE)
    ones = jnp.ones((ROWS, ATTEND_HEAD_SIZE), bf16)

    def straighten(t, carry):
        rows = pl.ds(pl.multiple_of(t * 128, 128), 128)
        value = window[place, rows]
        pair_now[rows, :ATTEND_HEAD_SIZE] = value[:, 0, :]
        pair_now[rows, ATTEND_HEAD_SIZE:] = value[:, 1, :]
        return carry

    lax.fori_loop(0, ROWS // 128, straighten, 0)

    def tile(t, carry):
        rows = pl.ds(pl.multiple_of(t * TILE, TILE), TILE)
        keys = pair_now[:, :ATTEND_HEAD_SIZE]
        values = jnp.concatenate([pair_now[:, ATTEND_HEAD_SIZE:], ones], axis=1)
        scores = mm_nt(queries[rows, :], keys) * scale
        if relation is not None:
            i, j = grid_of(TILE, ROWS)
            i = i + lax.rem(t, ROWS // TILE) * TILE
            scores = jnp.where(i >= j if relation == "causal" else i < j, scores, -jnp.inf)
        block_peak = jnp.max(scores, axis=-1, keepdims=True)
        if relation == "causal":
            weights = jnp.exp2(scores - block_peak).astype(bf16)
            total[rows, :] = dot(weights, values)
            peak[rows, :] = jnp.broadcast_to(block_peak, (TILE, ATTEND_HEAD_SIZE))
        else:
            before = peak[rows, :1]
            now = jnp.maximum(before, block_peak)
            weights = jnp.exp2(scores - now).astype(bf16)
            total[rows, :] = total[rows, :] * jnp.exp2(before - now) + dot(weights, values)
            peak[rows, :] = jnp.broadcast_to(now, (TILE, ATTEND_HEAD_SIZE))
        return carry

    lax.fori_loop(0, 2 * ROWS // TILE, tile, 0)


FAR_FIRST = (4, 3, 5, 2, 6, 1, 7)


def straight(raw, weight, at, turn):
    width = raw.shape[2]

    def step(t, carry):
        rows = pl.ds(pl.multiple_of(turn * 256 + t * 64, 64), 64)
        value = raw[rows]
        weight[rows, at:at + width] = value[:, 0, :]
        weight[rows, at + width:at + 2 * width] = value[:, 1, :]
        return carry

    lax.fori_loop(0, 4, step, 0)


def layer_kernel(queries_ref, pairs_ref, out_weight_ref, residual_ref, gain_ref, qk_weight_ref,
                 vg_weight_ref, decay_ref, strength_ref, initial_ref, head_gain_ref, delta_weight_ref, out_ref,
                 packed_ref, pair_now, queries, window, peak, total_mix, out_weight, mix, normed, hidden_ref, projected,
                 squares, qk_raw, vg_raw, weight, delta_weight,
                 zero_ref, lead_ref, message_ref, slab_prefix,
                 row, total, column, prefix, first, back, landed,
                 gate, gated, to_sibling, from_sibling, far, relay, waiting, near, arrived,
                 kv_send, kv_recv, ow_send, ow_recv, mix_send, mix_recv, norm_send, norm_recv,
                 local_sem, row_send, row_recv, col_send, col_recv, back_send, back_recv,
                 pair_send, pair_recv, out_send, out_recv):
    s, head = lax.axis_index("seq"), lax.axis_index("head")
    seq_count = Y * Z
    y, z = s // Z, s % Z
    x, c = head // 2, head % 2
    sibling, to_left, to_right = at_head(x, 1 - c), at_head(x + X - 1, c), at_head(x + 1, c)

    def along(d):
        return {"seq": (s + d + seq_count) % seq_count}

    def other(d):
        return {"head": (head + d) % HEADS}

    def in_row(d):
        return {"seq": y * Z + (z + d + Z) % Z}

    def in_column(d):
        return {"seq": ((y + d) % Y) * Z + z}

    own_columns = pl.ds(pl.multiple_of(head * SHARE, SHARE), SHARE)
    locals_ = [
        pltpu.make_async_copy(pairs_ref, window.at[0], local_sem.at[0]),
        pltpu.make_async_copy(qk_weight_ref, qk_raw, local_sem.at[1]),
        pltpu.make_async_copy(vg_weight_ref, vg_raw, local_sem.at[2]),
        pltpu.make_async_copy(out_weight_ref.at[:, own_columns], out_weight.at[head], local_sem.at[3]),
        pltpu.make_async_copy(delta_weight_ref, delta_weight, local_sem.at[4]),
    ]
    locals_[0].start()
    greet([along(1), along(-1)] + [other(d) for d in range(1, HEADS)]
          + [in_row(d) for d in range(1, Z)] + [in_column(d) for d in range(1, Y)])

    half = ROWS // 2
    halves = (slice(0, half), slice(half, ROWS))
    hops = {}

    def describe(d, part, source, device):
        rows, n = halves[part], 2 * d + part
        return pltpu.make_async_remote_copy(
            src_ref=pairs_ref.at[rows] if source == 0 else window.at[source, rows],
            dst_ref=window.at[d, rows], send_sem=kv_send.at[n], recv_sem=kv_recv.at[n],
            device_id=device, device_id_type=MESH)

    def first_hop(d, part, source, device):
        describe(d, part, source, device).start()

    def hop(d, part, by):
        source = 0 if d == Z else d - 1 if by == 1 else d + 1
        hops[2 * d + part] = describe(d, part, source, along(by))
        hops[2 * d + part].start()

    def landed_part(d, part, by):
        hops[2 * d + part].wait_recv()
        if d == Z:
            pl.when(z == Z - 1)(lambda: first_hop(1, part, Z, in_row(1)))
            pl.when(z != 0)(lambda: first_hop(Z - 1, part, Z, along(-1)))
            return
        if by == 1 and (d < 3 or (d == 3 and part == 0)):
            hop(d + 1, part, 1)
        if by == -1 and (d > 5 or (d == 5 and part == 1)):
            hop(d - 1, part, -1)

    hop(Z, 1, Z)
    hop(Z, 0, Z)
    for part in range(2):
        hops[2 + part] = describe(1, part, 0, along(1))
        hops[2 * (Z - 1) + part] = describe(Z - 1, part, 0, along(-1))
    for part in range(2):
        pl.when(z != Z - 1)(lambda: first_hop(1, part, 0, along(1)))
        pl.when(z == 0)(lambda: first_hop(Z - 1, 1 - part, 0, in_row(-1)))
    for copy in locals_[1:]:
        copy.start()
    weights = []
    for d in range(1, HEADS):
        target = (head + d) % HEADS
        weights.append(send(
            out_weight_ref.at[:, pl.ds(pl.multiple_of(target * SHARE, SHARE), SHARE)],
            out_weight.at[head], ow_send.at[d], ow_recv.at[d], other(d)))
    for g in range(2):
        queries[g * ROWS:(g + 1) * ROWS, :] = queries_ref[:, g * ATTEND_HEAD_SIZE:(g + 1) * ATTEND_HEAD_SIZE]
    packed_ref[:VALUE_HEADS, :] = decay_ref[...]
    packed_ref[VALUE_HEADS:, :] = strength_ref[...]
    locals_[0].wait()
    attend_block(queries, window, pair_now, 0, peak, total_mix, "causal")

    def attend_earlier(d):
        @pl.when(s >= d)
        def _():
            attend_block(queries, window, pair_now, d, peak, total_mix, "window" if d == Z else None)

    def prepare(turn):
        straight(qk_raw, weight, 0, turn)
        straight(vg_raw, weight, 2 * KEY_HEADS * DK, turn)

    landed_part(Z, 1, -1)
    landed_part(1, 0, 1)
    landed_part(Z, 0, -1)
    landed_part(1, 1, 1)
    attend_earlier(1)
    landed_part(7, 1, -1)
    locals_[1].wait()
    locals_[2].wait()
    prepare(0)
    landed_part(2, 0, 1)
    attend_earlier(Z)
    landed_part(7, 0, -1)
    attend_earlier(7)
    landed_part(2, 1, 1)
    prepare(1)
    landed_part(6, 1, -1)
    attend_earlier(2)
    landed_part(3, 0, 1)
    prepare(2)
    landed_part(6, 0, -1)
    attend_earlier(6)
    landed_part(3, 1, 1)
    prepare(3)
    prepare(4)
    landed_part(5, 1, -1)
    attend_earlier(3)
    landed_part(4, 0, 1)
    prepare(5)
    prepare(6)
    prepare(7)
    landed_part(5, 0, -1)
    attend_earlier(5)
    landed_part(4, 1, -1)
    attend_earlier(4)
    for g in range(2):
        rows = slice(g * ROWS, (g + 1) * ROWS)
        mix[head, :, g * ATTEND_HEAD_SIZE:(g + 1) * ATTEND_HEAD_SIZE] = (
            total_mix[rows, :ATTEND_HEAD_SIZE] / total_mix[rows, ATTEND_HEAD_SIZE:]).astype(bf16)
    for copy in weights:
        copy.wait()
    locals_[3].wait()
    locals_[4].wait()
    for copy in hops.values():
        copy.wait_send()

    def add_branch(turn, blocks):
        part = sum(dot(mix[b], out_weight[b]) for b in blocks)
        hidden_ref[...] = part if turn == 0 else hidden_ref[...] + part

    gather_heads(mix, mix_send, mix_recv, x, c, add_branch)
    hidden = residual_ref[...].astype(f32) + hidden_ref[...]
    hidden_ref[...] = hidden
    normed[head] = (hidden * gain_ref[:, own_columns]).astype(bf16)

    def add_projected(turn, blocks):
        square = None
        for block in blocks:
            cols = pl.ds(pl.multiple_of(block * SHARE, SHARE), SHARE)
            value = normed[block].astype(f32) * (1.0 / gain_ref[:, cols])
            value = value * value
            value = value[:, :128] + value[:, 128:]
            square = value if square is None else square + value
        squares[...] = square if turn == 0 else squares[...] + square
        for at in range(0, PROJECTED, 256):
            cols = slice(at, at + 256)
            part = sum(
                dot(normed[b], weight[pl.ds(pl.multiple_of(b * SHARE, SHARE), SHARE), cols])
                for b in blocks)
            projected[:, cols] = part if turn == 0 else projected[:, cols] + part

    gather_heads(normed, norm_send, norm_recv, x, c, add_projected)
    inverse = lax.rsqrt(jnp.sum(squares[...], axis=-1, keepdims=True) * (1.0 / MODEL) + epsilon)
    squares[...] = jnp.broadcast_to(inverse, (ROWS, 128))
    local_slab(projected, squares, packed_ref, zero_ref, lead_ref, message_ref, slab_prefix)

    sends = []
    for d in FAR_FIRST:
        copy = pltpu.make_async_remote_copy(
            src_ref=message_ref.at[(z + d) % Z], dst_ref=row.at[z], send_sem=row_send.at[d],
            recv_sem=row_recv.at[d], device_id=in_row(d), device_id_type=MESH)
        copy.start()
        sends.append(copy)
    row[z] = message_ref[z]
    first[...] = initial_ref[z // 2].T
    i, j = grid_of(DK + HALF, DK)
    run = (i == j).astype(f32)
    decay = jnp.ones((1, DK), f32)
    for h in range(VALUE_HEADS):
        cols = slice(h * DV, (h + 1) * DV)
        at = 2 * KEY_HEADS * DK + (VALUE_HEADS + h) * DV
        u = projected[:, at:at + DV] * squares[...]
        gate[:, cols] = head_gain_ref[...] * (u / (1.0 + jnp.exp(-u)))
    for copy in sends:
        copy.wait()
    zero = jnp.zeros((DK, DK), f32)
    for place in range(Z):
        prefix[place] = run
        a = sum_rows(row[place, DK + HALF:])
        offset = jnp.concatenate([zero, row[place, DK:DK + HALF].astype(f32)], axis=0)
        run = a * run + mm2(run, row[place, :DK]) + offset
        decay = decay * a
    total[:DK + HALF] = jnp.where(i == j, run - decay, run).astype(bf16)
    total[DK + HALF:] = three_rows(decay)
    sends = []
    for d in (2, 1, 3):
        copy = pltpu.make_async_remote_copy(
            src_ref=total, dst_ref=column.at[y], send_sem=col_send.at[d], recv_sem=col_recv.at[d],
            device_id=in_column(d), device_id_type=MESH)
        copy.start()
        sends.append(copy)
    column[y] = total[...]
    state = first[pl.ds(pl.multiple_of((z % 2) * HALF, HALF), HALF), :]
    for copy in sends:
        copy.wait()
    for place in range(Y - 1):
        a = sum_rows(column[place, DK + HALF:])
        after = a * state + mm2(state, column[place, :DK]) + column[place, DK:DK + HALF].astype(f32)
        state = jnp.where(place < y, after, state)
    for place in range(Z):
        entering = mm3(state, prefix[place, :DK]) + prefix[place, DK:]
        back[place] = entering.astype(bf16)
    sends = []
    for d in FAR_FIRST:
        copy = pltpu.make_async_remote_copy(
            src_ref=back.at[(z + d) % Z], dst_ref=landed.at[z], send_sem=back_send.at[d],
            recv_sem=back_recv.at[d], device_id=in_row(d), device_id_type=MESH)
        copy.start()
        sends.append(copy)
    landed[z] = back[z]
    for copy in sends:
        copy.wait()
    for h in range(VALUE_HEADS):
        cols = slice(h * DV, (h + 1) * DV)
        state = jnp.concatenate([landed[2 * h], landed[2 * h + 1]], axis=0)
        delta = zero_ref[:, cols] + mm_nt(lead_ref[:, cols], state)
        gated[:, cols] = (delta * inverse_rms(delta) * gate[:, cols]).astype(bf16)

    def partial(d, core):
        at = ((x + d) % X * 2 + core) * SHARE
        return dot(gated[...], delta_weight[:, pl.ds(pl.multiple_of(at, SHARE), SHARE)])

    order, half = (2, 1, X - 1, 0), ROWS // 2
    top, bottom = slice(0, half), slice(half, ROWS)
    pairs, sends = {}, {}

    def over_pair(n):
        to_sibling[n] = partial(order[n], 1 - c).astype(bf16)
        pairs[n] = send(to_sibling.at[n], from_sibling.at[n], pair_send.at[n], pair_recv.at[n], sibling)

    def out_send_rows(n, source, target, device):
        sends[n] = send(source, target, out_send.at[n], out_recv.at[n], device)

    over_pair(0)
    over_pair(1)
    value = partial(2, c)
    pairs[0].wait_recv()
    far[...] = (value + from_sibling[0].astype(f32)).astype(bf16)
    out_send_rows(0, far.at[top], relay.at[0], to_right)
    out_send_rows(1, far.at[bottom], relay.at[1], to_left)
    over_pair(2)
    value = partial(order[1], c)
    pairs[1].wait_recv()
    value = value + from_sibling[1].astype(f32)
    near[0, bottom] = value[bottom].astype(bf16)
    out_send_rows(2, near.at[0, bottom], arrived.at[0, bottom], to_right)
    waiting[0] = value[top]
    value = partial(order[2], c)
    pairs[2].wait_recv()
    value = value + from_sibling[2].astype(f32)
    near[1, top] = value[top].astype(bf16)
    out_send_rows(3, near.at[1, top], arrived.at[1, top], to_left)
    waiting[1] = value[bottom]
    over_pair(3)
    sends[0].wait_recv()
    near[0, top] = (waiting[0] + relay[0].astype(f32)).astype(bf16)
    out_send_rows(4, near.at[0, top], arrived.at[0, top], to_right)
    sends[1].wait_recv()
    near[1, bottom] = (waiting[1] + relay[1].astype(f32)).astype(bf16)
    out_send_rows(5, near.at[1, bottom], arrived.at[1, bottom], to_left)
    value = hidden_ref[...] + partial(0, c)
    pairs[3].wait_recv()
    value = value + from_sibling[3].astype(f32)
    for n in range(2, 6):
        sends[n].wait_recv()
    out_ref[...] = (value + arrived[0].astype(f32) + arrived[1].astype(f32)).astype(bf16)
    for copy in list(pairs.values()) + list(sends.values()):
        copy.wait_send()


def inverse_rms(values):
    return lax.rsqrt(jnp.mean(values * values, axis=-1, keepdims=True) + epsilon)


def body(residual, queries, key_value_pairs, attention_out, norm_gain, query_key_weight,
         value_gate_weight, write_strength, log_decay, initial_state, head_gain, delta_output):
    vmem, hbm = pl.BlockSpec(memory_space=pltpu.VMEM), pl.BlockSpec(memory_space=pl.ANY)
    dma = pltpu.SemaphoreType.DMA
    return pl.pallas_call(
        layer_kernel,
        out_shape=jax.ShapeDtypeStruct((ROWS, SHARE), bf16),
        in_specs=[vmem, hbm, hbm, vmem, vmem, hbm, hbm, vmem, vmem, vmem, vmem, hbm],
        out_specs=vmem,
        scratch_shapes=[
            pltpu.VMEM((2 * VALUE_HEADS, ROWS), f32),
            pltpu.VMEM((ROWS, 2 * ATTEND_HEAD_SIZE), bf16),
            pltpu.VMEM((2 * ROWS, ATTEND_HEAD_SIZE), bf16),
            pltpu.VMEM((Z + 1, ROWS, 2, ATTEND_HEAD_SIZE), bf16),
            pltpu.VMEM((2 * ROWS, ATTEND_HEAD_SIZE), f32),
            pltpu.VMEM((2 * ROWS, 2 * ATTEND_HEAD_SIZE), f32),
            pltpu.VMEM((HEADS, SHARE, SHARE), bf16),
            pltpu.VMEM((HEADS, ROWS, SHARE), bf16),
            pltpu.VMEM((HEADS, ROWS, SHARE), bf16),
            pltpu.VMEM((ROWS, SHARE), f32),
            pltpu.VMEM((ROWS, PROJECTED), f32),
            pltpu.VMEM((ROWS, 128), f32),
            pltpu.VMEM((MODEL, 2, KEY_HEADS * DK), bf16),
            pltpu.VMEM((MODEL, 2, VALUE_HEADS * DV), bf16),
            pltpu.VMEM((MODEL, PROJECTED), bf16),
            pltpu.VMEM((VALUE_HEADS * DV, MODEL), bf16),
            pltpu.VMEM((ROWS, VALUE_HEADS * DV), f32),
            pltpu.VMEM((ROWS, VALUE_HEADS * DK), bf16),
            pltpu.VMEM((Z, MESSAGE, DK), bf16),
            pltpu.VMEM((VALUE_HEADS, DK, DK + DV), f32),
            pltpu.VMEM((Z, MESSAGE, DK), bf16),
            pltpu.VMEM((MESSAGE, DK), bf16),
            pltpu.VMEM((Y, MESSAGE, DK), bf16),
            pltpu.VMEM((Z, DK + HALF, DK), f32),
            pltpu.VMEM((DV, DK), f32),
            pltpu.VMEM((Z, HALF, DK), bf16),
            pltpu.VMEM((Z, HALF, DK), bf16),
            pltpu.VMEM((ROWS, VALUE_HEADS * DV), f32),
            pltpu.VMEM((ROWS, VALUE_HEADS * DV), bf16),
            pltpu.VMEM((X, ROWS, SHARE), bf16),
            pltpu.VMEM((X, ROWS, SHARE), bf16),
            pltpu.VMEM((ROWS, SHARE), bf16),
            pltpu.VMEM((2, ROWS // 2, SHARE), bf16),
            pltpu.VMEM((2, ROWS // 2, SHARE), f32),
            pltpu.VMEM((2, ROWS, SHARE), bf16),
            pltpu.VMEM((2, ROWS, SHARE), bf16),
            dma((2 * Z + 2,)), dma((2 * Z + 2,)), dma((HEADS,)), dma((HEADS,)),
            dma((11,)), dma((11,)), dma((11,)), dma((11,)), dma((5,)),
            dma((Z,)), dma((Z,)), dma((Y,)), dma((Y,)), dma((Z,)), dma((Z,)),
            dma((X,)), dma((X,)), dma((6,)), dma((6,)),
        ],
        compiler_params=pltpu.CompilerParams(
            collective_id=0, has_side_effects=True, vmem_limit_bytes=60 * 2**20),
        name="layer",
    )(queries, key_value_pairs, attention_out, residual,
      norm_gain.reshape(1, MODEL), query_key_weight, value_gate_weight, log_decay, write_strength,
      initial_state,
      head_gain.reshape(1, DV), delta_output)


def solution(mesh):
    return jax.shard_map(
        body,
        mesh=mesh,
        in_specs=(
            P("seq", "head"),
            P("seq", "head"),
            P("seq", None, "head"),
            P("head", None),
            P(),
            P(None, None, "head"),
            P(None, None, "head"),
            P("head", "seq"),
            P("head", "seq"),
            P("head", None, None),
            P(),
            P("head", None),
        ),
        out_specs=P("seq", "head"),
        check_vma=False,
    )
```

```python
import math

import jax
import jax.numpy as jnp
from jax import lax
from jax.experimental import pallas as pl
from jax.experimental.pallas import tpu as pltpu
from jax.sharding import PartitionSpec as P

DK = 128
DV = 128
ATTEND_HEAD_SIZE = 128
WINDOW_KEYS = 4096
X = 4
HEADS = 8
MODEL = 2048
SHARE = 256
PROJECTED = 1536
TILE = 128
TOGETHER = 4
CHUNK = 128
ROWS = 512
KEY_HEADS = 2
VALUE_HEADS = 4
Z = 8
Y = 4
HALF = DV // 2
MESSAGE = DK + HALF + 16
MESH = pl.DeviceIdType.MESH
f32 = jnp.float32
bf16 = jnp.bfloat16


epsilon = 1e-06


def dot(a, b, contract=((1,), (0,))):
    return lax.dot_general(a, b, (contract, ((), ())), preferred_element_type=f32)


def mm(a, b):
    return dot(a.astype(bf16), b.astype(bf16))


def mm_nt(a, b):
    return dot(a.astype(bf16), b.astype(bf16), ((1,), (1,)))


def split(a):
    high = a.astype(bf16)
    return high, (a - high.astype(f32)).astype(bf16)


def mm2(a, b):
    high, low = split(a)
    return dot(high, b) + dot(low, b)


def mm3(a, b):
    high, low = split(a)
    b_high, b_low = split(b)
    return dot(high, b_high) + dot(low, b_high) + dot(high, b_low)


def grid_of(rows, columns):
    shape = (rows, columns)
    return lax.broadcasted_iota(jnp.int32, shape, 0), lax.broadcasted_iota(jnp.int32, shape, 1)


def three_rows(a):
    high = a.astype(bf16).astype(f32)
    mid = (a - high).astype(bf16).astype(f32)
    low = a - high - mid
    row = lax.broadcasted_iota(jnp.int32, (16, a.shape[1]), 0)
    return jnp.where(row == 0, high, jnp.where(row == 1, mid, jnp.where(row == 2, low, 0.0))).astype(bf16)


def sum_rows(block):
    return jnp.sum(block.astype(f32), axis=0, keepdims=True)


def local_slab(projected, inverse_ref, packed_ref, zero_ref, lead_ref, message_ref, prefix):
    i, j = grid_of(CHUNK, CHUNK)
    inclusive, strict = i >= j, i > j
    eye = (i == j).astype(f32)
    lower = inclusive.astype(f32)
    for h in range(VALUE_HEADS):
        prefix[h] = jnp.concatenate([eye, jnp.zeros_like(eye)], axis=1)
    per_turn = 2

    def turn(t, carry):
        items = []
        for u in range(per_turn):
            rows = pl.ds(pl.multiple_of((t * per_turn + u) * CHUNK, CHUNK), CHUNK)
            packed = packed_ref[:, rows]
            columns = packed.T
            total_row = lax.dot_general(
                packed, lower, (((1,), (1,)), ((), ())),
                precision=lax.Precision.HIGHEST, preferred_element_type=f32)
            total_col = lax.dot_general(
                lower, columns, (((1,), (0,)), ((), ())),
                precision=lax.Precision.HIGHEST, preferred_element_type=f32)
            keys = []
            for kh in range(KEY_HEADS):
                q = projected[rows, kh * DK:(kh + 1) * DK] * inverse_ref[rows, :]
                q = q * lax.rsqrt(jnp.sum(q * q, axis=-1, keepdims=True) + epsilon) * DK ** (-0.5)
                at = KEY_HEADS * DK + kh * DK
                k = projected[rows, at:at + DK] * inverse_ref[rows, :]
                k = k * lax.rsqrt(jnp.sum(k * k, axis=-1, keepdims=True) + epsilon)
                kb = k.astype(bf16)
                keys.append((q, kb, k.T, mm_nt(kb, kb), mm_nt(q, kb)))
            for h in range(VALUE_HEADS):
                q, k, k_t, key_key, query_key = keys[h // 2]
                cum_col, cum_row = total_col[:, h:h + 1], total_row[h:h + 1, :]
                strength_col = columns[:, VALUE_HEADS + h:VALUE_HEADS + h + 1]
                strength_row = packed[VALUE_HEADS + h:VALUE_HEADS + h + 1, :]
                ratio = jnp.where(inclusive, jnp.exp(jnp.minimum(cum_col - cum_row, 0.0)), 0.0)
                coupling = jnp.where(strict, strength_col * ratio * key_key, 0.0)
                items.append(dict(
                    h=h, rows=rows, q=q, k=k, k_t=k_t, coupling=coupling, mixing=ratio * query_key,
                    cum_col=cum_col, cum_row=cum_row, strength_row=strength_row,
                    inverse=eye - jnp.where((i // 2) == (j // 2), coupling, 0.0)))
        size = 2
        while size < CHUNK:
            level = ((i // (2 * size)) == (j // (2 * size))) & ((i // size) != (j // size))
            for it in items:
                it["half"] = mm(jnp.where(level, it["coupling"], 0.0), it["inverse"])
            for it in items:
                it["inverse"] = it["inverse"] - mm(it["inverse"], it["half"])
            size *= 2
        for it in items:
            scaled = it["inverse"] * it["strength_row"]
            at = 2 * KEY_HEADS * DK + it["h"] * DV
            v = projected[it["rows"], at:at + DV] * inverse_ref[it["rows"], :]
            w = mm(scaled * jnp.exp(it["cum_row"]), it["k"])
            u = mm(scaled, v)
            it["wu"] = jnp.concatenate([w, u], axis=1).astype(bf16)
        for it in items:
            mixed = mm(it["mixing"], it["wu"])
            it["lead"] = jnp.exp(it["cum_col"]) * it["q"] - mixed[:, :DK]
            it["own"] = mixed[:, DK:]
            end = it["cum_row"][:, CHUNK - 1:]
            it["end"] = jnp.exp(end)
            it["step"] = mm(it["k_t"] * jnp.exp(end - it["cum_row"]), it["wu"])
        for it in items:
            h = it["h"]
            before = prefix[h]
            out = mm(it["lead"], before)
            lead_ref[it["rows"], h * DK:(h + 1) * DK] = out[:, :DK].astype(bf16)
            zero_ref[it["rows"], h * DV:(h + 1) * DV] = out[:, DK:] + it["own"]
            offset = jnp.concatenate([jnp.zeros((DK, DK), f32), it["step"][:, DK:]], axis=1)
            prefix[h] = it["end"] * before - mm(it["step"][:, :DK], before) + offset
        return carry

    lax.fori_loop(0, ROWS // CHUNK // per_turn, turn, 0)
    slab_decay = jnp.exp(jnp.sum(packed_ref[...], axis=1, keepdims=True))
    for h in range(VALUE_HEADS):
        decay = slab_decay[h:h + 1, :]
        change = (prefix[h, :, :DK] - decay * eye).T.astype(bf16)
        offset = prefix[h, :, DK:].T.astype(bf16)
        tail = three_rows(jnp.broadcast_to(decay, (1, DK)))
        for c in range(2):
            message_ref[2 * h + c, :DK] = change
            message_ref[2 * h + c, DK:DK + HALF] = offset[c * HALF:(c + 1) * HALF]
            message_ref[2 * h + c, DK + HALF:] = tail


def at_head(x, c):
    return {"head": (x % X) * 2 + c}


def send(source, target, send_sem, recv_sem, device):
    copy = pltpu.make_async_remote_copy(
        src_ref=source, dst_ref=target, send_sem=send_sem, recv_sem=recv_sem,
        device_id=device, device_id_type=MESH)
    copy.start()
    return copy


def greet(devices):
    barrier = pltpu.get_barrier_semaphore()
    for device in devices:
        pl.semaphore_signal(barrier, inc=1, device_id=device, device_id_type=MESH)
    pl.semaphore_wait(barrier, len(devices))


def gather_heads(blocks, send_sem, recv_sem, x, c, use):
    mid = ROWS // 2
    every, top, bottom = slice(0, ROWS), slice(0, mid), slice(mid, ROWS)
    left, right, far = (x + X - 1) % X, (x + 1) % X, (x + 2) % X
    sibling, to_left, to_right = at_head(x, 1 - c), at_head(x + X - 1, c), at_head(x + 1, c)
    mine = pl.ds(pl.multiple_of(c * SHARE, SHARE), SHARE)
    copies = {}

    def go(n, chip, device, rows):
        ref = blocks.at[chip, rows, mine]
        copies[n] = send(ref, ref, send_sem.at[n], recv_sem.at[n], device)

    go(1, x, to_right, top)
    go(3, x, to_left, bottom)
    go(0, x, sibling, every)
    go(2, x, to_right, bottom)
    go(4, x, to_left, top)
    copies[0].wait_recv()
    use(0, x)
    copies[1].wait_recv()
    go(5, left, to_right, top)
    copies[3].wait_recv()
    go(6, right, to_left, bottom)
    copies[2].wait_recv()
    go(7, left, sibling, every)
    copies[4].wait_recv()
    go(8, right, sibling, every)
    copies[7].wait_recv()
    use(1, left)
    copies[5].wait_recv()
    go(9, far, sibling, top)
    copies[6].wait_recv()
    go(10, far, sibling, bottom)
    copies[8].wait_recv()
    use(2, right)
    copies[9].wait_recv()
    copies[10].wait_recv()
    use(3, far)
    for copy in copies.values():
        copy.wait_send()


def attend_block(queries, window, pair_now, place, peak, total, relation):
    scale = math.log2(math.e) / math.sqrt(ATTEND_HEAD_SIZE)
    ones = jnp.ones((ROWS, ATTEND_HEAD_SIZE), bf16)

    def straighten(t, carry):
        rows = pl.ds(pl.multiple_of(t * 128, 128), 128)
        value = window[place, rows]
        pair_now[rows, :ATTEND_HEAD_SIZE] = value[:, 0, :]
        pair_now[rows, ATTEND_HEAD_SIZE:] = value[:, 1, :]
        return carry

    lax.fori_loop(0, ROWS // 128, straighten, 0)

    keys = pair_now[:, :ATTEND_HEAD_SIZE]
    values = jnp.concatenate([pair_now[:, ATTEND_HEAD_SIZE:], ones], axis=1)
    tiles = 2 * ROWS // TILE
    for start in range(0, tiles, TOGETHER):
        group = [slice(t * TILE, (t + 1) * TILE) for t in range(start, start + TOGETHER)]
        all_scores = [mm_nt(queries[rows, :], keys) * scale for rows in group]
        for rows, scores in zip(group, all_scores):
            if relation is not None:
                i, j = grid_of(TILE, ROWS)
                i = i + rows.start % ROWS
                scores = jnp.where(i >= j if relation == "causal" else i < j, scores, -jnp.inf)
            block_peak = jnp.max(scores, axis=-1, keepdims=True)
            if relation == "causal":
                weights = jnp.exp2(scores - block_peak).astype(bf16)
                total[rows, :] = dot(weights, values)
                peak[rows, :] = jnp.broadcast_to(block_peak, (TILE, ATTEND_HEAD_SIZE))
            else:
                before = peak[rows, :1]
                now = jnp.maximum(before, block_peak)
                weights = jnp.exp2(scores - now).astype(bf16)
                total[rows, :] = total[rows, :] * jnp.exp2(before - now) + dot(weights, values)
                peak[rows, :] = jnp.broadcast_to(now, (TILE, ATTEND_HEAD_SIZE))


FAR_FIRST = (4, 3, 5, 2, 6, 1, 7)


def straight(raw, weight, at, turn):
    width = raw.shape[2]

    def step(t, carry):
        rows = pl.ds(pl.multiple_of(turn * 256 + t * 64, 64), 64)
        value = raw[rows]
        weight[rows, at:at + width] = value[:, 0, :]
        weight[rows, at + width:at + 2 * width] = value[:, 1, :]
        return carry

    lax.fori_loop(0, 4, step, 0)


def layer_kernel(queries_ref, pairs_ref, out_weight_ref, residual_ref, gain_ref, qk_weight_ref,
                 vg_weight_ref, decay_ref, strength_ref, initial_ref, head_gain_ref, delta_weight_ref, out_ref,
                 packed_ref, pair_now, queries, window, peak, total_mix, out_weight, mix, normed, hidden_ref, projected,
                 squares, qk_raw, vg_raw, weight, delta_weight,
                 zero_ref, lead_ref, message_ref, slab_prefix,
                 row, total, column, prefix, first, back, landed,
                 gate, gated, to_sibling, from_sibling, far, relay, waiting, near, arrived,
                 kv_send, kv_recv, ow_send, ow_recv, mix_send, mix_recv, norm_send, norm_recv,
                 local_sem, row_send, row_recv, col_send, col_recv, back_send, back_recv,
                 pair_send, pair_recv, out_send, out_recv):
    s, head = lax.axis_index("seq"), lax.axis_index("head")
    seq_count = Y * Z
    y, z = s // Z, s % Z
    x, c = head // 2, head % 2
    sibling, to_left, to_right = at_head(x, 1 - c), at_head(x + X - 1, c), at_head(x + 1, c)

    def along(d):
        return {"seq": (s + d + seq_count) % seq_count}

    def other(d):
        return {"head": (head + d) % HEADS}

    def in_row(d):
        return {"seq": y * Z + (z + d + Z) % Z}

    def in_column(d):
        return {"seq": ((y + d) % Y) * Z + z}

    own_columns = pl.ds(pl.multiple_of(head * SHARE, SHARE), SHARE)
    locals_ = [
        pltpu.make_async_copy(pairs_ref, window.at[0], local_sem.at[0]),
        pltpu.make_async_copy(qk_weight_ref, qk_raw, local_sem.at[1]),
        pltpu.make_async_copy(vg_weight_ref, vg_raw, local_sem.at[2]),
        pltpu.make_async_copy(out_weight_ref.at[:, own_columns], out_weight.at[own_columns], local_sem.at[3]),
        pltpu.make_async_copy(delta_weight_ref, delta_weight, local_sem.at[4]),
    ]
    locals_[0].start()
    greet([along(1), along(-1)] + [other(d) for d in range(1, HEADS)]
          + [in_row(d) for d in range(1, Z)] + [in_column(d) for d in range(1, Y)])

    half = ROWS // 2
    halves = (slice(0, half), slice(half, ROWS))
    hops = {}

    def describe(d, part, source, device):
        rows, n = halves[part], 2 * d + part
        return pltpu.make_async_remote_copy(
            src_ref=pairs_ref.at[rows] if source == 0 else window.at[source, rows],
            dst_ref=window.at[d, rows], send_sem=kv_send.at[n], recv_sem=kv_recv.at[n],
            device_id=device, device_id_type=MESH)

    def first_hop(d, part, source, device):
        describe(d, part, source, device).start()

    def hop(d, part, by):
        source = 0 if d == Z else d - 1 if by == 1 else d + 1
        hops[2 * d + part] = describe(d, part, source, along(by))
        hops[2 * d + part].start()

    def landed_part(d, part, by):
        hops[2 * d + part].wait_recv()
        if d == Z:
            pl.when(z == Z - 1)(lambda: first_hop(1, part, Z, in_row(1)))
            pl.when(z != 0)(lambda: first_hop(Z - 1, part, Z, along(-1)))
            return
        if by == 1 and (d < 3 or (d == 3 and part == 0)):
            hop(d + 1, part, 1)
        if by == -1 and (d > 5 or (d == 5 and part == 1)):
            hop(d - 1, part, -1)

    hop(Z, 1, Z)
    hop(Z, 0, Z)
    for part in range(2):
        hops[2 + part] = describe(1, part, 0, along(1))
        hops[2 * (Z - 1) + part] = describe(Z - 1, part, 0, along(-1))
    for part in range(2):
        pl.when(z != Z - 1)(lambda: first_hop(1, part, 0, along(1)))
        pl.when(z == 0)(lambda: first_hop(Z - 1, 1 - part, 0, in_row(-1)))
    for copy in locals_[1:]:
        copy.start()
    weights = []
    for d in range(1, HEADS):
        target = (head + d) % HEADS
        weights.append(send(
            out_weight_ref.at[:, pl.ds(pl.multiple_of(target * SHARE, SHARE), SHARE)],
            out_weight.at[own_columns], ow_send.at[d], ow_recv.at[d], other(d)))
    for g in range(2):
        queries[g * ROWS:(g + 1) * ROWS, :] = queries_ref[:, g * ATTEND_HEAD_SIZE:(g + 1) * ATTEND_HEAD_SIZE]
    packed_ref[:VALUE_HEADS, :] = decay_ref[...]
    packed_ref[VALUE_HEADS:, :] = strength_ref[...]
    locals_[0].wait()
    attend_block(queries, window, pair_now, 0, peak, total_mix, "causal")

    def attend_earlier(d):
        @pl.when(s >= d)
        def _():
            attend_block(queries, window, pair_now, d, peak, total_mix, "window" if d == Z else None)

    def prepare(turn):
        straight(qk_raw, weight, 0, turn)
        straight(vg_raw, weight, 2 * KEY_HEADS * DK, turn)

    landed_part(Z, 1, -1)
    landed_part(1, 0, 1)
    landed_part(Z, 0, -1)
    landed_part(1, 1, 1)
    attend_earlier(1)
    landed_part(7, 1, -1)
    locals_[1].wait()
    locals_[2].wait()
    prepare(0)
    landed_part(2, 0, 1)
    attend_earlier(Z)
    landed_part(7, 0, -1)
    attend_earlier(7)
    landed_part(2, 1, 1)
    prepare(1)
    landed_part(6, 1, -1)
    attend_earlier(2)
    landed_part(3, 0, 1)
    prepare(2)
    landed_part(6, 0, -1)
    attend_earlier(6)
    landed_part(3, 1, 1)
    prepare(3)
    prepare(4)
    landed_part(5, 1, -1)
    attend_earlier(3)
    landed_part(4, 0, 1)
    prepare(5)
    prepare(6)
    prepare(7)
    landed_part(5, 0, -1)
    attend_earlier(5)
    landed_part(4, 1, -1)
    attend_earlier(4)
    for g in range(2):
        rows = slice(g * ROWS, (g + 1) * ROWS)
        at = pl.ds(pl.multiple_of(c * SHARE + g * ATTEND_HEAD_SIZE, ATTEND_HEAD_SIZE), ATTEND_HEAD_SIZE)
        mix[x, :, at] = (
            total_mix[rows, :ATTEND_HEAD_SIZE] / total_mix[rows, ATTEND_HEAD_SIZE:]).astype(bf16)
    for copy in weights:
        copy.wait()
    locals_[3].wait()
    locals_[4].wait()
    for copy in hops.values():
        copy.wait_send()

    def of_chip(chip):
        return pl.ds(pl.multiple_of(chip * 2 * SHARE, 2 * SHARE), 2 * SHARE)

    def add_branch(turn, chip):
        part = dot(mix[chip], out_weight[of_chip(chip), :])
        hidden_ref[...] = part if turn == 0 else hidden_ref[...] + part

    gather_heads(mix, mix_send, mix_recv, x, c, add_branch)
    hidden = residual_ref[...].astype(f32) + hidden_ref[...]
    hidden_ref[...] = hidden
    normed[x, :, pl.ds(pl.multiple_of(c * SHARE, SHARE), SHARE)] = (hidden * gain_ref[:, own_columns]).astype(bf16)

    def add_projected(turn, chip):
        for at in range(0, PROJECTED, 256):
            cols = slice(at, at + 256)
            part = dot(normed[chip], weight[of_chip(chip), cols])
            projected[:, cols] = part if turn == 0 else projected[:, cols] + part
        value = normed[chip].astype(f32) * (1.0 / gain_ref[:, of_chip(chip)])
        value = value * value
        value = value[:, :256] + value[:, 256:]
        square = value[:, :128] + value[:, 128:]
        squares[...] = square if turn == 0 else squares[...] + square

    gather_heads(normed, norm_send, norm_recv, x, c, add_projected)
    inverse = lax.rsqrt(jnp.sum(squares[...], axis=-1, keepdims=True) * (1.0 / MODEL) + epsilon)
    squares[...] = jnp.broadcast_to(inverse, (ROWS, 128))
    local_slab(projected, squares, packed_ref, zero_ref, lead_ref, message_ref, slab_prefix)

    sends = []
    for d in FAR_FIRST:
        copy = pltpu.make_async_remote_copy(
            src_ref=message_ref.at[(z + d) % Z], dst_ref=row.at[z], send_sem=row_send.at[d],
            recv_sem=row_recv.at[d], device_id=in_row(d), device_id_type=MESH)
        copy.start()
        sends.append(copy)
    row[z] = message_ref[z]
    first[...] = initial_ref[z // 2].T
    i, j = grid_of(DK + HALF, DK)
    run = (i == j).astype(f32)
    decay = jnp.ones((1, DK), f32)
    for h in range(VALUE_HEADS):
        cols = slice(h * DV, (h + 1) * DV)
        at = 2 * KEY_HEADS * DK + (VALUE_HEADS + h) * DV
        u = projected[:, at:at + DV] * squares[...]
        gate[:, cols] = head_gain_ref[...] * (u / (1.0 + jnp.exp(-u)))
    for copy in sends:
        copy.wait()
    zero = jnp.zeros((DK, DK), f32)
    for place in range(Z):
        prefix[place] = run
        a = sum_rows(row[place, DK + HALF:])
        offset = jnp.concatenate([zero, row[place, DK:DK + HALF].astype(f32)], axis=0)
        run = a * run + mm2(run, row[place, :DK]) + offset
        decay = decay * a
    total[:DK + HALF] = jnp.where(i == j, run - decay, run).astype(bf16)
    total[DK + HALF:] = three_rows(decay)
    sends = []
    for d in (2, 1, 3):
        copy = pltpu.make_async_remote_copy(
            src_ref=total, dst_ref=column.at[y], send_sem=col_send.at[d], recv_sem=col_recv.at[d],
            device_id=in_column(d), device_id_type=MESH)
        copy.start()
        sends.append(copy)
    column[y] = total[...]
    state = first[pl.ds(pl.multiple_of((z % 2) * HALF, HALF), HALF), :]
    for copy in sends:
        copy.wait()
    for place in range(Y - 1):
        a = sum_rows(column[place, DK + HALF:])
        after = a * state + mm2(state, column[place, :DK]) + column[place, DK:DK + HALF].astype(f32)
        state = jnp.where(place < y, after, state)
    for place in range(Z):
        entering = mm3(state, prefix[place, :DK]) + prefix[place, DK:]
        back[place] = entering.astype(bf16)
    sends = []
    for d in FAR_FIRST:
        copy = pltpu.make_async_remote_copy(
            src_ref=back.at[(z + d) % Z], dst_ref=landed.at[z], send_sem=back_send.at[d],
            recv_sem=back_recv.at[d], device_id=in_row(d), device_id_type=MESH)
        copy.start()
        sends.append(copy)
    landed[z] = back[z]
    for copy in sends:
        copy.wait()
    for h in range(VALUE_HEADS):
        cols = slice(h * DV, (h + 1) * DV)
        state = jnp.concatenate([landed[2 * h], landed[2 * h + 1]], axis=0)
        delta = zero_ref[:, cols] + mm_nt(lead_ref[:, cols], state)
        gated[:, cols] = (delta * inverse_rms(delta) * gate[:, cols]).astype(bf16)

    def partial(d, core):
        at = ((x + d) % X * 2 + core) * SHARE
        return dot(gated[...], delta_weight[:, pl.ds(pl.multiple_of(at, SHARE), SHARE)])

    order, half = (2, 1, X - 1, 0), ROWS // 2
    top, bottom = slice(0, half), slice(half, ROWS)
    pairs, sends = {}, {}

    def over_pair(n):
        to_sibling[n] = partial(order[n], 1 - c).astype(bf16)
        pairs[n] = send(to_sibling.at[n], from_sibling.at[n], pair_send.at[n], pair_recv.at[n], sibling)

    def out_send_rows(n, source, target, device):
        sends[n] = send(source, target, out_send.at[n], out_recv.at[n], device)

    over_pair(0)
    over_pair(1)
    value = partial(2, c)
    pairs[0].wait_recv()
    far[...] = (value + from_sibling[0].astype(f32)).astype(bf16)
    out_send_rows(0, far.at[top], relay.at[0], to_right)
    out_send_rows(1, far.at[bottom], relay.at[1], to_left)
    over_pair(2)
    value = partial(order[1], c)
    pairs[1].wait_recv()
    value = value + from_sibling[1].astype(f32)
    near[0, bottom] = value[bottom].astype(bf16)
    out_send_rows(2, near.at[0, bottom], arrived.at[0, bottom], to_right)
    waiting[0] = value[top]
    value = partial(order[2], c)
    pairs[2].wait_recv()
    value = value + from_sibling[2].astype(f32)
    near[1, top] = value[top].astype(bf16)
    out_send_rows(3, near.at[1, top], arrived.at[1, top], to_left)
    waiting[1] = value[bottom]
    over_pair(3)
    sends[0].wait_recv()
    near[0, top] = (waiting[0] + relay[0].astype(f32)).astype(bf16)
    out_send_rows(4, near.at[0, top], arrived.at[0, top], to_right)
    sends[1].wait_recv()
    near[1, bottom] = (waiting[1] + relay[1].astype(f32)).astype(bf16)
    out_send_rows(5, near.at[1, bottom], arrived.at[1, bottom], to_left)
    value = hidden_ref[...] + partial(0, c)
    pairs[3].wait_recv()
    value = value + from_sibling[3].astype(f32)
    for n in range(2, 6):
        sends[n].wait_recv()
    out_ref[...] = (value + arrived[0].astype(f32) + arrived[1].astype(f32)).astype(bf16)
    for copy in list(pairs.values()) + list(sends.values()):
        copy.wait_send()


def inverse_rms(values):
    return lax.rsqrt(jnp.mean(values * values, axis=-1, keepdims=True) + epsilon)


def body(residual, queries, key_value_pairs, attention_out, norm_gain, query_key_weight,
         value_gate_weight, write_strength, log_decay, initial_state, head_gain, delta_output):
    vmem, hbm = pl.BlockSpec(memory_space=pltpu.VMEM), pl.BlockSpec(memory_space=pl.ANY)
    dma = pltpu.SemaphoreType.DMA
    return pl.pallas_call(
        layer_kernel,
        out_shape=jax.ShapeDtypeStruct((ROWS, SHARE), bf16),
        in_specs=[vmem, hbm, hbm, vmem, vmem, hbm, hbm, vmem, vmem, vmem, vmem, hbm],
        out_specs=vmem,
        scratch_shapes=[
            pltpu.VMEM((2 * VALUE_HEADS, ROWS), f32),
            pltpu.VMEM((ROWS, 2 * ATTEND_HEAD_SIZE), bf16),
            pltpu.VMEM((2 * ROWS, ATTEND_HEAD_SIZE), bf16),
            pltpu.VMEM((Z + 1, ROWS, 2, ATTEND_HEAD_SIZE), bf16),
            pltpu.VMEM((2 * ROWS, ATTEND_HEAD_SIZE), f32),
            pltpu.VMEM((2 * ROWS, 2 * ATTEND_HEAD_SIZE), f32),
            pltpu.VMEM((MODEL, SHARE), bf16),
            pltpu.VMEM((X, ROWS, 2 * SHARE), bf16),
            pltpu.VMEM((X, ROWS, 2 * SHARE), bf16),
            pltpu.VMEM((ROWS, SHARE), f32),
            pltpu.VMEM((ROWS, PROJECTED), f32),
            pltpu.VMEM((ROWS, 128), f32),
            pltpu.VMEM((MODEL, 2, KEY_HEADS * DK), bf16),
            pltpu.VMEM((MODEL, 2, VALUE_HEADS * DV), bf16),
            pltpu.VMEM((MODEL, PROJECTED), bf16),
            pltpu.VMEM((VALUE_HEADS * DV, MODEL), bf16),
            pltpu.VMEM((ROWS, VALUE_HEADS * DV), f32),
            pltpu.VMEM((ROWS, VALUE_HEADS * DK), bf16),
            pltpu.VMEM((Z, MESSAGE, DK), bf16),
            pltpu.VMEM((VALUE_HEADS, DK, DK + DV), f32),
            pltpu.VMEM((Z, MESSAGE, DK), bf16),
            pltpu.VMEM((MESSAGE, DK), bf16),
            pltpu.VMEM((Y, MESSAGE, DK), bf16),
            pltpu.VMEM((Z, DK + HALF, DK), f32),
            pltpu.VMEM((DV, DK), f32),
            pltpu.VMEM((Z, HALF, DK), bf16),
            pltpu.VMEM((Z, HALF, DK), bf16),
            pltpu.VMEM((ROWS, VALUE_HEADS * DV), f32),
            pltpu.VMEM((ROWS, VALUE_HEADS * DV), bf16),
            pltpu.VMEM((X, ROWS, SHARE), bf16),
            pltpu.VMEM((X, ROWS, SHARE), bf16),
            pltpu.VMEM((ROWS, SHARE), bf16),
            pltpu.VMEM((2, ROWS // 2, SHARE), bf16),
            pltpu.VMEM((2, ROWS // 2, SHARE), f32),
            pltpu.VMEM((2, ROWS, SHARE), bf16),
            pltpu.VMEM((2, ROWS, SHARE), bf16),
            dma((2 * Z + 2,)), dma((2 * Z + 2,)), dma((HEADS,)), dma((HEADS,)),
            dma((11,)), dma((11,)), dma((11,)), dma((11,)), dma((5,)),
            dma((Z,)), dma((Z,)), dma((Y,)), dma((Y,)), dma((Z,)), dma((Z,)),
            dma((X,)), dma((X,)), dma((6,)), dma((6,)),
        ],
        compiler_params=pltpu.CompilerParams(
            collective_id=0, has_side_effects=True, vmem_limit_bytes=60 * 2**20),
        name="layer",
    )(queries, key_value_pairs, attention_out, residual,
      norm_gain.reshape(1, MODEL), query_key_weight, value_gate_weight, log_decay, write_strength,
      initial_state,
      head_gain.reshape(1, DV), delta_output)


def solution(mesh):
    return jax.shard_map(
        body,
        mesh=mesh,
        in_specs=(
            P("seq", "head"),
            P("seq", "head"),
            P("seq", None, "head"),
            P("head", None),
            P(),
            P(None, None, "head"),
            P(None, None, "head"),
            P("head", "seq"),
            P("head", "seq"),
            P("head", None, None),
            P(),
            P("head", None),
        ),
        out_specs=P("seq", "head"),
        check_vma=False,
    )
```

```python
import math

import jax
import jax.numpy as jnp
from jax import lax
from jax.experimental import pallas as pl
from jax.experimental.pallas import tpu as pltpu
from jax.sharding import PartitionSpec as P

DK = 128
DV = 128
ATTEND_HEAD_SIZE = 128
WINDOW_KEYS = 4096
X = 4
HEADS = 8
MODEL = 2048
SHARE = 256
PROJECTED = 1536
TILE = 128
TOGETHER = 4
CHUNK = 128
ROWS = 512
KEY_HEADS = 2
VALUE_HEADS = 4
CHUNKS = VALUE_HEADS * ROWS // CHUNK
Z = 8
Y = 4
HALF = DV // 2
MESSAGE = DK + HALF + 16
MESH = pl.DeviceIdType.MESH
f32 = jnp.float32
bf16 = jnp.bfloat16


epsilon = 1e-06


def dot(a, b, contract=((1,), (0,))):
    return lax.dot_general(a, b, (contract, ((), ())), preferred_element_type=f32)


def mm(a, b):
    return dot(a.astype(bf16), b.astype(bf16))


def mm_nt(a, b):
    return dot(a.astype(bf16), b.astype(bf16), ((1,), (1,)))


def split(a):
    high = a.astype(bf16)
    return high, (a - high.astype(f32)).astype(bf16)


def mm2(a, b):
    high, low = split(a)
    return dot(high, b) + dot(low, b)


def mm3(a, b):
    high, low = split(a)
    b_high, b_low = split(b)
    return dot(high, b_high) + dot(low, b_high) + dot(high, b_low)


def grid_of(rows, columns):
    shape = (rows, columns)
    return lax.broadcasted_iota(jnp.int32, shape, 0), lax.broadcasted_iota(jnp.int32, shape, 1)


def three_rows(a):
    high = a.astype(bf16).astype(f32)
    mid = (a - high).astype(bf16).astype(f32)
    low = a - high - mid
    row = lax.broadcasted_iota(jnp.int32, (16, a.shape[1]), 0)
    return jnp.where(row == 0, high, jnp.where(row == 1, mid, jnp.where(row == 2, low, 0.0))).astype(bf16)


def sum_rows(block):
    return jnp.sum(block.astype(f32), axis=0, keepdims=True)


def local_slab(projected, inverse_ref, packed_ref, message_ref, prefix, mixing, both, before_ref, query):
    i, j = grid_of(CHUNK, CHUNK)
    inclusive, strict = i >= j, i > j
    eye = (i == j).astype(f32)
    lower = inclusive.astype(f32)
    for h in range(VALUE_HEADS):
        prefix[h] = jnp.concatenate([eye, jnp.zeros_like(eye)], axis=1)
    per_turn = 2

    def turn(t, carry):
        items = []
        for u in range(per_turn):
            rows = pl.ds(pl.multiple_of((t * per_turn + u) * CHUNK, CHUNK), CHUNK)
            packed = packed_ref[:, rows]
            columns = packed.T
            total_row = lax.dot_general(
                packed, lower, (((1,), (1,)), ((), ())),
                precision=lax.Precision.HIGHEST, preferred_element_type=f32)
            total_col = lax.dot_general(
                lower, columns, (((1,), (0,)), ((), ())),
                precision=lax.Precision.HIGHEST, preferred_element_type=f32)
            keys = []
            for kh in range(KEY_HEADS):
                q = projected[rows, kh * DK:(kh + 1) * DK] * inverse_ref[rows, :]
                q = q * lax.rsqrt(jnp.sum(q * q, axis=-1, keepdims=True) + epsilon) * DK ** (-0.5)
                at = KEY_HEADS * DK + kh * DK
                k = projected[rows, at:at + DK] * inverse_ref[rows, :]
                k = k * lax.rsqrt(jnp.sum(k * k, axis=-1, keepdims=True) + epsilon)
                kb = k.astype(bf16)
                keys.append((q, kb, k.T, mm_nt(kb, kb), mm_nt(q, kb)))
            for h in range(VALUE_HEADS):
                q, k, k_t, key_key, query_key = keys[h // 2]
                cum_col, cum_row = total_col[:, h:h + 1], total_row[h:h + 1, :]
                strength_col = columns[:, VALUE_HEADS + h:VALUE_HEADS + h + 1]
                strength_row = packed[VALUE_HEADS + h:VALUE_HEADS + h + 1, :]
                ratio = jnp.where(inclusive, jnp.exp(jnp.minimum(cum_col - cum_row, 0.0)), 0.0)
                coupling = jnp.where(strict, strength_col * ratio * key_key, 0.0)
                items.append(dict(
                    h=h, n=(t * per_turn + u) * VALUE_HEADS + h, rows=rows, q=q, k=k, k_t=k_t, coupling=coupling, mixing=ratio * query_key,
                    cum_col=cum_col, cum_row=cum_row, strength_row=strength_row,
                    inverse=eye - jnp.where((i // 2) == (j // 2), coupling, 0.0)))
        size = 2
        while size < CHUNK:
            level = ((i // (2 * size)) == (j // (2 * size))) & ((i // size) != (j // size))
            for it in items:
                it["half"] = mm(jnp.where(level, it["coupling"], 0.0), it["inverse"])
            for it in items:
                it["inverse"] = it["inverse"] - mm(it["inverse"], it["half"])
            size *= 2
        for it in items:
            scaled = it["inverse"] * it["strength_row"]
            at = 2 * KEY_HEADS * DK + it["h"] * DV
            v = projected[it["rows"], at:at + DV] * inverse_ref[it["rows"], :]
            w = mm(scaled * jnp.exp(it["cum_row"]), it["k"])
            u = mm(scaled, v)
            it["wu"] = jnp.concatenate([w, u], axis=1).astype(bf16)
            both[it["n"]] = it["wu"]
            mixing[it["n"]] = it["mixing"].astype(bf16)
            query[it["n"]] = jnp.exp(it["cum_col"]) * it["q"]
        for it in items:
            end = it["cum_row"][:, CHUNK - 1:]
            it["end"] = jnp.exp(end)
            it["step"] = mm(it["k_t"] * jnp.exp(end - it["cum_row"]), it["wu"])
        for it in items:
            h = it["h"]
            before = prefix[h]
            before_ref[it["n"]] = before.astype(bf16)
            offset = jnp.concatenate([jnp.zeros((DK, DK), f32), it["step"][:, DK:]], axis=1)
            prefix[h] = it["end"] * before - mm(it["step"][:, :DK], before) + offset
        return carry

    lax.fori_loop(0, ROWS // CHUNK // per_turn, turn, 0)
    slab_decay = jnp.exp(jnp.sum(packed_ref[...], axis=1, keepdims=True))
    for h in range(VALUE_HEADS):
        decay = slab_decay[h:h + 1, :]
        change = (prefix[h, :, :DK] - decay * eye).T.astype(bf16)
        offset = prefix[h, :, DK:].T.astype(bf16)
        tail = three_rows(jnp.broadcast_to(decay, (1, DK)))
        for c in range(2):
            message_ref[2 * h + c, :DK] = change
            message_ref[2 * h + c, DK:DK + HALF] = offset[c * HALF:(c + 1) * HALF]
            message_ref[2 * h + c, DK + HALF:] = tail


def slab_outputs(zero_ref, lead_ref, mixing, both, before_ref, query):
    def turn(t, carry):
        rows = pl.ds(pl.multiple_of(t * CHUNK, CHUNK), CHUNK)
        places = [t * VALUE_HEADS + h for h in range(VALUE_HEADS)]
        mixed = [dot(mixing[n], both[n]) for n in places]
        out = [mm(query[n] - m[:, :DK], before_ref[n]) for n, m in zip(places, mixed)]
        for h in range(VALUE_HEADS):
            lead_ref[rows, h * DK:(h + 1) * DK] = out[h][:, :DK].astype(bf16)
            zero_ref[rows, h * DV:(h + 1) * DV] = out[h][:, DK:] + mixed[h][:, DK:]
        return carry

    lax.fori_loop(0, ROWS // CHUNK, turn, 0)


def at_head(x, c):
    return {"head": (x % X) * 2 + c}


def send(source, target, send_sem, recv_sem, device):
    copy = pltpu.make_async_remote_copy(
        src_ref=source, dst_ref=target, send_sem=send_sem, recv_sem=recv_sem,
        device_id=device, device_id_type=MESH)
    copy.start()
    return copy


def greet(devices):
    barrier = pltpu.get_barrier_semaphore()
    for device in devices:
        pl.semaphore_signal(barrier, inc=1, device_id=device, device_id_type=MESH)
    pl.semaphore_wait(barrier, len(devices))


def gather_heads(blocks, send_sem, recv_sem, x, c, use):
    mid = ROWS // 2
    every, top, bottom = slice(0, ROWS), slice(0, mid), slice(mid, ROWS)
    left, right, far = (x + X - 1) % X, (x + 1) % X, (x + 2) % X
    sibling, to_left, to_right = at_head(x, 1 - c), at_head(x + X - 1, c), at_head(x + 1, c)
    mine = pl.ds(pl.multiple_of(c * SHARE, SHARE), SHARE)
    copies = {}

    def go(n, chip, device, rows):
        ref = blocks.at[chip, rows, mine]
        copies[n] = send(ref, ref, send_sem.at[n], recv_sem.at[n], device)

    go(1, x, to_right, top)
    go(3, x, to_left, bottom)
    go(0, x, sibling, every)
    go(2, x, to_right, bottom)
    go(4, x, to_left, top)
    copies[0].wait_recv()
    use(0, x)
    copies[1].wait_recv()
    go(5, left, to_right, top)
    copies[3].wait_recv()
    go(6, right, to_left, bottom)
    copies[2].wait_recv()
    go(7, left, sibling, every)
    copies[4].wait_recv()
    go(8, right, sibling, every)
    copies[7].wait_recv()
    use(1, left)
    copies[5].wait_recv()
    go(9, far, sibling, top)
    copies[6].wait_recv()
    go(10, far, sibling, bottom)
    copies[8].wait_recv()
    use(2, right)
    copies[9].wait_recv()
    copies[10].wait_recv()
    use(3, far)
    for copy in copies.values():
        copy.wait_send()


def attend_block(queries, window, pair_now, place, peak, total, relation):
    scale = math.log2(math.e) / math.sqrt(ATTEND_HEAD_SIZE)
    ones = jnp.ones((ROWS, ATTEND_HEAD_SIZE), bf16)

    def straighten(t, carry):
        rows = pl.ds(pl.multiple_of(t * 128, 128), 128)
        value = window[place, rows]
        pair_now[rows, :ATTEND_HEAD_SIZE] = value[:, 0, :]
        pair_now[rows, ATTEND_HEAD_SIZE:] = value[:, 1, :]
        return carry

    lax.fori_loop(0, ROWS // 128, straighten, 0)

    keys = pair_now[:, :ATTEND_HEAD_SIZE]
    values = jnp.concatenate([pair_now[:, ATTEND_HEAD_SIZE:], ones], axis=1)
    tiles = 2 * ROWS // TILE
    for start in range(0, tiles, TOGETHER):
        group = [slice(t * TILE, (t + 1) * TILE) for t in range(start, start + TOGETHER)]
        all_scores = [mm_nt(queries[rows, :], keys) * scale for rows in group]
        for rows, scores in zip(group, all_scores):
            if relation is not None:
                i, j = grid_of(TILE, ROWS)
                i = i + rows.start % ROWS
                scores = jnp.where(i >= j if relation == "causal" else i < j, scores, -jnp.inf)
            block_peak = jnp.max(scores, axis=-1, keepdims=True)
            if relation == "causal":
                weights = jnp.exp2(scores - block_peak).astype(bf16)
                total[rows, :] = dot(weights, values)
                peak[rows, :] = jnp.broadcast_to(block_peak, (TILE, ATTEND_HEAD_SIZE))
            else:
                before = peak[rows, :1]
                now = jnp.maximum(before, block_peak)
                weights = jnp.exp2(scores - now).astype(bf16)
                total[rows, :] = total[rows, :] * jnp.exp2(before - now) + dot(weights, values)
                peak[rows, :] = jnp.broadcast_to(now, (TILE, ATTEND_HEAD_SIZE))


FAR_FIRST = (4, 3, 5, 2, 6, 1, 7)


def straight(raw, weight, at, turn):
    width = raw.shape[2]

    def step(t, carry):
        rows = pl.ds(pl.multiple_of(turn * 256 + t * 64, 64), 64)
        value = raw[rows]
        weight[rows, at:at + width] = value[:, 0, :]
        weight[rows, at + width:at + 2 * width] = value[:, 1, :]
        return carry

    lax.fori_loop(0, 4, step, 0)


def layer_kernel(queries_ref, pairs_ref, out_weight_ref, residual_ref, gain_ref, qk_weight_ref,
                 vg_weight_ref, decay_ref, strength_ref, initial_ref, head_gain_ref, delta_weight_ref, out_ref,
                 packed_ref, pair_now, queries, window, peak, total_mix, out_weight, mix, normed, hidden_ref, projected,
                 squares, qk_raw, vg_raw, weight, delta_weight,
                 zero_ref, lead_ref, message_ref, slab_prefix, mixing, both, before_ref, query,
                 row, total, column, prefix, first, back, landed,
                 gate, gated, to_sibling, from_sibling, far, relay, waiting, near, arrived,
                 kv_send, kv_recv, ow_send, ow_recv, mix_send, mix_recv, norm_send, norm_recv,
                 local_sem, row_send, row_recv, col_send, col_recv, back_send, back_recv,
                 pair_send, pair_recv, out_send, out_recv):
    s, head = lax.axis_index("seq"), lax.axis_index("head")
    seq_count = Y * Z
    y, z = s // Z, s % Z
    x, c = head // 2, head % 2
    sibling, to_left, to_right = at_head(x, 1 - c), at_head(x + X - 1, c), at_head(x + 1, c)

    def along(d):
        return {"seq": (s + d + seq_count) % seq_count}

    def other(d):
        return {"head": (head + d) % HEADS}

    def in_row(d):
        return {"seq": y * Z + (z + d + Z) % Z}

    def in_column(d):
        return {"seq": ((y + d) % Y) * Z + z}

    own_columns = pl.ds(pl.multiple_of(head * SHARE, SHARE), SHARE)
    locals_ = [
        pltpu.make_async_copy(pairs_ref, window.at[0], local_sem.at[0]),
        pltpu.make_async_copy(qk_weight_ref, qk_raw, local_sem.at[1]),
        pltpu.make_async_copy(vg_weight_ref, vg_raw, local_sem.at[2]),
        pltpu.make_async_copy(out_weight_ref.at[:, own_columns], out_weight.at[own_columns], local_sem.at[3]),
        pltpu.make_async_copy(delta_weight_ref, delta_weight, local_sem.at[4]),
    ]
    locals_[0].start()
    greet([along(1), along(-1)] + [other(d) for d in range(1, HEADS)]
          + [in_row(d) for d in range(1, Z)] + [in_column(d) for d in range(1, Y)])

    half = ROWS // 2
    halves = (slice(0, half), slice(half, ROWS))
    hops = {}

    def describe(d, part, source, device):
        rows, n = halves[part], 2 * d + part
        return pltpu.make_async_remote_copy(
            src_ref=pairs_ref.at[rows] if source == 0 else window.at[source, rows],
            dst_ref=window.at[d, rows], send_sem=kv_send.at[n], recv_sem=kv_recv.at[n],
            device_id=device, device_id_type=MESH)

    def first_hop(d, part, source, device):
        describe(d, part, source, device).start()

    def hop(d, part, by):
        source = 0 if d == Z else d - 1 if by == 1 else d + 1
        hops[2 * d + part] = describe(d, part, source, along(by))
        hops[2 * d + part].start()

    def landed_part(d, part, by):
        hops[2 * d + part].wait_recv()
        if d == Z:
            pl.when(z == Z - 1)(lambda: first_hop(1, part, Z, in_row(1)))
            pl.when(z != 0)(lambda: first_hop(Z - 1, part, Z, along(-1)))
            return
        if by == 1 and (d < 3 or (d == 3 and part == 0)):
            hop(d + 1, part, 1)
        if by == -1 and (d > 5 or (d == 5 and part == 1)):
            hop(d - 1, part, -1)

    hop(Z, 1, Z)
    hop(Z, 0, Z)
    for part in range(2):
        hops[2 + part] = describe(1, part, 0, along(1))
        hops[2 * (Z - 1) + part] = describe(Z - 1, part, 0, along(-1))
    for part in range(2):
        pl.when(z != Z - 1)(lambda: first_hop(1, part, 0, along(1)))
        pl.when(z == 0)(lambda: first_hop(Z - 1, 1 - part, 0, in_row(-1)))
    for copy in locals_[1:]:
        copy.start()
    weights = []
    for d in range(1, HEADS):
        target = (head + d) % HEADS
        weights.append(send(
            out_weight_ref.at[:, pl.ds(pl.multiple_of(target * SHARE, SHARE), SHARE)],
            out_weight.at[own_columns], ow_send.at[d], ow_recv.at[d], other(d)))
    for g in range(2):
        queries[g * ROWS:(g + 1) * ROWS, :] = queries_ref[:, g * ATTEND_HEAD_SIZE:(g + 1) * ATTEND_HEAD_SIZE]
    packed_ref[:VALUE_HEADS, :] = decay_ref[...]
    packed_ref[VALUE_HEADS:, :] = strength_ref[...]
    locals_[0].wait()
    attend_block(queries, window, pair_now, 0, peak, total_mix, "causal")

    def attend_earlier(d):
        @pl.when(s >= d)
        def _():
            attend_block(queries, window, pair_now, d, peak, total_mix, "window" if d == Z else None)

    def prepare(turn):
        straight(qk_raw, weight, 0, turn)
        straight(vg_raw, weight, 2 * KEY_HEADS * DK, turn)

    landed_part(Z, 1, -1)
    landed_part(1, 0, 1)
    landed_part(Z, 0, -1)
    landed_part(1, 1, 1)
    attend_earlier(1)
    landed_part(7, 1, -1)
    locals_[1].wait()
    locals_[2].wait()
    prepare(0)
    landed_part(2, 0, 1)
    attend_earlier(Z)
    landed_part(7, 0, -1)
    attend_earlier(7)
    landed_part(2, 1, 1)
    prepare(1)
    landed_part(6, 1, -1)
    attend_earlier(2)
    landed_part(3, 0, 1)
    prepare(2)
    landed_part(6, 0, -1)
    attend_earlier(6)
    landed_part(3, 1, 1)
    prepare(3)
    prepare(4)
    landed_part(5, 1, -1)
    attend_earlier(3)
    landed_part(4, 0, 1)
    prepare(5)
    prepare(6)
    prepare(7)
    landed_part(5, 0, -1)
    attend_earlier(5)
    landed_part(4, 1, -1)
    attend_earlier(4)
    for g in range(2):
        rows = slice(g * ROWS, (g + 1) * ROWS)
        at = pl.ds(pl.multiple_of(c * SHARE + g * ATTEND_HEAD_SIZE, ATTEND_HEAD_SIZE), ATTEND_HEAD_SIZE)
        mix[x, :, at] = (
            total_mix[rows, :ATTEND_HEAD_SIZE] / total_mix[rows, ATTEND_HEAD_SIZE:]).astype(bf16)
    for copy in weights:
        copy.wait()
    locals_[3].wait()
    locals_[4].wait()
    for copy in hops.values():
        copy.wait_send()

    def of_chip(chip):
        return pl.ds(pl.multiple_of(chip * 2 * SHARE, 2 * SHARE), 2 * SHARE)

    def add_branch(turn, chip):
        part = dot(mix[chip], out_weight[of_chip(chip), :])
        hidden_ref[...] = part if turn == 0 else hidden_ref[...] + part

    gather_heads(mix, mix_send, mix_recv, x, c, add_branch)
    hidden = residual_ref[...].astype(f32) + hidden_ref[...]
    hidden_ref[...] = hidden
    normed[x, :, pl.ds(pl.multiple_of(c * SHARE, SHARE), SHARE)] = (hidden * gain_ref[:, own_columns]).astype(bf16)

    def add_projected(turn, chip):
        for at in range(0, PROJECTED - VALUE_HEADS * DV, 256):
            cols = slice(at, at + 256)
            part = dot(normed[chip], weight[of_chip(chip), cols])
            projected[:, cols] = part if turn == 0 else projected[:, cols] + part
        value = normed[chip].astype(f32) * (1.0 / gain_ref[:, of_chip(chip)])
        value = value * value
        value = value[:, :256] + value[:, 256:]
        square = value[:, :128] + value[:, 128:]
        squares[...] = square if turn == 0 else squares[...] + square

    gather_heads(normed, norm_send, norm_recv, x, c, add_projected)
    inverse = lax.rsqrt(jnp.sum(squares[...], axis=-1, keepdims=True) * (1.0 / MODEL) + epsilon)
    squares[...] = jnp.broadcast_to(inverse, (ROWS, 128))
    local_slab(projected, squares, packed_ref, message_ref, slab_prefix, mixing, both, before_ref, query)

    sends = []
    for d in FAR_FIRST:
        copy = pltpu.make_async_remote_copy(
            src_ref=message_ref.at[(z + d) % Z], dst_ref=row.at[z], send_sem=row_send.at[d],
            recv_sem=row_recv.at[d], device_id=in_row(d), device_id_type=MESH)
        copy.start()
        sends.append(copy)
    row[z] = message_ref[z]
    first[...] = initial_ref[z // 2].T
    i, j = grid_of(DK + HALF, DK)
    run = (i == j).astype(f32)
    decay = jnp.ones((1, DK), f32)
    slab_outputs(zero_ref, lead_ref, mixing, both, before_ref, query)
    for at in range(PROJECTED - VALUE_HEADS * DV, PROJECTED, 256):
        projected[:, at:at + 256] = sum(
            dot(normed[chip], weight[of_chip(chip), at:at + 256]) for chip in range(X))
    for h in range(VALUE_HEADS):
        cols = slice(h * DV, (h + 1) * DV)
        at = 2 * KEY_HEADS * DK + (VALUE_HEADS + h) * DV
        u = projected[:, at:at + DV] * squares[...]
        gate[:, cols] = head_gain_ref[...] * (u / (1.0 + jnp.exp(-u)))
    for copy in sends:
        copy.wait()
    zero = jnp.zeros((DK, DK), f32)
    for place in range(Z):
        prefix[place] = run
        a = sum_rows(row[place, DK + HALF:])
        offset = jnp.concatenate([zero, row[place, DK:DK + HALF].astype(f32)], axis=0)
        run = a * run + mm2(run, row[place, :DK]) + offset
        decay = decay * a
    total[:DK + HALF] = jnp.where(i == j, run - decay, run).astype(bf16)
    total[DK + HALF:] = three_rows(decay)
    sends = []
    for d in (2, 1, 3):
        copy = pltpu.make_async_remote_copy(
            src_ref=total, dst_ref=column.at[y], send_sem=col_send.at[d], recv_sem=col_recv.at[d],
            device_id=in_column(d), device_id_type=MESH)
        copy.start()
        sends.append(copy)
    column[y] = total[...]
    state = first[pl.ds(pl.multiple_of((z % 2) * HALF, HALF), HALF), :]
    for copy in sends:
        copy.wait()
    for place in range(Y - 1):
        a = sum_rows(column[place, DK + HALF:])
        after = a * state + mm2(state, column[place, :DK]) + column[place, DK:DK + HALF].astype(f32)
        state = jnp.where(place < y, after, state)
    for place in range(Z):
        entering = mm3(state, prefix[place, :DK]) + prefix[place, DK:]
        back[place] = entering.astype(bf16)
    sends = []
    for d in FAR_FIRST:
        copy = pltpu.make_async_remote_copy(
            src_ref=back.at[(z + d) % Z], dst_ref=landed.at[z], send_sem=back_send.at[d],
            recv_sem=back_recv.at[d], device_id=in_row(d), device_id_type=MESH)
        copy.start()
        sends.append(copy)
    landed[z] = back[z]
    for copy in sends:
        copy.wait()
    for h in range(VALUE_HEADS):
        cols = slice(h * DV, (h + 1) * DV)
        state = jnp.concatenate([landed[2 * h], landed[2 * h + 1]], axis=0)
        delta = zero_ref[:, cols] + mm_nt(lead_ref[:, cols], state)
        gated[:, cols] = (delta * inverse_rms(delta) * gate[:, cols]).astype(bf16)

    def partial(d, core):
        at = ((x + d) % X * 2 + core) * SHARE
        return dot(gated[...], delta_weight[:, pl.ds(pl.multiple_of(at, SHARE), SHARE)])

    order, half = (2, 1, X - 1, 0), ROWS // 2
    top, bottom = slice(0, half), slice(half, ROWS)
    pairs, sends = {}, {}

    def over_pair(n):
        to_sibling[n] = partial(order[n], 1 - c).astype(bf16)
        pairs[n] = send(to_sibling.at[n], from_sibling.at[n], pair_send.at[n], pair_recv.at[n], sibling)

    def out_send_rows(n, source, target, device):
        sends[n] = send(source, target, out_send.at[n], out_recv.at[n], device)

    over_pair(0)
    over_pair(1)
    value = partial(2, c)
    pairs[0].wait_recv()
    far[...] = (value + from_sibling[0].astype(f32)).astype(bf16)
    out_send_rows(0, far.at[top], relay.at[0], to_right)
    out_send_rows(1, far.at[bottom], relay.at[1], to_left)
    over_pair(2)
    value = partial(order[1], c)
    pairs[1].wait_recv()
    value = value + from_sibling[1].astype(f32)
    near[0, bottom] = value[bottom].astype(bf16)
    out_send_rows(2, near.at[0, bottom], arrived.at[0, bottom], to_right)
    waiting[0] = value[top]
    value = partial(order[2], c)
    pairs[2].wait_recv()
    value = value + from_sibling[2].astype(f32)
    near[1, top] = value[top].astype(bf16)
    out_send_rows(3, near.at[1, top], arrived.at[1, top], to_left)
    waiting[1] = value[bottom]
    over_pair(3)
    sends[0].wait_recv()
    near[0, top] = (waiting[0] + relay[0].astype(f32)).astype(bf16)
    out_send_rows(4, near.at[0, top], arrived.at[0, top], to_right)
    sends[1].wait_recv()
    near[1, bottom] = (waiting[1] + relay[1].astype(f32)).astype(bf16)
    out_send_rows(5, near.at[1, bottom], arrived.at[1, bottom], to_left)
    value = hidden_ref[...] + partial(0, c)
    pairs[3].wait_recv()
    value = value + from_sibling[3].astype(f32)
    for n in range(2, 6):
        sends[n].wait_recv()
    out_ref[...] = (value + arrived[0].astype(f32) + arrived[1].astype(f32)).astype(bf16)
    for copy in list(pairs.values()) + list(sends.values()):
        copy.wait_send()


def inverse_rms(values):
    return lax.rsqrt(jnp.mean(values * values, axis=-1, keepdims=True) + epsilon)


def body(residual, queries, key_value_pairs, attention_out, norm_gain, query_key_weight,
         value_gate_weight, write_strength, log_decay, initial_state, head_gain, delta_output):
    vmem, hbm = pl.BlockSpec(memory_space=pltpu.VMEM), pl.BlockSpec(memory_space=pl.ANY)
    dma = pltpu.SemaphoreType.DMA
    return pl.pallas_call(
        layer_kernel,
        out_shape=jax.ShapeDtypeStruct((ROWS, SHARE), bf16),
        in_specs=[vmem, hbm, hbm, vmem, vmem, hbm, hbm, vmem, vmem, vmem, vmem, hbm],
        out_specs=vmem,
        scratch_shapes=[
            pltpu.VMEM((2 * VALUE_HEADS, ROWS), f32),
            pltpu.VMEM((ROWS, 2 * ATTEND_HEAD_SIZE), bf16),
            pltpu.VMEM((2 * ROWS, ATTEND_HEAD_SIZE), bf16),
            pltpu.VMEM((Z + 1, ROWS, 2, ATTEND_HEAD_SIZE), bf16),
            pltpu.VMEM((2 * ROWS, ATTEND_HEAD_SIZE), f32),
            pltpu.VMEM((2 * ROWS, 2 * ATTEND_HEAD_SIZE), f32),
            pltpu.VMEM((MODEL, SHARE), bf16),
            pltpu.VMEM((X, ROWS, 2 * SHARE), bf16),
            pltpu.VMEM((X, ROWS, 2 * SHARE), bf16),
            pltpu.VMEM((ROWS, SHARE), f32),
            pltpu.VMEM((ROWS, PROJECTED), f32),
            pltpu.VMEM((ROWS, 128), f32),
            pltpu.VMEM((MODEL, 2, KEY_HEADS * DK), bf16),
            pltpu.VMEM((MODEL, 2, VALUE_HEADS * DV), bf16),
            pltpu.VMEM((MODEL, PROJECTED), bf16),
            pltpu.VMEM((VALUE_HEADS * DV, MODEL), bf16),
            pltpu.VMEM((ROWS, VALUE_HEADS * DV), f32),
            pltpu.VMEM((ROWS, VALUE_HEADS * DK), bf16),
            pltpu.VMEM((Z, MESSAGE, DK), bf16),
            pltpu.VMEM((VALUE_HEADS, DK, DK + DV), f32),
            pltpu.VMEM((CHUNKS, CHUNK, CHUNK), bf16),
            pltpu.VMEM((CHUNKS, CHUNK, DK + DV), bf16),
            pltpu.VMEM((CHUNKS, DK, DK + DV), bf16),
            pltpu.VMEM((CHUNKS, CHUNK, DK), f32),
            pltpu.VMEM((Z, MESSAGE, DK), bf16),
            pltpu.VMEM((MESSAGE, DK), bf16),
            pltpu.VMEM((Y, MESSAGE, DK), bf16),
            pltpu.VMEM((Z, DK + HALF, DK), f32),
            pltpu.VMEM((DV, DK), f32),
            pltpu.VMEM((Z, HALF, DK), bf16),
            pltpu.VMEM((Z, HALF, DK), bf16),
            pltpu.VMEM((ROWS, VALUE_HEADS * DV), f32),
            pltpu.VMEM((ROWS, VALUE_HEADS * DV), bf16),
            pltpu.VMEM((X, ROWS, SHARE), bf16),
            pltpu.VMEM((X, ROWS, SHARE), bf16),
            pltpu.VMEM((ROWS, SHARE), bf16),
            pltpu.VMEM((2, ROWS // 2, SHARE), bf16),
            pltpu.VMEM((2, ROWS // 2, SHARE), f32),
            pltpu.VMEM((2, ROWS, SHARE), bf16),
            pltpu.VMEM((2, ROWS, SHARE), bf16),
            dma((2 * Z + 2,)), dma((2 * Z + 2,)), dma((HEADS,)), dma((HEADS,)),
            dma((11,)), dma((11,)), dma((11,)), dma((11,)), dma((5,)),
            dma((Z,)), dma((Z,)), dma((Y,)), dma((Y,)), dma((Z,)), dma((Z,)),
            dma((X,)), dma((X,)), dma((6,)), dma((6,)),
        ],
        compiler_params=pltpu.CompilerParams(
            collective_id=0, has_side_effects=True, vmem_limit_bytes=60 * 2**20),
        name="layer",
    )(queries, key_value_pairs, attention_out, residual,
      norm_gain.reshape(1, MODEL), query_key_weight, value_gate_weight, log_decay, write_strength,
      initial_state,
      head_gain.reshape(1, DV), delta_output)


def solution(mesh):
    return jax.shard_map(
        body,
        mesh=mesh,
        in_specs=(
            P("seq", "head"),
            P("seq", "head"),
            P("seq", None, "head"),
            P("head", None),
            P(),
            P(None, None, "head"),
            P(None, None, "head"),
            P("head", "seq"),
            P("head", "seq"),
            P("head", None, None),
            P(),
            P("head", None),
        ),
        out_specs=P("seq", "head"),
        check_vma=False,
    )
```

```python
import math

import jax
import jax.numpy as jnp
from jax import lax
from jax.experimental import pallas as pl
from jax.experimental.pallas import tpu as pltpu
from jax.sharding import PartitionSpec as P

DK = 128
DV = 128
ATTEND_HEAD_SIZE = 128
WINDOW_KEYS = 4096
X = 4
HEADS = 8
MODEL = 2048
SHARE = 256
PROJECTED = 1536
TILE = 128
TOGETHER = 4
CHUNK = 128
ROWS = 512
KEY_HEADS = 2
VALUE_HEADS = 4
CHUNKS = VALUE_HEADS * ROWS // CHUNK
Z = 8
Y = 4
MESSAGE = DK + DV + 16
PER_TURN = 2
MESH = pl.DeviceIdType.MESH
f32 = jnp.float32
bf16 = jnp.bfloat16


epsilon = 1e-06


def dot(a, b, contract=((1,), (0,))):
    return lax.dot_general(a, b, (contract, ((), ())), preferred_element_type=f32)


def mm(a, b):
    return dot(a.astype(bf16), b.astype(bf16))


def mm_nt(a, b):
    return dot(a.astype(bf16), b.astype(bf16), ((1,), (1,)))


def split(a):
    high = a.astype(bf16)
    return high, (a - high.astype(f32)).astype(bf16)


def mm2(a, b):
    high, low = split(a)
    return dot(high, b) + dot(low, b)


def mm3(a, b):
    high, low = split(a)
    b_high, b_low = split(b)
    return dot(high, b_high) + dot(low, b_high) + dot(high, b_low)


def grid_of(rows, columns):
    shape = (rows, columns)
    return lax.broadcasted_iota(jnp.int32, shape, 0), lax.broadcasted_iota(jnp.int32, shape, 1)


def three_rows(a):
    high = a.astype(bf16).astype(f32)
    mid = (a - high).astype(bf16).astype(f32)
    low = a - high - mid
    row = lax.broadcasted_iota(jnp.int32, (16, a.shape[1]), 0)
    return jnp.where(row == 0, high, jnp.where(row == 1, mid, jnp.where(row == 2, low, 0.0))).astype(bf16)


def sum_rows(block):
    return jnp.sum(block.astype(f32), axis=0, keepdims=True)


def local_slab(projected, inverse_ref, packed_ref, message_ref, prefix, mixing, both, before_ref, query):
    i, j = grid_of(CHUNK, CHUNK)
    inclusive, strict = i >= j, i > j
    eye = (i == j).astype(f32)
    lower = inclusive.astype(f32)
    for h in range(VALUE_HEADS):
        prefix[h] = jnp.concatenate([eye, jnp.zeros_like(eye)], axis=1)
    per_turn = PER_TURN

    def turn(t, carry):
        items = []
        for u in range(per_turn):
            rows = pl.ds(pl.multiple_of((t * per_turn + u) * CHUNK, CHUNK), CHUNK)
            packed = packed_ref[:, rows]
            columns = packed.T
            total_row = lax.dot_general(
                packed, lower, (((1,), (1,)), ((), ())),
                precision=lax.Precision.HIGHEST, preferred_element_type=f32)
            total_col = lax.dot_general(
                lower, columns, (((1,), (0,)), ((), ())),
                precision=lax.Precision.HIGHEST, preferred_element_type=f32)
            keys = []
            for kh in range(KEY_HEADS):
                q = projected[rows, kh * DK:(kh + 1) * DK] * inverse_ref[rows, :]
                q = q * lax.rsqrt(jnp.sum(q * q, axis=-1, keepdims=True) + epsilon) * DK ** (-0.5)
                at = KEY_HEADS * DK + kh * DK
                k = projected[rows, at:at + DK] * inverse_ref[rows, :]
                k = k * lax.rsqrt(jnp.sum(k * k, axis=-1, keepdims=True) + epsilon)
                kb = k.astype(bf16)
                keys.append((q, kb, k.T, mm_nt(kb, kb), mm_nt(q, kb)))
            for h in range(VALUE_HEADS):
                q, k, k_t, key_key, query_key = keys[h // 2]
                cum_col, cum_row = total_col[:, h:h + 1], total_row[h:h + 1, :]
                strength_col = columns[:, VALUE_HEADS + h:VALUE_HEADS + h + 1]
                strength_row = packed[VALUE_HEADS + h:VALUE_HEADS + h + 1, :]
                ratio = jnp.where(inclusive, jnp.exp(jnp.minimum(cum_col - cum_row, 0.0)), 0.0)
                coupling = jnp.where(strict, strength_col * ratio * key_key, 0.0)
                items.append(dict(
                    h=h, n=(t * per_turn + u) * VALUE_HEADS + h, rows=rows, q=q, k=k, k_t=k_t, coupling=coupling, mixing=ratio * query_key,
                    cum_col=cum_col, cum_row=cum_row, strength_row=strength_row,
                    inverse=eye - jnp.where((i // 2) == (j // 2), coupling, 0.0)))
        size = 2
        while size < CHUNK:
            level = ((i // (2 * size)) == (j // (2 * size))) & ((i // size) != (j // size))
            for it in items:
                it["half"] = mm(jnp.where(level, it["coupling"], 0.0), it["inverse"])
            for it in items:
                it["inverse"] = it["inverse"] - mm(it["inverse"], it["half"])
            size *= 2
        for it in items:
            scaled = it["inverse"] * it["strength_row"]
            at = 2 * KEY_HEADS * DK + it["h"] * DV
            v = projected[it["rows"], at:at + DV] * inverse_ref[it["rows"], :]
            w = mm(scaled * jnp.exp(it["cum_row"]), it["k"])
            u = mm(scaled, v)
            it["wu"] = jnp.concatenate([w, u], axis=1).astype(bf16)
            both[it["n"]] = it["wu"]
            mixing[it["n"]] = it["mixing"].astype(bf16)
            query[it["n"]] = jnp.exp(it["cum_col"]) * it["q"]
        for it in items:
            end = it["cum_row"][:, CHUNK - 1:]
            it["end"] = jnp.exp(end)
            it["step"] = mm(it["k_t"] * jnp.exp(end - it["cum_row"]), it["wu"])
        for it in items:
            h = it["h"]
            before = prefix[h]
            before_ref[it["n"]] = before.astype(bf16)
            offset = jnp.concatenate([jnp.zeros((DK, DK), f32), it["step"][:, DK:]], axis=1)
            prefix[h] = it["end"] * before - mm(it["step"][:, :DK], before) + offset
        return carry

    lax.fori_loop(0, ROWS // CHUNK // per_turn, turn, 0)
    slab_decay = jnp.exp(jnp.sum(packed_ref[...], axis=1, keepdims=True))
    for h in range(VALUE_HEADS):
        decay = slab_decay[h:h + 1, :]
        change = (prefix[h, :, :DK] - decay * eye).T.astype(bf16)
        offset = prefix[h, :, DK:].T.astype(bf16)
        tail = three_rows(jnp.broadcast_to(decay, (1, DK)))
        message_ref[h, :DK] = change
        message_ref[h, DK:DK + DV] = offset
        message_ref[h, DK + DV:] = tail


def slab_outputs(zero_ref, lead_ref, mixing, both, before_ref, query):
    def turn(t, carry):
        rows = pl.ds(pl.multiple_of(t * CHUNK, CHUNK), CHUNK)
        places = [t * VALUE_HEADS + h for h in range(VALUE_HEADS)]
        mixed = [dot(mixing[n], both[n]) for n in places]
        out = [mm(query[n] - m[:, :DK], before_ref[n]) for n, m in zip(places, mixed)]
        for h in range(VALUE_HEADS):
            lead_ref[rows, h * DK:(h + 1) * DK] = out[h][:, :DK].astype(bf16)
            zero_ref[rows, h * DV:(h + 1) * DV] = out[h][:, DK:] + mixed[h][:, DK:]
        return carry

    lax.fori_loop(0, ROWS // CHUNK, turn, 0)


def at_head(x, c):
    return {"head": (x % X) * 2 + c}


def send(source, target, send_sem, recv_sem, device):
    copy = pltpu.make_async_remote_copy(
        src_ref=source, dst_ref=target, send_sem=send_sem, recv_sem=recv_sem,
        device_id=device, device_id_type=MESH)
    copy.start()
    return copy


def greet(devices):
    barrier = pltpu.get_barrier_semaphore()
    for device in devices:
        pl.semaphore_signal(barrier, inc=1, device_id=device, device_id_type=MESH)
    pl.semaphore_wait(barrier, len(devices))


def gather_heads(blocks, send_sem, recv_sem, x, c, use):
    mid = ROWS // 2
    every, top, bottom = slice(0, ROWS), slice(0, mid), slice(mid, ROWS)
    left, right, far = (x + X - 1) % X, (x + 1) % X, (x + 2) % X
    sibling, to_left, to_right = at_head(x, 1 - c), at_head(x + X - 1, c), at_head(x + 1, c)
    mine = pl.ds(pl.multiple_of(c * SHARE, SHARE), SHARE)
    copies = {}

    def go(n, chip, device, rows):
        ref = blocks.at[chip, rows, mine]
        copies[n] = send(ref, ref, send_sem.at[n], recv_sem.at[n], device)

    go(1, x, to_right, top)
    go(3, x, to_left, bottom)
    go(0, x, sibling, every)
    go(2, x, to_right, bottom)
    go(4, x, to_left, top)
    copies[0].wait_recv()
    use(0, x)
    copies[1].wait_recv()
    go(5, left, to_right, top)
    copies[3].wait_recv()
    go(6, right, to_left, bottom)
    copies[2].wait_recv()
    go(7, left, sibling, every)
    copies[4].wait_recv()
    go(8, right, sibling, every)
    copies[7].wait_recv()
    use(1, left)
    copies[5].wait_recv()
    go(9, far, sibling, top)
    copies[6].wait_recv()
    go(10, far, sibling, bottom)
    copies[8].wait_recv()
    use(2, right)
    copies[9].wait_recv()
    copies[10].wait_recv()
    use(3, far)
    for copy in copies.values():
        copy.wait_send()


def attend_block(queries, window, pair_now, place, peak, total, relation):
    scale = math.log2(math.e) / math.sqrt(ATTEND_HEAD_SIZE)
    ones = jnp.ones((ROWS, ATTEND_HEAD_SIZE), bf16)

    def straighten(t, carry):
        rows = pl.ds(pl.multiple_of(t * 128, 128), 128)
        value = window[place, rows]
        pair_now[rows, :ATTEND_HEAD_SIZE] = value[:, 0, :]
        pair_now[rows, ATTEND_HEAD_SIZE:] = value[:, 1, :]
        return carry

    lax.fori_loop(0, ROWS // 128, straighten, 0)

    keys = pair_now[:, :ATTEND_HEAD_SIZE]
    values = jnp.concatenate([pair_now[:, ATTEND_HEAD_SIZE:], ones], axis=1)
    tiles = 2 * ROWS // TILE
    for start in range(0, tiles, TOGETHER):
        group = [slice(t * TILE, (t + 1) * TILE) for t in range(start, start + TOGETHER)]
        all_scores = [mm_nt(queries[rows, :], keys) * scale for rows in group]
        for rows, scores in zip(group, all_scores):
            if relation is not None:
                i, j = grid_of(TILE, ROWS)
                i = i + rows.start % ROWS
                scores = jnp.where(i >= j if relation == "causal" else i < j, scores, -jnp.inf)
            block_peak = jnp.max(scores, axis=-1, keepdims=True)
            if relation == "causal":
                weights = jnp.exp2(scores - block_peak).astype(bf16)
                total[rows, :] = dot(weights, values)
                peak[rows, :] = jnp.broadcast_to(block_peak, (TILE, ATTEND_HEAD_SIZE))
            else:
                before = peak[rows, :1]
                now = jnp.maximum(before, block_peak)
                weights = jnp.exp2(scores - now).astype(bf16)
                total[rows, :] = total[rows, :] * jnp.exp2(before - now) + dot(weights, values)
                peak[rows, :] = jnp.broadcast_to(now, (TILE, ATTEND_HEAD_SIZE))


FAR_FIRST = (4, 3, 5, 2, 6, 1, 7)


def straight(raw, weight, at, turn):
    width = raw.shape[2]

    def step(t, carry):
        rows = pl.ds(pl.multiple_of(turn * 256 + t * 64, 64), 64)
        value = raw[rows]
        weight[rows, at:at + width] = value[:, 0, :]
        weight[rows, at + width:at + 2 * width] = value[:, 1, :]
        return carry

    lax.fori_loop(0, 4, step, 0)


def layer_kernel(queries_ref, pairs_ref, out_weight_ref, residual_ref, gain_ref, qk_weight_ref,
                 vg_weight_ref, decay_ref, strength_ref, initial_ref, head_gain_ref, delta_weight_ref, out_ref,
                 packed_ref, pair_now, queries, window, peak, total_mix, out_weight, mix, normed, hidden_ref, projected,
                 squares, qk_raw, vg_raw, weight, delta_weight,
                 zero_ref, lead_ref, message_ref, slab_prefix, mixing, both, before_ref, query,
                 row, total, column, prefix, back, landed,
                 gate, gated, to_sibling, from_sibling, far, relay, waiting, near, arrived,
                 kv_send, kv_recv, ow_send, ow_recv, mix_send, mix_recv, norm_send, norm_recv,
                 local_sem, row_send, row_recv, col_send, col_recv, back_send, back_recv,
                 pair_send, pair_recv, out_send, out_recv):
    s, head = lax.axis_index("seq"), lax.axis_index("head")
    seq_count = Y * Z
    y, z = s // Z, s % Z
    x, c = head // 2, head % 2
    sibling, to_left, to_right = at_head(x, 1 - c), at_head(x + X - 1, c), at_head(x + 1, c)

    def along(d):
        return {"seq": (s + d + seq_count) % seq_count}

    def other(d):
        return {"head": (head + d) % HEADS}

    def in_row(d):
        return {"seq": y * Z + (z + d + Z) % Z}

    def in_column(d):
        return {"seq": ((y + d) % Y) * Z + z}

    own_columns = pl.ds(pl.multiple_of(head * SHARE, SHARE), SHARE)
    locals_ = [
        pltpu.make_async_copy(pairs_ref, window.at[0], local_sem.at[0]),
        pltpu.make_async_copy(qk_weight_ref, qk_raw, local_sem.at[1]),
        pltpu.make_async_copy(vg_weight_ref, vg_raw, local_sem.at[2]),
        pltpu.make_async_copy(out_weight_ref.at[:, own_columns], out_weight.at[own_columns], local_sem.at[3]),
        pltpu.make_async_copy(delta_weight_ref, delta_weight, local_sem.at[4]),
    ]
    locals_[0].start()
    greet([along(1), along(-1)] + [other(d) for d in range(1, HEADS)]
          + [in_row(d) for d in range(1, Z)] + [in_column(d) for d in range(1, Y)])

    half = ROWS // 2
    halves = (slice(0, half), slice(half, ROWS))
    hops = {}

    def describe(d, part, source, device):
        rows, n = halves[part], 2 * d + part
        return pltpu.make_async_remote_copy(
            src_ref=pairs_ref.at[rows] if source == 0 else window.at[source, rows],
            dst_ref=window.at[d, rows], send_sem=kv_send.at[n], recv_sem=kv_recv.at[n],
            device_id=device, device_id_type=MESH)

    def first_hop(d, part, source, device):
        describe(d, part, source, device).start()

    def hop(d, part, by):
        source = 0 if d == Z else d - 1 if by == 1 else d + 1
        hops[2 * d + part] = describe(d, part, source, along(by))
        hops[2 * d + part].start()

    def landed_part(d, part, by):
        hops[2 * d + part].wait_recv()
        if d == Z:
            pl.when(z == Z - 1)(lambda: first_hop(1, part, Z, in_row(1)))
            pl.when(z != 0)(lambda: first_hop(Z - 1, part, Z, along(-1)))
            return
        if by == 1 and (d < 3 or (d == 3 and part == 0)):
            hop(d + 1, part, 1)
        if by == -1 and (d > 5 or (d == 5 and part == 1)):
            hop(d - 1, part, -1)

    hop(Z, 1, Z)
    hop(Z, 0, Z)
    for part in range(2):
        hops[2 + part] = describe(1, part, 0, along(1))
        hops[2 * (Z - 1) + part] = describe(Z - 1, part, 0, along(-1))
    for part in range(2):
        pl.when(z != Z - 1)(lambda: first_hop(1, part, 0, along(1)))
        pl.when(z == 0)(lambda: first_hop(Z - 1, 1 - part, 0, in_row(-1)))
    for copy in locals_[1:]:
        copy.start()
    weights = []
    for d in range(1, HEADS):
        target = (head + d) % HEADS
        weights.append(send(
            out_weight_ref.at[:, pl.ds(pl.multiple_of(target * SHARE, SHARE), SHARE)],
            out_weight.at[own_columns], ow_send.at[d], ow_recv.at[d], other(d)))
    for g in range(2):
        queries[g * ROWS:(g + 1) * ROWS, :] = queries_ref[:, g * ATTEND_HEAD_SIZE:(g + 1) * ATTEND_HEAD_SIZE]
    packed_ref[:VALUE_HEADS, :] = decay_ref[...]
    packed_ref[VALUE_HEADS:, :] = strength_ref[...]
    locals_[0].wait()
    attend_block(queries, window, pair_now, 0, peak, total_mix, "causal")

    def attend_earlier(d):
        @pl.when(s >= d)
        def _():
            attend_block(queries, window, pair_now, d, peak, total_mix, "window" if d == Z else None)

    def prepare(turn):
        straight(qk_raw, weight, 0, turn)
        straight(vg_raw, weight, 2 * KEY_HEADS * DK, turn)

    landed_part(Z, 1, -1)
    landed_part(1, 0, 1)
    landed_part(Z, 0, -1)
    landed_part(1, 1, 1)
    attend_earlier(1)
    landed_part(7, 1, -1)
    locals_[1].wait()
    locals_[2].wait()
    prepare(0)
    landed_part(2, 0, 1)
    attend_earlier(Z)
    landed_part(7, 0, -1)
    attend_earlier(7)
    landed_part(2, 1, 1)
    prepare(1)
    landed_part(6, 1, -1)
    attend_earlier(2)
    landed_part(3, 0, 1)
    prepare(2)
    landed_part(6, 0, -1)
    attend_earlier(6)
    landed_part(3, 1, 1)
    prepare(3)
    prepare(4)
    landed_part(5, 1, -1)
    attend_earlier(3)
    landed_part(4, 0, 1)
    prepare(5)
    prepare(6)
    prepare(7)
    landed_part(5, 0, -1)
    attend_earlier(5)
    landed_part(4, 1, -1)
    attend_earlier(4)
    for g in range(2):
        rows = slice(g * ROWS, (g + 1) * ROWS)
        at = pl.ds(pl.multiple_of(c * SHARE + g * ATTEND_HEAD_SIZE, ATTEND_HEAD_SIZE), ATTEND_HEAD_SIZE)
        mix[x, :, at] = (
            total_mix[rows, :ATTEND_HEAD_SIZE] / total_mix[rows, ATTEND_HEAD_SIZE:]).astype(bf16)
    for copy in weights:
        copy.wait()
    locals_[3].wait()
    locals_[4].wait()
    for copy in hops.values():
        copy.wait_send()

    def of_chip(chip):
        return pl.ds(pl.multiple_of(chip * 2 * SHARE, 2 * SHARE), 2 * SHARE)

    def add_branch(turn, chip):
        part = dot(mix[chip], out_weight[of_chip(chip), :])
        hidden_ref[...] = part if turn == 0 else hidden_ref[...] + part

    gather_heads(mix, mix_send, mix_recv, x, c, add_branch)
    hidden = residual_ref[...].astype(f32) + hidden_ref[...]
    hidden_ref[...] = hidden
    normed[x, :, pl.ds(pl.multiple_of(c * SHARE, SHARE), SHARE)] = (hidden * gain_ref[:, own_columns]).astype(bf16)

    def add_projected(turn, chip):
        for at in range(0, PROJECTED - VALUE_HEADS * DV, 256):
            cols = slice(at, at + 256)
            part = dot(normed[chip], weight[of_chip(chip), cols])
            projected[:, cols] = part if turn == 0 else projected[:, cols] + part
        value = normed[chip].astype(f32) * (1.0 / gain_ref[:, of_chip(chip)])
        value = value * value
        value = value[:, :256] + value[:, 256:]
        square = value[:, :128] + value[:, 128:]
        squares[...] = square if turn == 0 else squares[...] + square

    gather_heads(normed, norm_send, norm_recv, x, c, add_projected)
    inverse = lax.rsqrt(jnp.sum(squares[...], axis=-1, keepdims=True) * (1.0 / MODEL) + epsilon)
    squares[...] = jnp.broadcast_to(inverse, (ROWS, 128))
    local_slab(projected, squares, packed_ref, message_ref, slab_prefix, mixing, both, before_ref, query)

    def to_job(h):
        return pltpu.make_async_remote_copy(
            src_ref=message_ref.at[h], dst_ref=row.at[z], send_sem=row_send.at[h],
            recv_sem=row_recv.at[z], device_id={"seq": y * Z + 2 * h}, device_id_type=MESH)

    def from_place(place):
        return pltpu.make_async_remote_copy(
            src_ref=message_ref.at[0], dst_ref=row.at[place], send_sem=row_send.at[0],
            recv_sem=row_recv.at[place], device_id={"seq": y * Z + 2 * 0}, device_id_type=MESH)

    def entering_to(d):
        return pltpu.make_async_remote_copy(
            src_ref=back.at[(z + d) % Z], dst_ref=landed.at[z // 2], send_sem=back_send.at[d],
            recv_sem=back_recv.at[z // 2], device_id=in_row(d), device_id_type=MESH)

    def entering_from(h):
        return pltpu.make_async_remote_copy(
            src_ref=back.at[0], dst_ref=landed.at[h], send_sem=back_send.at[0],
            recv_sem=back_recv.at[h], device_id=in_row(1), device_id_type=MESH)

    for h in range(VALUE_HEADS):
        @pl.when(z != 2 * h)
        def _():
            to_job(h).start()

        @pl.when(z == 2 * h)
        def _():
            row[z] = message_ref[h]

    slab_outputs(zero_ref, lead_ref, mixing, both, before_ref, query)
    for at in range(PROJECTED - VALUE_HEADS * DV, PROJECTED, 256):
        projected[:, at:at + 256] = sum(
            dot(normed[chip], weight[of_chip(chip), at:at + 256]) for chip in range(X))
    for h in range(VALUE_HEADS):
        cols = slice(h * DV, (h + 1) * DV)
        at = 2 * KEY_HEADS * DK + (VALUE_HEADS + h) * DV
        u = projected[:, at:at + DV] * squares[...]
        gate[:, cols] = head_gain_ref[...] * (u / (1.0 + jnp.exp(-u)))
    is_job = z % 2 == 0

    @pl.when(is_job)
    def _():
        for place in range(Z):
            @pl.when(z != place)
            def _():
                from_place(place).wait_recv()

        i, j = grid_of(DK + DV, DK)
        run = (i == j).astype(f32)
        decay = jnp.ones((1, DK), f32)
        zero = jnp.zeros((DK, DK), f32)
        for place in range(Z):
            prefix[place] = run
            a = sum_rows(row[place, DK + DV:])
            offset = jnp.concatenate([zero, row[place, DK:DK + DV].astype(f32)], axis=0)
            run = a * run + mm2(run, row[place, :DK]) + offset
            decay = decay * a
        total[:DK + DV] = jnp.where(i == j, run - decay, run).astype(bf16)
        total[DK + DV:] = three_rows(decay)
        sends = []
        for d in (2, 1, 3):
            sends.append(send(total, column.at[y], col_send.at[d], col_recv.at[d], in_column(d)))
        column[y] = total[...]
        state = initial_ref[z // 2].T
        for copy in sends:
            copy.wait()
        for place in range(Y - 1):
            a = sum_rows(column[place, DK + DV:])
            after = a * state + mm2(state, column[place, :DK]) + column[place, DK:DK + DV].astype(f32)
            state = jnp.where(place < y, after, state)
        for place in range(Z):
            entering = mm3(state, prefix[place, :DK]) + prefix[place, DK:]
            back[place] = entering.astype(bf16)
        for d in FAR_FIRST:
            entering_to(d).start()
        landed[z // 2] = back[z]

    for h in range(VALUE_HEADS):
        @pl.when(z != 2 * h)
        def _():
            to_job(h).wait_send()
            entering_from(h).wait_recv()

    @pl.when(is_job)
    def _():
        for d in FAR_FIRST:
            entering_to(d).wait_send()

    for h in range(VALUE_HEADS):
        cols = slice(h * DV, (h + 1) * DV)
        delta = zero_ref[:, cols] + mm_nt(lead_ref[:, cols], landed[h])
        gated[:, cols] = (delta * inverse_rms(delta) * gate[:, cols]).astype(bf16)

    def partial(d, core):
        at = ((x + d) % X * 2 + core) * SHARE
        return dot(gated[...], delta_weight[:, pl.ds(pl.multiple_of(at, SHARE), SHARE)])

    order, half = (2, 1, X - 1, 0), ROWS // 2
    top, bottom = slice(0, half), slice(half, ROWS)
    pairs, sends = {}, {}

    def over_pair(n):
        to_sibling[n] = partial(order[n], 1 - c).astype(bf16)
        pairs[n] = send(to_sibling.at[n], from_sibling.at[n], pair_send.at[n], pair_recv.at[n], sibling)

    def out_send_rows(n, source, target, device):
        sends[n] = send(source, target, out_send.at[n], out_recv.at[n], device)

    over_pair(0)
    over_pair(1)
    value = partial(2, c)
    pairs[0].wait_recv()
    far[...] = (value + from_sibling[0].astype(f32)).astype(bf16)
    out_send_rows(0, far.at[top], relay.at[0], to_right)
    out_send_rows(1, far.at[bottom], relay.at[1], to_left)
    over_pair(2)
    value = partial(order[1], c)
    pairs[1].wait_recv()
    value = value + from_sibling[1].astype(f32)
    near[0, bottom] = value[bottom].astype(bf16)
    out_send_rows(2, near.at[0, bottom], arrived.at[0, bottom], to_right)
    waiting[0] = value[top]
    value = partial(order[2], c)
    pairs[2].wait_recv()
    value = value + from_sibling[2].astype(f32)
    near[1, top] = value[top].astype(bf16)
    out_send_rows(3, near.at[1, top], arrived.at[1, top], to_left)
    waiting[1] = value[bottom]
    over_pair(3)
    sends[0].wait_recv()
    near[0, top] = (waiting[0] + relay[0].astype(f32)).astype(bf16)
    out_send_rows(4, near.at[0, top], arrived.at[0, top], to_right)
    sends[1].wait_recv()
    near[1, bottom] = (waiting[1] + relay[1].astype(f32)).astype(bf16)
    out_send_rows(5, near.at[1, bottom], arrived.at[1, bottom], to_left)
    value = hidden_ref[...] + partial(0, c)
    pairs[3].wait_recv()
    value = value + from_sibling[3].astype(f32)
    for n in range(2, 6):
        sends[n].wait_recv()
    out_ref[...] = (value + arrived[0].astype(f32) + arrived[1].astype(f32)).astype(bf16)
    for copy in list(pairs.values()) + list(sends.values()):
        copy.wait_send()


def inverse_rms(values):
    return lax.rsqrt(jnp.mean(values * values, axis=-1, keepdims=True) + epsilon)


def body(residual, queries, key_value_pairs, attention_out, norm_gain, query_key_weight,
         value_gate_weight, write_strength, log_decay, initial_state, head_gain, delta_output):
    vmem, hbm = pl.BlockSpec(memory_space=pltpu.VMEM), pl.BlockSpec(memory_space=pl.ANY)
    dma = pltpu.SemaphoreType.DMA
    return pl.pallas_call(
        layer_kernel,
        out_shape=jax.ShapeDtypeStruct((ROWS, SHARE), bf16),
        in_specs=[vmem, hbm, hbm, vmem, vmem, hbm, hbm, vmem, vmem, vmem, vmem, hbm],
        out_specs=vmem,
        scratch_shapes=[
            pltpu.VMEM((2 * VALUE_HEADS, ROWS), f32),
            pltpu.VMEM((ROWS, 2 * ATTEND_HEAD_SIZE), bf16),
            pltpu.VMEM((2 * ROWS, ATTEND_HEAD_SIZE), bf16),
            pltpu.VMEM((Z + 1, ROWS, 2, ATTEND_HEAD_SIZE), bf16),
            pltpu.VMEM((2 * ROWS, ATTEND_HEAD_SIZE), f32),
            pltpu.VMEM((2 * ROWS, 2 * ATTEND_HEAD_SIZE), f32),
            pltpu.VMEM((MODEL, SHARE), bf16),
            pltpu.VMEM((X, ROWS, 2 * SHARE), bf16),
            pltpu.VMEM((X, ROWS, 2 * SHARE), bf16),
            pltpu.VMEM((ROWS, SHARE), f32),
            pltpu.VMEM((ROWS, PROJECTED), f32),
            pltpu.VMEM((ROWS, 128), f32),
            pltpu.VMEM((MODEL, 2, KEY_HEADS * DK), bf16),
            pltpu.VMEM((MODEL, 2, VALUE_HEADS * DV), bf16),
            pltpu.VMEM((MODEL, PROJECTED), bf16),
            pltpu.VMEM((VALUE_HEADS * DV, MODEL), bf16),
            pltpu.VMEM((ROWS, VALUE_HEADS * DV), f32),
            pltpu.VMEM((ROWS, VALUE_HEADS * DK), bf16),
            pltpu.VMEM((VALUE_HEADS, MESSAGE, DK), bf16),
            pltpu.VMEM((VALUE_HEADS, DK, DK + DV), f32),
            pltpu.VMEM((CHUNKS, CHUNK, CHUNK), bf16),
            pltpu.VMEM((CHUNKS, CHUNK, DK + DV), bf16),
            pltpu.VMEM((CHUNKS, DK, DK + DV), bf16),
            pltpu.VMEM((CHUNKS, CHUNK, DK), f32),
            pltpu.VMEM((Z, MESSAGE, DK), bf16),
            pltpu.VMEM((MESSAGE, DK), bf16),
            pltpu.VMEM((Y, MESSAGE, DK), bf16),
            pltpu.VMEM((Z, DK + DV, DK), f32),
            pltpu.VMEM((Z, DV, DK), bf16),
            pltpu.VMEM((VALUE_HEADS, DV, DK), bf16),
            pltpu.VMEM((ROWS, VALUE_HEADS * DV), f32),
            pltpu.VMEM((ROWS, VALUE_HEADS * DV), bf16),
            pltpu.VMEM((X, ROWS, SHARE), bf16),
            pltpu.VMEM((X, ROWS, SHARE), bf16),
            pltpu.VMEM((ROWS, SHARE), bf16),
            pltpu.VMEM((2, ROWS // 2, SHARE), bf16),
            pltpu.VMEM((2, ROWS // 2, SHARE), f32),
            pltpu.VMEM((2, ROWS, SHARE), bf16),
            pltpu.VMEM((2, ROWS, SHARE), bf16),
            dma((2 * Z + 2,)), dma((2 * Z + 2,)), dma((HEADS,)), dma((HEADS,)),
            dma((11,)), dma((11,)), dma((11,)), dma((11,)), dma((5,)),
            dma((Z,)), dma((Z,)), dma((Y,)), dma((Y,)), dma((Z,)), dma((Z,)),
            dma((X,)), dma((X,)), dma((6,)), dma((6,)),
        ],
        compiler_params=pltpu.CompilerParams(
            collective_id=0, has_side_effects=True, vmem_limit_bytes=60 * 2**20),
        name="layer",
    )(queries, key_value_pairs, attention_out, residual,
      norm_gain.reshape(1, MODEL), query_key_weight, value_gate_weight, log_decay, write_strength,
      initial_state,
      head_gain.reshape(1, DV), delta_output)


def solution(mesh):
    return jax.shard_map(
        body,
        mesh=mesh,
        in_specs=(
            P("seq", "head"),
            P("seq", "head"),
            P("seq", None, "head"),
            P("head", None),
            P(),
            P(None, None, "head"),
            P(None, None, "head"),
            P("head", "seq"),
            P("head", "seq"),
            P("head", None, None),
            P(),
            P("head", None),
        ),
        out_specs=P("seq", "head"),
        check_vma=False,
    )
```

```python
import math

import jax
import jax.numpy as jnp
from jax import lax
from jax.experimental import pallas as pl
from jax.experimental.pallas import tpu as pltpu
from jax.sharding import PartitionSpec as P

DK = 128
DV = 128
ATTEND_HEAD_SIZE = 128
WINDOW_KEYS = 4096
X = 4
HEADS = 8
MODEL = 2048
SHARE = 256
PROJECTED = 1536
TILE = 128
TOGETHER = 4
CHUNK = 128
ROWS = 512
KEY_HEADS = 2
VALUE_HEADS = 4
CHUNKS = VALUE_HEADS * ROWS // CHUNK
Z = 8
Y = 4
HALF = DV // 2
MESSAGE = DK + HALF + 16
MESH = pl.DeviceIdType.MESH
f32 = jnp.float32
bf16 = jnp.bfloat16


epsilon = 1e-06


def dot(a, b, contract=((1,), (0,))):
    return lax.dot_general(a, b, (contract, ((), ())), preferred_element_type=f32)


def mm(a, b):
    return dot(a.astype(bf16), b.astype(bf16))


def mm_nt(a, b):
    return dot(a.astype(bf16), b.astype(bf16), ((1,), (1,)))


def split(a):
    high = a.astype(bf16)
    return high, (a - high.astype(f32)).astype(bf16)


def mm2(a, b):
    high, low = split(a)
    return dot(high, b) + dot(low, b)


def mm3(a, b):
    high, low = split(a)
    b_high, b_low = split(b)
    return dot(high, b_high) + dot(low, b_high) + dot(high, b_low)


def grid_of(rows, columns):
    shape = (rows, columns)
    return lax.broadcasted_iota(jnp.int32, shape, 0), lax.broadcasted_iota(jnp.int32, shape, 1)


def three_rows(a):
    high = a.astype(bf16).astype(f32)
    mid = (a - high).astype(bf16).astype(f32)
    low = a - high - mid
    row = lax.broadcasted_iota(jnp.int32, (16, a.shape[1]), 0)
    return jnp.where(row == 0, high, jnp.where(row == 1, mid, jnp.where(row == 2, low, 0.0))).astype(bf16)


def sum_rows(block):
    return jnp.sum(block.astype(f32), axis=0, keepdims=True)


def local_slab(projected, inverse_ref, packed_ref, message_ref, prefix, mixing, both, before_ref, query):
    i, j = grid_of(CHUNK, CHUNK)
    inclusive, strict = i >= j, i > j
    eye = (i == j).astype(f32)
    lower = inclusive.astype(f32)
    for h in range(VALUE_HEADS):
        prefix[h] = jnp.concatenate([eye, jnp.zeros_like(eye)], axis=1)
    per_turn = 4

    def turn(t, carry):
        items = []
        for u in range(per_turn):
            rows = pl.ds(pl.multiple_of((t * per_turn + u) * CHUNK, CHUNK), CHUNK)
            packed = packed_ref[:, rows]
            columns = packed.T
            total_row = lax.dot_general(
                packed, lower, (((1,), (1,)), ((), ())),
                precision=lax.Precision.HIGHEST, preferred_element_type=f32)
            total_col = lax.dot_general(
                lower, columns, (((1,), (0,)), ((), ())),
                precision=lax.Precision.HIGHEST, preferred_element_type=f32)
            keys = []
            for kh in range(KEY_HEADS):
                q = projected[rows, kh * DK:(kh + 1) * DK] * inverse_ref[rows, :]
                q = q * lax.rsqrt(jnp.sum(q * q, axis=-1, keepdims=True) + epsilon) * DK ** (-0.5)
                at = KEY_HEADS * DK + kh * DK
                k = projected[rows, at:at + DK] * inverse_ref[rows, :]
                k = k * lax.rsqrt(jnp.sum(k * k, axis=-1, keepdims=True) + epsilon)
                kb = k.astype(bf16)
                keys.append((q, kb, k.T, mm_nt(kb, kb), mm_nt(q, kb)))
            for h in range(VALUE_HEADS):
                q, k, k_t, key_key, query_key = keys[h // 2]
                cum_col, cum_row = total_col[:, h:h + 1], total_row[h:h + 1, :]
                strength_col = columns[:, VALUE_HEADS + h:VALUE_HEADS + h + 1]
                strength_row = packed[VALUE_HEADS + h:VALUE_HEADS + h + 1, :]
                ratio = jnp.where(inclusive, jnp.exp(jnp.minimum(cum_col - cum_row, 0.0)), 0.0)
                coupling = jnp.where(strict, strength_col * ratio * key_key, 0.0)
                items.append(dict(
                    h=h, n=(t * per_turn + u) * VALUE_HEADS + h, rows=rows, q=q, k=k, k_t=k_t, coupling=coupling, mixing=ratio * query_key,
                    cum_col=cum_col, cum_row=cum_row, strength_row=strength_row,
                    inverse=eye - jnp.where((i // 2) == (j // 2), coupling, 0.0)))
        size = 2
        while size < CHUNK:
            level = ((i // (2 * size)) == (j // (2 * size))) & ((i // size) != (j // size))
            for it in items:
                it["half"] = mm(jnp.where(level, it["coupling"], 0.0), it["inverse"])
            for it in items:
                it["inverse"] = it["inverse"] - mm(it["inverse"], it["half"])
            size *= 2
        for it in items:
            scaled = it["inverse"] * it["strength_row"]
            at = 2 * KEY_HEADS * DK + it["h"] * DV
            v = projected[it["rows"], at:at + DV] * inverse_ref[it["rows"], :]
            w = mm(scaled * jnp.exp(it["cum_row"]), it["k"])
            u = mm(scaled, v)
            it["wu"] = jnp.concatenate([w, u], axis=1).astype(bf16)
            both[it["n"]] = it["wu"]
            mixing[it["n"]] = it["mixing"].astype(bf16)
            query[it["n"]] = jnp.exp(it["cum_col"]) * it["q"]
        for it in items:
            end = it["cum_row"][:, CHUNK - 1:]
            it["end"] = jnp.exp(end)
            it["step"] = mm(it["k_t"] * jnp.exp(end - it["cum_row"]), it["wu"])
        for it in items:
            h = it["h"]
            before = prefix[h]
            before_ref[it["n"]] = before.astype(bf16)
            offset = jnp.concatenate([jnp.zeros((DK, DK), f32), it["step"][:, DK:]], axis=1)
            prefix[h] = it["end"] * before - mm(it["step"][:, :DK], before) + offset
        return carry

    lax.fori_loop(0, ROWS // CHUNK // per_turn, turn, 0)
    slab_decay = jnp.exp(jnp.sum(packed_ref[...], axis=1, keepdims=True))
    for h in range(VALUE_HEADS):
        decay = slab_decay[h:h + 1, :]
        change = (prefix[h, :, :DK] - decay * eye).T.astype(bf16)
        offset = prefix[h, :, DK:].T.astype(bf16)
        tail = three_rows(jnp.broadcast_to(decay, (1, DK)))
        for c in range(2):
            message_ref[2 * h + c, :DK] = change
            message_ref[2 * h + c, DK:DK + HALF] = offset[c * HALF:(c + 1) * HALF]
            message_ref[2 * h + c, DK + HALF:] = tail


def slab_outputs(zero_ref, lead_ref, mixing, both, before_ref, query):
    def turn(t, carry):
        rows = pl.ds(pl.multiple_of(t * CHUNK, CHUNK), CHUNK)
        places = [t * VALUE_HEADS + h for h in range(VALUE_HEADS)]
        mixed = [dot(mixing[n], both[n]) for n in places]
        out = [mm(query[n] - m[:, :DK], before_ref[n]) for n, m in zip(places, mixed)]
        for h in range(VALUE_HEADS):
            lead_ref[rows, h * DK:(h + 1) * DK] = out[h][:, :DK].astype(bf16)
            zero_ref[rows, h * DV:(h + 1) * DV] = out[h][:, DK:] + mixed[h][:, DK:]
        return carry

    lax.fori_loop(0, ROWS // CHUNK, turn, 0)


def at_head(x, c):
    return {"head": (x % X) * 2 + c}


def send(source, target, send_sem, recv_sem, device):
    copy = pltpu.make_async_remote_copy(
        src_ref=source, dst_ref=target, send_sem=send_sem, recv_sem=recv_sem,
        device_id=device, device_id_type=MESH)
    copy.start()
    return copy


def greet(devices):
    barrier = pltpu.get_barrier_semaphore()
    for device in devices:
        pl.semaphore_signal(barrier, inc=1, device_id=device, device_id_type=MESH)
    pl.semaphore_wait(barrier, len(devices))


def gather_heads(blocks, send_sem, recv_sem, x, c, use):
    mid = ROWS // 2
    every, top, bottom = slice(0, ROWS), slice(0, mid), slice(mid, ROWS)
    left, right, far = (x + X - 1) % X, (x + 1) % X, (x + 2) % X
    sibling, to_left, to_right = at_head(x, 1 - c), at_head(x + X - 1, c), at_head(x + 1, c)
    mine = pl.ds(pl.multiple_of(c * SHARE, SHARE), SHARE)
    copies = {}

    def go(n, chip, device, rows):
        ref = blocks.at[chip, rows, mine]
        copies[n] = send(ref, ref, send_sem.at[n], recv_sem.at[n], device)

    go(1, x, to_right, top)
    go(3, x, to_left, bottom)
    go(0, x, sibling, every)
    go(2, x, to_right, bottom)
    go(4, x, to_left, top)
    copies[0].wait_recv()
    use(0, x)
    copies[1].wait_recv()
    go(5, left, to_right, top)
    copies[3].wait_recv()
    go(6, right, to_left, bottom)
    copies[2].wait_recv()
    go(7, left, sibling, every)
    copies[4].wait_recv()
    go(8, right, sibling, every)
    copies[7].wait_recv()
    use(1, left)
    copies[5].wait_recv()
    go(9, far, sibling, top)
    copies[6].wait_recv()
    go(10, far, sibling, bottom)
    copies[8].wait_recv()
    use(2, right)
    copies[9].wait_recv()
    copies[10].wait_recv()
    use(3, far)
    for copy in copies.values():
        copy.wait_send()


def attend_block(queries, window, pair_now, place, peak, total, relation):
    scale = math.log2(math.e) / math.sqrt(ATTEND_HEAD_SIZE)
    ones = jnp.ones((ROWS, ATTEND_HEAD_SIZE), bf16)

    def straighten(t, carry):
        rows = pl.ds(pl.multiple_of(t * 128, 128), 128)
        value = window[place, rows]
        pair_now[rows, :ATTEND_HEAD_SIZE] = value[:, 0, :]
        pair_now[rows, ATTEND_HEAD_SIZE:] = value[:, 1, :]
        return carry

    lax.fori_loop(0, ROWS // 128, straighten, 0)

    keys = pair_now[:, :ATTEND_HEAD_SIZE]
    values = jnp.concatenate([pair_now[:, ATTEND_HEAD_SIZE:], ones], axis=1)
    tiles = 2 * ROWS // TILE
    for start in range(0, tiles, TOGETHER):
        group = [slice(t * TILE, (t + 1) * TILE) for t in range(start, start + TOGETHER)]
        all_scores = [mm_nt(queries[rows, :], keys) * scale for rows in group]
        for rows, scores in zip(group, all_scores):
            if relation is not None:
                i, j = grid_of(TILE, ROWS)
                i = i + rows.start % ROWS
                scores = jnp.where(i >= j if relation == "causal" else i < j, scores, -jnp.inf)
            block_peak = jnp.max(scores, axis=-1, keepdims=True)
            if relation == "causal":
                weights = jnp.exp2(scores - block_peak).astype(bf16)
                total[rows, :] = dot(weights, values)
                peak[rows, :] = jnp.broadcast_to(block_peak, (TILE, ATTEND_HEAD_SIZE))
            else:
                before = peak[rows, :1]
                now = jnp.maximum(before, block_peak)
                weights = jnp.exp2(scores - now).astype(bf16)
                total[rows, :] = total[rows, :] * jnp.exp2(before - now) + dot(weights, values)
                peak[rows, :] = jnp.broadcast_to(now, (TILE, ATTEND_HEAD_SIZE))


FAR_FIRST = (4, 3, 5, 2, 6, 1, 7)


def straight(raw, weight, at, turn):
    width = raw.shape[2]

    def step(t, carry):
        rows = pl.ds(pl.multiple_of(turn * 256 + t * 64, 64), 64)
        value = raw[rows]
        weight[rows, at:at + width] = value[:, 0, :]
        weight[rows, at + width:at + 2 * width] = value[:, 1, :]
        return carry

    lax.fori_loop(0, 4, step, 0)


def layer_kernel(queries_ref, pairs_ref, out_weight_ref, residual_ref, gain_ref, qk_weight_ref,
                 vg_weight_ref, decay_ref, strength_ref, initial_ref, head_gain_ref, delta_weight_ref, out_ref,
                 packed_ref, pair_now, queries, window, peak, total_mix, out_weight, mix, normed, hidden_ref, projected,
                 squares, qk_raw, vg_raw, weight, delta_weight,
                 zero_ref, lead_ref, message_ref, slab_prefix, mixing, both, before_ref, query,
                 row, total, column, prefix, first, back, landed,
                 gate, gated, to_sibling, from_sibling, far, relay, waiting, near, arrived,
                 kv_send, kv_recv, ow_send, ow_recv, mix_send, mix_recv, norm_send, norm_recv,
                 local_sem, row_send, row_recv, col_send, col_recv, back_send, back_recv,
                 pair_send, pair_recv, out_send, out_recv):
    s, head = lax.axis_index("seq"), lax.axis_index("head")
    seq_count = Y * Z
    y, z = s // Z, s % Z
    x, c = head // 2, head % 2
    sibling, to_left, to_right = at_head(x, 1 - c), at_head(x + X - 1, c), at_head(x + 1, c)

    def along(d):
        return {"seq": (s + d + seq_count) % seq_count}

    def other(d):
        return {"head": (head + d) % HEADS}

    def in_row(d):
        return {"seq": y * Z + (z + d + Z) % Z}

    def in_column(d):
        return {"seq": ((y + d) % Y) * Z + z}

    own_columns = pl.ds(pl.multiple_of(head * SHARE, SHARE), SHARE)
    locals_ = [
        pltpu.make_async_copy(pairs_ref, window.at[0], local_sem.at[0]),
        pltpu.make_async_copy(qk_weight_ref, qk_raw, local_sem.at[1]),
        pltpu.make_async_copy(vg_weight_ref, vg_raw, local_sem.at[2]),
        pltpu.make_async_copy(out_weight_ref.at[:, own_columns], out_weight.at[own_columns], local_sem.at[3]),
        pltpu.make_async_copy(delta_weight_ref, delta_weight, local_sem.at[4]),
    ]
    locals_[0].start()
    greet([along(1), along(-1)] + [other(d) for d in range(1, HEADS)]
          + [in_row(d) for d in range(1, Z)] + [in_column(d) for d in range(1, Y)])

    half = ROWS // 2
    halves = (slice(0, half), slice(half, ROWS))
    hops = {}

    def describe(d, part, source, device):
        rows, n = halves[part], 2 * d + part
        return pltpu.make_async_remote_copy(
            src_ref=pairs_ref.at[rows] if source == 0 else window.at[source, rows],
            dst_ref=window.at[d, rows], send_sem=kv_send.at[n], recv_sem=kv_recv.at[n],
            device_id=device, device_id_type=MESH)

    def first_hop(d, part, source, device):
        describe(d, part, source, device).start()

    def hop(d, part, by):
        source = 0 if d == Z else d - 1 if by == 1 else d + 1
        hops[2 * d + part] = describe(d, part, source, along(by))
        hops[2 * d + part].start()

    def landed_part(d, part, by):
        hops[2 * d + part].wait_recv()
        if d == Z:
            pl.when(z == Z - 1)(lambda: first_hop(1, part, Z, in_row(1)))
            pl.when(z != 0)(lambda: first_hop(Z - 1, part, Z, along(-1)))
            return
        if by == 1 and (d < 3 or (d == 3 and part == 0)):
            hop(d + 1, part, 1)
        if by == -1 and (d > 5 or (d == 5 and part == 1)):
            hop(d - 1, part, -1)

    hop(Z, 1, Z)
    hop(Z, 0, Z)
    for part in range(2):
        hops[2 + part] = describe(1, part, 0, along(1))
        hops[2 * (Z - 1) + part] = describe(Z - 1, part, 0, along(-1))
    for part in range(2):
        pl.when(z != Z - 1)(lambda: first_hop(1, part, 0, along(1)))
        pl.when(z == 0)(lambda: first_hop(Z - 1, 1 - part, 0, in_row(-1)))
    for copy in locals_[1:]:
        copy.start()
    weights = []
    for d in range(1, HEADS):
        target = (head + d) % HEADS
        weights.append(send(
            out_weight_ref.at[:, pl.ds(pl.multiple_of(target * SHARE, SHARE), SHARE)],
            out_weight.at[own_columns], ow_send.at[d], ow_recv.at[d], other(d)))
    for g in range(2):
        queries[g * ROWS:(g + 1) * ROWS, :] = queries_ref[:, g * ATTEND_HEAD_SIZE:(g + 1) * ATTEND_HEAD_SIZE]
    packed_ref[:VALUE_HEADS, :] = decay_ref[...]
    packed_ref[VALUE_HEADS:, :] = strength_ref[...]
    locals_[0].wait()
    attend_block(queries, window, pair_now, 0, peak, total_mix, "causal")

    def attend_earlier(d):
        @pl.when(s >= d)
        def _():
            attend_block(queries, window, pair_now, d, peak, total_mix, "window" if d == Z else None)

    def prepare(turn):
        straight(qk_raw, weight, 0, turn)
        straight(vg_raw, weight, 2 * KEY_HEADS * DK, turn)

    landed_part(Z, 1, -1)
    landed_part(1, 0, 1)
    landed_part(Z, 0, -1)
    landed_part(1, 1, 1)
    attend_earlier(1)
    landed_part(7, 1, -1)
    locals_[1].wait()
    locals_[2].wait()
    prepare(0)
    landed_part(2, 0, 1)
    attend_earlier(Z)
    landed_part(7, 0, -1)
    attend_earlier(7)
    landed_part(2, 1, 1)
    prepare(1)
    landed_part(6, 1, -1)
    attend_earlier(2)
    landed_part(3, 0, 1)
    prepare(2)
    landed_part(6, 0, -1)
    attend_earlier(6)
    landed_part(3, 1, 1)
    prepare(3)
    prepare(4)
    landed_part(5, 1, -1)
    attend_earlier(3)
    landed_part(4, 0, 1)
    prepare(5)
    prepare(6)
    prepare(7)
    landed_part(5, 0, -1)
    attend_earlier(5)
    landed_part(4, 1, -1)
    attend_earlier(4)
    for g in range(2):
        rows = slice(g * ROWS, (g + 1) * ROWS)
        at = pl.ds(pl.multiple_of(c * SHARE + g * ATTEND_HEAD_SIZE, ATTEND_HEAD_SIZE), ATTEND_HEAD_SIZE)
        mix[x, :, at] = (
            total_mix[rows, :ATTEND_HEAD_SIZE] / total_mix[rows, ATTEND_HEAD_SIZE:]).astype(bf16)
    for copy in weights:
        copy.wait()
    locals_[3].wait()
    locals_[4].wait()
    for copy in hops.values():
        copy.wait_send()

    def of_chip(chip):
        return pl.ds(pl.multiple_of(chip * 2 * SHARE, 2 * SHARE), 2 * SHARE)

    def add_branch(turn, chip):
        part = dot(mix[chip], out_weight[of_chip(chip), :])
        hidden_ref[...] = part if turn == 0 else hidden_ref[...] + part

    gather_heads(mix, mix_send, mix_recv, x, c, add_branch)
    hidden = residual_ref[...].astype(f32) + hidden_ref[...]
    hidden_ref[...] = hidden
    normed[x, :, pl.ds(pl.multiple_of(c * SHARE, SHARE), SHARE)] = (hidden * gain_ref[:, own_columns]).astype(bf16)

    def add_projected(turn, chip):
        for at in range(0, PROJECTED - VALUE_HEADS * DV, 256):
            cols = slice(at, at + 256)
            part = dot(normed[chip], weight[of_chip(chip), cols])
            projected[:, cols] = part if turn == 0 else projected[:, cols] + part
        value = normed[chip].astype(f32) * (1.0 / gain_ref[:, of_chip(chip)])
        value = value * value
        value = value[:, :256] + value[:, 256:]
        square = value[:, :128] + value[:, 128:]
        squares[...] = square if turn == 0 else squares[...] + square

    gather_heads(normed, norm_send, norm_recv, x, c, add_projected)
    inverse = lax.rsqrt(jnp.sum(squares[...], axis=-1, keepdims=True) * (1.0 / MODEL) + epsilon)
    squares[...] = jnp.broadcast_to(inverse, (ROWS, 128))
    local_slab(projected, squares, packed_ref, message_ref, slab_prefix, mixing, both, before_ref, query)

    sends = []
    for d in FAR_FIRST:
        copy = pltpu.make_async_remote_copy(
            src_ref=message_ref.at[(z + d) % Z], dst_ref=row.at[z], send_sem=row_send.at[d],
            recv_sem=row_recv.at[d], device_id=in_row(d), device_id_type=MESH)
        copy.start()
        sends.append(copy)
    row[z] = message_ref[z]
    first[...] = initial_ref[z // 2].T
    i, j = grid_of(DK + HALF, DK)
    run = (i == j).astype(f32)
    decay = jnp.ones((1, DK), f32)
    slab_outputs(zero_ref, lead_ref, mixing, both, before_ref, query)
    for at in range(PROJECTED - VALUE_HEADS * DV, PROJECTED, 256):
        projected[:, at:at + 256] = sum(
            dot(normed[chip], weight[of_chip(chip), at:at + 256]) for chip in range(X))
    for h in range(VALUE_HEADS):
        cols = slice(h * DV, (h + 1) * DV)
        at = 2 * KEY_HEADS * DK + (VALUE_HEADS + h) * DV
        u = projected[:, at:at + DV] * squares[...]
        gate[:, cols] = head_gain_ref[...] * (u / (1.0 + jnp.exp(-u)))
    for copy in sends:
        copy.wait()
    zero = jnp.zeros((DK, DK), f32)
    for place in range(Z):
        prefix[place] = run
        a = sum_rows(row[place, DK + HALF:])
        offset = jnp.concatenate([zero, row[place, DK:DK + HALF].astype(f32)], axis=0)
        run = a * run + mm2(run, row[place, :DK]) + offset
        decay = decay * a
    total[:DK + HALF] = jnp.where(i == j, run - decay, run).astype(bf16)
    total[DK + HALF:] = three_rows(decay)
    sends = []
    for d in (2, 1, 3):
        copy = pltpu.make_async_remote_copy(
            src_ref=total, dst_ref=column.at[y], send_sem=col_send.at[d], recv_sem=col_recv.at[d],
            device_id=in_column(d), device_id_type=MESH)
        copy.start()
        sends.append(copy)
    column[y] = total[...]
    state = first[pl.ds(pl.multiple_of((z % 2) * HALF, HALF), HALF), :]
    for copy in sends:
        copy.wait()
    for place in range(Y - 1):
        a = sum_rows(column[place, DK + HALF:])
        after = a * state + mm2(state, column[place, :DK]) + column[place, DK:DK + HALF].astype(f32)
        state = jnp.where(place < y, after, state)
    for place in range(Z):
        entering = mm3(state, prefix[place, :DK]) + prefix[place, DK:]
        back[place] = entering.astype(bf16)
    sends = []
    for d in FAR_FIRST:
        copy = pltpu.make_async_remote_copy(
            src_ref=back.at[(z + d) % Z], dst_ref=landed.at[z], send_sem=back_send.at[d],
            recv_sem=back_recv.at[d], device_id=in_row(d), device_id_type=MESH)
        copy.start()
        sends.append(copy)
    landed[z] = back[z]
    for copy in sends:
        copy.wait()
    for h in range(VALUE_HEADS):
        cols = slice(h * DV, (h + 1) * DV)
        state = jnp.concatenate([landed[2 * h], landed[2 * h + 1]], axis=0)
        delta = zero_ref[:, cols] + mm_nt(lead_ref[:, cols], state)
        gated[:, cols] = (delta * inverse_rms(delta) * gate[:, cols]).astype(bf16)

    def partial(d, core):
        at = ((x + d) % X * 2 + core) * SHARE
        return dot(gated[...], delta_weight[:, pl.ds(pl.multiple_of(at, SHARE), SHARE)])

    order, half = (2, 1, X - 1, 0), ROWS // 2
    top, bottom = slice(0, half), slice(half, ROWS)
    pairs, sends = {}, {}

    def over_pair(n):
        to_sibling[n] = partial(order[n], 1 - c).astype(bf16)
        pairs[n] = send(to_sibling.at[n], from_sibling.at[n], pair_send.at[n], pair_recv.at[n], sibling)

    def out_send_rows(n, source, target, device):
        sends[n] = send(source, target, out_send.at[n], out_recv.at[n], device)

    over_pair(0)
    over_pair(1)
    value = partial(2, c)
    pairs[0].wait_recv()
    far[...] = (value + from_sibling[0].astype(f32)).astype(bf16)
    out_send_rows(0, far.at[top], relay.at[0], to_right)
    out_send_rows(1, far.at[bottom], relay.at[1], to_left)
    over_pair(2)
    value = partial(order[1], c)
    pairs[1].wait_recv()
    value = value + from_sibling[1].astype(f32)
    near[0, bottom] = value[bottom].astype(bf16)
    out_send_rows(2, near.at[0, bottom], arrived.at[0, bottom], to_right)
    waiting[0] = value[top]
    value = partial(order[2], c)
    pairs[2].wait_recv()
    value = value + from_sibling[2].astype(f32)
    near[1, top] = value[top].astype(bf16)
    out_send_rows(3, near.at[1, top], arrived.at[1, top], to_left)
    waiting[1] = value[bottom]
    over_pair(3)
    sends[0].wait_recv()
    near[0, top] = (waiting[0] + relay[0].astype(f32)).astype(bf16)
    out_send_rows(4, near.at[0, top], arrived.at[0, top], to_right)
    sends[1].wait_recv()
    near[1, bottom] = (waiting[1] + relay[1].astype(f32)).astype(bf16)
    out_send_rows(5, near.at[1, bottom], arrived.at[1, bottom], to_left)
    value = hidden_ref[...] + partial(0, c)
    pairs[3].wait_recv()
    value = value + from_sibling[3].astype(f32)
    for n in range(2, 6):
        sends[n].wait_recv()
    out_ref[...] = (value + arrived[0].astype(f32) + arrived[1].astype(f32)).astype(bf16)
    for copy in list(pairs.values()) + list(sends.values()):
        copy.wait_send()


def inverse_rms(values):
    return lax.rsqrt(jnp.mean(values * values, axis=-1, keepdims=True) + epsilon)


def body(residual, queries, key_value_pairs, attention_out, norm_gain, query_key_weight,
         value_gate_weight, write_strength, log_decay, initial_state, head_gain, delta_output):
    vmem, hbm = pl.BlockSpec(memory_space=pltpu.VMEM), pl.BlockSpec(memory_space=pl.ANY)
    dma = pltpu.SemaphoreType.DMA
    return pl.pallas_call(
        layer_kernel,
        out_shape=jax.ShapeDtypeStruct((ROWS, SHARE), bf16),
        in_specs=[vmem, hbm, hbm, vmem, vmem, hbm, hbm, vmem, vmem, vmem, vmem, hbm],
        out_specs=vmem,
        scratch_shapes=[
            pltpu.VMEM((2 * VALUE_HEADS, ROWS), f32),
            pltpu.VMEM((ROWS, 2 * ATTEND_HEAD_SIZE), bf16),
            pltpu.VMEM((2 * ROWS, ATTEND_HEAD_SIZE), bf16),
            pltpu.VMEM((Z + 1, ROWS, 2, ATTEND_HEAD_SIZE), bf16),
            pltpu.VMEM((2 * ROWS, ATTEND_HEAD_SIZE), f32),
            pltpu.VMEM((2 * ROWS, 2 * ATTEND_HEAD_SIZE), f32),
            pltpu.VMEM((MODEL, SHARE), bf16),
            pltpu.VMEM((X, ROWS, 2 * SHARE), bf16),
            pltpu.VMEM((X, ROWS, 2 * SHARE), bf16),
            pltpu.VMEM((ROWS, SHARE), f32),
            pltpu.VMEM((ROWS, PROJECTED), f32),
            pltpu.VMEM((ROWS, 128), f32),
            pltpu.VMEM((MODEL, 2, KEY_HEADS * DK), bf16),
            pltpu.VMEM((MODEL, 2, VALUE_HEADS * DV), bf16),
            pltpu.VMEM((MODEL, PROJECTED), bf16),
            pltpu.VMEM((VALUE_HEADS * DV, MODEL), bf16),
            pltpu.VMEM((ROWS, VALUE_HEADS * DV), f32),
            pltpu.VMEM((ROWS, VALUE_HEADS * DK), bf16),
            pltpu.VMEM((Z, MESSAGE, DK), bf16),
            pltpu.VMEM((VALUE_HEADS, DK, DK + DV), f32),
            pltpu.VMEM((CHUNKS, CHUNK, CHUNK), bf16),
            pltpu.VMEM((CHUNKS, CHUNK, DK + DV), bf16),
            pltpu.VMEM((CHUNKS, DK, DK + DV), bf16),
            pltpu.VMEM((CHUNKS, CHUNK, DK), f32),
            pltpu.VMEM((Z, MESSAGE, DK), bf16),
            pltpu.VMEM((MESSAGE, DK), bf16),
            pltpu.VMEM((Y, MESSAGE, DK), bf16),
            pltpu.VMEM((Z, DK + HALF, DK), f32),
            pltpu.VMEM((DV, DK), f32),
            pltpu.VMEM((Z, HALF, DK), bf16),
            pltpu.VMEM((Z, HALF, DK), bf16),
            pltpu.VMEM((ROWS, VALUE_HEADS * DV), f32),
            pltpu.VMEM((ROWS, VALUE_HEADS * DV), bf16),
            pltpu.VMEM((X, ROWS, SHARE), bf16),
            pltpu.VMEM((X, ROWS, SHARE), bf16),
            pltpu.VMEM((ROWS, SHARE), bf16),
            pltpu.VMEM((2, ROWS // 2, SHARE), bf16),
            pltpu.VMEM((2, ROWS // 2, SHARE), f32),
            pltpu.VMEM((2, ROWS, SHARE), bf16),
            pltpu.VMEM((2, ROWS, SHARE), bf16),
            dma((2 * Z + 2,)), dma((2 * Z + 2,)), dma((HEADS,)), dma((HEADS,)),
            dma((11,)), dma((11,)), dma((11,)), dma((11,)), dma((5,)),
            dma((Z,)), dma((Z,)), dma((Y,)), dma((Y,)), dma((Z,)), dma((Z,)),
            dma((X,)), dma((X,)), dma((6,)), dma((6,)),
        ],
        compiler_params=pltpu.CompilerParams(
            collective_id=0, has_side_effects=True, vmem_limit_bytes=60 * 2**20),
        name="layer",
    )(queries, key_value_pairs, attention_out, residual,
      norm_gain.reshape(1, MODEL), query_key_weight, value_gate_weight, log_decay, write_strength,
      initial_state,
      head_gain.reshape(1, DV), delta_output)


def solution(mesh):
    return jax.shard_map(
        body,
        mesh=mesh,
        in_specs=(
            P("seq", "head"),
            P("seq", "head"),
            P("seq", None, "head"),
            P("head", None),
            P(),
            P(None, None, "head"),
            P(None, None, "head"),
            P("head", "seq"),
            P("head", "seq"),
            P("head", None, None),
            P(),
            P("head", None),
        ),
        out_specs=P("seq", "head"),
        check_vma=False,
    )
```
